32 devices in a mesh: space: 8 (over y, x, core), dp: 4 (over z).
Axes of the slice: x: 2, y: 2, z: 4, core: 2. Of those that a mesh axis runs over, the one named last changes fastest.
Arguments:
- tokens: bfloat16 [18432, 512], P(('space', 'dp')), may hold values from -6 to 6
- gain: float32 [512], replicated, may hold values from 0.25 to 1.75
- w_in: bfloat16 [8, 512, 1024], P('space'), may hold values from -0.25 to 0.25
- w_out: bfloat16 [8, 1024, 512], P('space'), may hold values from -0.1875 to 0.1875
- expert_ids: int32 [18432, 1], P(('space', 'dp')), may hold values from 0 to 7
- gate: bfloat16 [18432], P(('space', 'dp')), may hold values from 0.25 to 1
- grad_out: bfloat16 [18432, 512], P(('space', 'dp')), may hold values from -6 to 6
Outputs:
- grad_tokens: bfloat16 [18432, 512], P(('space', 'dp'))
- grad_gate: bfloat16 [18432], P(('space', 'dp'))
- grad_w_in: float32 [8, 512, 1024], P('space', 'dp')
- grad_w_out: float32 [8, 1024, 512], P('space', 'dp')
The draws below stay inside these ranges and needn't reach their ends.
All inputs are finite; a program needn't handle non-finite values.
Results may differ from the reference program's by a relative error of at most 0.02.
Values may be sent and summed in bfloat16 or wider, within the bound.
No kernel may reach another device: no remote copies, remote signals or barrier semaphores. Data moves between devices by JAX's collectives and lax.ppermute only.
A program may use at most 64 MiB of HBM per device.

```python
import jax
import jax.numpy as jnp
from jax import lax

D = 512
FF = 1024
TOK_DEV = 576
EXPERTS = 8
CAP = 96
TOKENS = 18432
N_SPACE = 8
N_DP = 4


def level_of(key, dims, split, smallest, high):
    level = 1.0
    for position, parts in split:
        draws = jax.random.uniform(jax.random.fold_in(jax.random.fold_in(key, 6), position), (parts,), jnp.float32, smallest / len(split), high / len(split))
        level = level * jnp.repeat(jnp.exp(draws), dims[position] // parts).reshape((-1,) + (1,) * (len(dims) - 1 - position))
    return level


def choose_distinct(own_key, rows, count, top, lift):
    sequence = jax.random.permutation(jax.random.fold_in(own_key, 1), count)
    favour = sequence
    for power in range(3):
        favour = favour * favour // count
    favour = favour * lift // count
    chance = jax.random.randint(jax.random.fold_in(own_key, 2), (rows, count), 0, 4096) + favour
    sure = jax.random.permutation(jax.random.fold_in(own_key, 3), rows)[jnp.arange(count) % rows]
    chance = jnp.where(jnp.arange(rows)[:, None] == sure[None, :], 1 << 14, chance)
    merit = chance * count + jnp.arange(count)
    return lax.top_k(merit.astype(jnp.int32), top)[1].astype(jnp.int32)


def normal_values(key, extent, deviation, bound, shards=(), kind=jnp.bfloat16):
    factor_of = level_of(key, extent, shards, -0.22, 0.18) if shards else 1.0
    values = jax.random.normal(key, extent, jnp.float32) * deviation * factor_of
    return jnp.minimum(jnp.maximum(values, -bound), bound).astype(kind)


def setup_inputs(seed: int = 0) -> dict:
    arg_keys = jax.random.split(jax.random.key(seed), 8)
    tokens = normal_values(arg_keys[0], (TOKENS, D), 1.0, 6.0, ((0, 32),))
    gain = jnp.clip(1.0 + 0.15 * jax.random.normal(arg_keys[1], (D,), jnp.float32), 0.25, 1.75)
    w_in = normal_values(arg_keys[2], (EXPERTS, D, FF), D ** -0.5, 0.25, ((0, 8),))
    w_out = normal_values(arg_keys[3], (EXPERTS, FF, D), FF ** -0.5, 0.1875, ((0, 8),))
    expert_ids = choose_distinct(arg_keys[4], TOKENS, EXPERTS, 1, 1024)
    gate = jnp.clip(0.25 + 0.75 * jax.random.uniform(arg_keys[5], (TOKENS,), jnp.float32) ** level_of(arg_keys[5], (TOKENS,), ((0, 32),), -0.2, 0.2), 0.25, 1.0).astype(jnp.bfloat16)
    grad_out = normal_values(arg_keys[6], (TOKENS, D), 1.0, 6.0, ((0, 32),))
    return dict(tokens=tokens, gain=gain, w_in=w_in, w_out=w_out, expert_ids=expert_ids, gate=gate, grad_out=grad_out)


epsilon = 1e-05

def normalize(tokens, gain):
    values = tokens.astype(jnp.float32)
    center = values - lax.optimization_barrier(jnp.mean(values, axis=-1, keepdims=True))
    spread = lax.rsqrt(lax.optimization_barrier(jnp.mean(center * center, axis=-1, keepdims=True)) + epsilon)
    scaled = center * spread
    return (scaled, spread, (scaled * gain).astype(jnp.bfloat16))

def slot_ranks(routes, experts):
    onehot = (routes[:, None] == jnp.arange(experts, dtype=jnp.int32)[None, :]).astype(jnp.int32)
    before = jnp.cumsum(onehot, axis=0) - onehot
    return lax.optimization_barrier(jnp.sum(before * onehot, axis=1)).astype(jnp.int32)

def norm_backward(grad_norm, scaled, spread, gain):
    scaled_grad = grad_norm.astype(jnp.float32) * gain
    grad_mean = lax.optimization_barrier(jnp.mean(scaled_grad, axis=-1, keepdims=True))
    grad_cross = lax.optimization_barrier(jnp.mean(scaled_grad * scaled, axis=-1, keepdims=True))
    return spread * (scaled_grad - grad_mean - scaled * grad_cross)

def place_rows(rows, target):
    blank_rows = jnp.zeros((EXPERTS * CAP, D), rows.dtype)
    return blank_rows.at[target].set(rows, mode='drop')

def expert_work(operands):
    normed_rows, delta_rows, weight_in, weight_out = operands
    preact = jnp.einsum('grd,df->grf', normed_rows.astype(jnp.float32), weight_in.astype(jnp.float32))
    act_float, gelu_back = jax.vjp(jax.nn.gelu, preact)
    activity = act_float.astype(jnp.bfloat16)
    token_out = jnp.einsum('grf,fd->grd', activity.astype(jnp.float32), weight_out.astype(jnp.float32)).astype(jnp.bfloat16)
    grad_activity = jnp.einsum('grd,fd->grf', delta_rows.astype(jnp.float32), weight_out.astype(jnp.float32))
    grad_preact = gelu_back(grad_activity)[0].astype(jnp.bfloat16)
    grad_normed = jnp.einsum('grf,df->grd', grad_preact.astype(jnp.float32), weight_in.astype(jnp.float32)).astype(jnp.bfloat16)
    part_in = jnp.einsum('grd,grf->gdf', normed_rows.astype(jnp.float32), grad_preact.astype(jnp.float32)).astype(jnp.bfloat16)
    part_out = jnp.einsum('grf,grd->gfd', activity.astype(jnp.float32), delta_rows.astype(jnp.float32)).astype(jnp.bfloat16)
    sum_in = lax.optimization_barrier(jnp.sum(lax.optimization_barrier(part_in).astype(jnp.float32), axis=0))
    sum_out = lax.optimization_barrier(jnp.sum(lax.optimization_barrier(part_out).astype(jnp.float32), axis=0))
    return (token_out, grad_normed, sum_in, sum_out)

def reference(tokens, gain, w_in, w_out, expert_ids, gate, grad_out):
    blocks = (N_SPACE, N_DP, TOK_DEV)
    scaled, spread, normed = normalize(tokens.reshape(blocks + (D,)), gain)
    routes = expert_ids.reshape(blocks)
    slot_rank = jax.vmap(jax.vmap(lambda routed: slot_ranks(routed, EXPERTS)))(routes)
    kept_mask = slot_rank < CAP
    target = jnp.where(kept_mask, routes * CAP + slot_rank, EXPERTS * CAP).astype(jnp.int32)
    grad_float = grad_out.reshape(blocks + (D,)).astype(jnp.float32)
    gate_float = gate.reshape(blocks).astype(jnp.float32)
    delta = (gate_float[..., None] * grad_float).astype(jnp.bfloat16)
    placer = jax.vmap(jax.vmap(place_rows))

    def to_experts(rows):
        placed = placer(rows, target).reshape(N_SPACE, N_DP, EXPERTS, CAP, D)
        return placed.transpose(2, 1, 0, 3, 4).reshape(EXPERTS, N_DP, N_SPACE * CAP, D)

    def to_tokens(rows):
        back = rows.reshape(EXPERTS, N_DP, N_SPACE, CAP, D).transpose(2, 1, 0, 3, 4)
        back = back.reshape(N_SPACE, N_DP, EXPERTS * CAP, D)
        row_index = jnp.minimum(target, EXPERTS * CAP - 1)
        return jnp.take_along_axis(back, row_index[..., None], axis=2)
    outputs, grads, grad_w_in, grad_w_out = lax.map(expert_work, (to_experts(normed), to_experts(delta), w_in, w_out))
    token_out = to_tokens(outputs)
    token_grad = to_tokens(grads)
    grad_gate = jnp.where(kept_mask, lax.optimization_barrier(jnp.sum(grad_float * token_out.astype(jnp.float32), axis=-1)), 0.0).astype(jnp.bfloat16)
    branch = jnp.where(kept_mask[..., None], norm_backward(token_grad, scaled, spread, gain), 0.0)
    grad_tokens = (grad_float + branch).astype(jnp.bfloat16)
    return (grad_tokens.reshape(TOKENS, D), grad_gate.reshape(TOKENS), grad_w_in, grad_w_out)
```

```python
import functools

import jax
import jax.numpy as jnp
from jax import lax
from jax.experimental import pallas as pl
from jax.experimental.pallas import tpu as pltpu
from jax.sharding import PartitionSpec as P

epsilon = 1e-05
F32 = jnp.float32
BF16 = jnp.bfloat16
LANES = 128
VMEM_BYTES = 56 * 1024 * 1024

vmem = pl.BlockSpec(memory_space=pltpu.VMEM)
smem = pl.BlockSpec(memory_space=pltpu.SMEM)


def dot(left, right, contract=((1,), (0,))):
    return lax.dot_general(left, right, (contract, ((), ())), preferred_element_type=F32)


def normalize(tokens):
    values = tokens.astype(F32)
    center = values - jnp.mean(values, axis=-1, keepdims=True)
    spread = lax.rsqrt(jnp.mean(center * center, axis=-1, keepdims=True) + epsilon)
    return center * spread, spread


def kernel_call(kernel, name, flops, nbytes, outs, ins, scratch=(), transcendentals=0):
    return pl.pallas_call(
        kernel,
        name=name,
        out_shape=outs,
        in_specs=ins,
        out_specs=[vmem] * len(outs),
        scratch_shapes=list(scratch),
        compiler_params=pltpu.CompilerParams(vmem_limit_bytes=VMEM_BYTES),
        cost_estimate=pl.CostEstimate(
            flops=flops, bytes_accessed=nbytes, transcendentals=transcendentals
        ),
    )


def place_kernel(sources, capacity, me, ids_ref, gate_ref, tok_ref, gain_ref, go_ref, target_ref, *outs):
    rows = sources * capacity
    tok_rows, width = tok_ref.shape
    scaled, _ = normalize(tok_ref[...])
    normed = (scaled * gain_ref[...]).astype(BF16)
    ids = ids_ref[...]
    onehot = (lax.broadcasted_iota(jnp.int32, (sources, tok_rows), 0) == ids).astype(F32)
    earlier = lax.broadcasted_iota(jnp.int32, (tok_rows, tok_rows), 0) < lax.broadcasted_iota(
        jnp.int32, (tok_rows, tok_rows), 1
    )
    before = dot(onehot.astype(BF16), jnp.where(earlier, 1.0, 0.0).astype(BF16))
    rank = jnp.sum(before * onehot, axis=0, keepdims=True).astype(jnp.int32)
    target = jnp.where(rank < capacity, jnp.bitwise_xor(ids, me[0]) * capacity + rank, -1)
    target_ref[...] = target
    hit = lax.broadcasted_iota(jnp.int32, (rows, tok_rows), 0) == target
    pick = jnp.where(hit, 1.0, 0.0).astype(BF16)
    pick_gate = jnp.where(hit, gate_ref[...].astype(F32), 0.0).astype(BF16)
    placed_normed = dot(pick, normed).astype(BF16)
    placed_delta = dot(pick_gate, go_ref[...]).astype(BF16)
    for k in range(sources):
        block = slice(k * capacity, (k + 1) * capacity)
        outs[k][:, :width] = placed_normed[block]
        outs[k][:, width:] = placed_delta[block]


def gelu_parts(value):
    root = 0.7978845608028654
    square = value * value
    tan = jnp.tanh(root * (value + 0.044715 * value * square))
    half = 0.5 * (1.0 + tan)
    slope = half + 0.5 * value * (1.0 - tan * tan) * (root * (1.0 + 3.0 * 0.044715 * square))
    return value * half, slope


def grads_kernel(sources, capacity, pieces, order, w_in_ref, w_out_ref, *refs):
    blocks = refs[:sources]
    outs_in = refs[sources : sources + pieces]
    outs_out = refs[sources + pieces : sources + 2 * pieces]
    gpre_ref, extra_ref, x_ref, d_ref, xt_ref = refs[sources + 2 * pieces :]
    width, hidden = w_in_ref.shape
    piece_d, piece_f = width // pieces, hidden // pieces
    for k in range(sources):
        block = slice(k * capacity, (k + 1) * capacity)
        x_ref[block, :] = blocks[k][:, :width]
        d_ref[block, :] = blocks[k][:, width:]
    for j in range(pieces):
        start = pl.multiple_of(order[j] * piece_d, piece_d)
        xt_ref[j * piece_d : (j + 1) * piece_d, :] = x_ref[:, pl.ds(start, piece_d)].T
    total = jnp.zeros((sources * capacity, 1), F32)
    for j in range(pieces):
        part = pl.ds(pl.multiple_of(order[j] * piece_f, piece_f), piece_f)
        delta = d_ref[...]
        preact = dot(x_ref[...], w_in_ref[:, part])
        act_float, slope = gelu_parts(preact)
        act = act_float.astype(BF16)
        grad_act = dot(delta, w_out_ref[part, :], ((1,), (1,)))
        total += jnp.sum(act.astype(F32) * grad_act, axis=1, keepdims=True)
        grad_pre = (grad_act * slope).astype(BF16)
        gpre_ref[:, part] = grad_pre
        outs_out[j][...] = dot(act.T, delta).astype(BF16)
        weight = dot(xt_ref[...], grad_pre).astype(BF16)
        for i in range(pieces):
            outs_in[i][:, part] = weight[i * piece_d : (i + 1) * piece_d]
    high = total.astype(BF16).astype(F32)
    lane = lax.broadcasted_iota(jnp.int32, extra_ref.shape, 1)
    extra_ref[...] = jnp.where(lane == 0, high, jnp.where(lane == 1, total - high, 0.0)).astype(BF16)


def back_kernel(sources, capacity, gpre_ref, w_in_ref, extra_ref, *outs):
    width = w_in_ref.shape[0]
    grad = dot(gpre_ref[...], w_in_ref[...], ((1,), (1,))).astype(BF16)
    for k in range(sources):
        block = slice(k * capacity, (k + 1) * capacity)
        outs[k][:, :width] = grad[block]
        outs[k][:, width:] = extra_ref[block, :]


def finish_kernel(sources, capacity, target_ref, gate_ref, tok_ref, gain_ref, go_ref, *refs):
    blocks = refs[:sources]
    tokens_out, gate_out, back_ref = refs[sources:]
    rows = sources * capacity
    tok_rows, width = tok_ref.shape
    for k in range(sources):
        back_ref[k * capacity : (k + 1) * capacity, :] = blocks[k][...]
    spots = jnp.broadcast_to(target_ref[...].astype(F32), (8, tok_rows)).T[:, :1].astype(jnp.int32)
    hit = lax.broadcasted_iota(jnp.int32, (tok_rows, rows), 1) == spots
    got = dot(jnp.where(hit, 1.0, 0.0).astype(BF16), back_ref[...])
    sums = got[:, width:].T
    gate_out[...] = ((sums[0:1] + sums[1:2]) / gate_ref[...].astype(F32)).astype(BF16)
    scaled, spread = normalize(tok_ref[...])
    grad = got[:, :width] * gain_ref[...]
    mean = jnp.mean(grad, axis=-1, keepdims=True)
    cross = jnp.mean(grad * scaled, axis=-1, keepdims=True)
    branch = spread * (grad - mean - scaled * cross)
    tokens_out[...] = (go_ref[...].astype(F32) + branch).astype(BF16)


def swap_blocks(blocks):
    count = len(blocks)
    return [blocks[0]] + [
        lax.ppermute(blocks[k], "space", [(i, i ^ k) for i in range(count)]) for k in range(1, count)
    ]


def add(*terms):
    return functools.reduce(jnp.add, [t.astype(F32) for t in terms])


def line_sums(first, second, third, own, place):
    swapped = lax.ppermute(first, "dp", [(0, 1), (1, 0), (2, 3), (3, 2)])
    middle = lax.ppermute(second, "dp", [(1, 2), (2, 1)])
    across = lax.ppermute(second, "dp", [(0, 2), (3, 1)])
    inner = (place == 1) | (place == 2)
    passed = jnp.where(inner, add(third, swapped), third.astype(F32)).astype(BF16)
    last = lax.ppermute(passed, "dp", [(0, 1), (3, 2), (1, 3), (2, 0)])
    kept = jnp.where(inner, 0.0, swapped.astype(F32))
    return add(own, middle, across, kept, last)


def body(tokens, gain, w_in, w_out, expert_ids, gate, grad_out):
    sources = lax.axis_size("space")
    groups = lax.axis_size("dp")
    tok_rows, width = tokens.shape
    hidden = w_in.shape[2]
    capacity = ((tok_rows * 5 // 4 + sources - 1) // sources + 7) // 8 * 8
    rows = sources * capacity
    pieces = 4
    me = lax.axis_index("space").astype(jnp.int32).reshape(1)
    place = lax.axis_index("dp").astype(jnp.int32)
    ids_row = expert_ids.reshape(1, tok_rows)
    gate_row = gate.reshape(1, tok_rows)
    gain_row = gain.reshape(1, width)
    weight_in, weight_out = w_in[0], w_out[0]
    shape = jax.ShapeDtypeStruct
    io_bytes = 2 * (2 * tok_rows * width + 2 * rows * width)

    target, *sent = kernel_call(
        functools.partial(place_kernel, sources, capacity),
        "place",
        4 * rows * tok_rows * width,
        io_bytes,
        [shape((1, tok_rows), jnp.int32)] + [shape((capacity, 2 * width), BF16)] * sources,
        [smem] + [vmem] * 5,
    )(me, ids_row, gate_row, tokens, gain_row, grad_out)
    arrived = swap_blocks(sent)

    if groups == 4:
        first = jnp.where(place % 2 == 0, 3, 0)
        second = jnp.where(place < 2, 2, 1)
        order = jnp.stack([first, second, 6 - first - second - place, place]).astype(jnp.int32)
    else:
        order = jnp.arange(pieces, dtype=jnp.int32)
    *parts, gpre, extra = kernel_call(
        functools.partial(grads_kernel, sources, capacity, pieces),
        "grads",
        8 * rows * width * hidden,
        2 * (2 * rows * width + 4 * width * hidden + rows * hidden),
        [shape((width // pieces, hidden), BF16)] * pieces
        + [shape((hidden // pieces, width), BF16)] * pieces
        + [shape((rows, hidden), BF16), shape((rows, LANES), BF16)],
        [smem] + [vmem] * (2 + sources),
        [
            pltpu.VMEM((rows, width), BF16),
            pltpu.VMEM((rows, width), BF16),
            pltpu.VMEM((width, rows), BF16),
        ],
        rows * hidden,
    )(order, weight_in, weight_out, *arrived)
    parts_in, parts_out = parts[:pieces], parts[pieces:]

    returned = kernel_call(
        functools.partial(back_kernel, sources, capacity),
        "back",
        2 * rows * width * hidden,
        2 * (rows * hidden + width * hidden + rows * width),
        [shape((capacity, width + LANES), BF16)] * sources,
        [vmem] * 3,
    )(gpre, weight_in, extra)

    if groups == 4:
        grad_w_out = line_sums(*parts_out, place)
        grad_w_in = line_sums(*parts_in, place)
    else:
        grad_w_in, grad_w_out = (
            lax.psum_scatter(
                jnp.concatenate(part), "dp", scatter_dimension=0, tiled=True
            ).astype(F32)
            for part in (parts_in, parts_out)
        )
    back = swap_blocks(returned)
    grad_tokens, grad_gate = kernel_call(
        functools.partial(finish_kernel, sources, capacity),
        "finish",
        2 * rows * tok_rows * width,
        io_bytes,
        [shape((tok_rows, width), BF16), shape((1, tok_rows), BF16)],
        [vmem] * (5 + sources),
        [pltpu.VMEM((rows, width + LANES), BF16)],
    )(target, gate_row, tokens, gain_row, grad_out, *back)
    return (grad_tokens, grad_gate.reshape(tok_rows), grad_w_in[None], grad_w_out[None])


def solution(mesh):
    placed = (
        P(("space", "dp"), None),
        P(),
        P("space", None, None),
        P("space", None, None),
        P(("space", "dp"), None),
        P(("space", "dp")),
        P(("space", "dp"), None),
    )
    return jax.shard_map(
        body,
        mesh=mesh,
        in_specs=placed,
        out_specs=(
            P(("space", "dp"), None),
            P(("space", "dp")),
            P("space", "dp", None),
            P("space", "dp", None),
        ),
        check_vma=False,
    )
```

```python
import functools

import jax
import jax.numpy as jnp
from jax import lax
from jax.experimental import pallas as pl
from jax.experimental.pallas import tpu as pltpu
from jax.sharding import PartitionSpec as P

epsilon = 1e-05
F32 = jnp.float32
BF16 = jnp.bfloat16
LANES = 128
VMEM_BYTES = 24 * 1024 * 1024

vmem = pl.BlockSpec(memory_space=pltpu.VMEM)
smem = pl.BlockSpec(memory_space=pltpu.SMEM)


def dot(left, right, contract=((1,), (0,))):
    return lax.dot_general(left, right, (contract, ((), ())), preferred_element_type=F32)


def normalize(tokens):
    values = tokens.astype(F32)
    center = values - jnp.mean(values, axis=-1, keepdims=True)
    spread = lax.rsqrt(jnp.mean(center * center, axis=-1, keepdims=True) + epsilon)
    return center * spread, spread


def kernel_call(kernel, name, flops, nbytes, outs, ins, scratch=(), transcendentals=0):
    return pl.pallas_call(
        kernel,
        name=name,
        out_shape=outs,
        in_specs=ins,
        out_specs=[vmem] * len(outs),
        scratch_shapes=list(scratch),
        compiler_params=pltpu.CompilerParams(vmem_limit_bytes=VMEM_BYTES),
        cost_estimate=pl.CostEstimate(
            flops=flops, bytes_accessed=nbytes, transcendentals=transcendentals
        ),
    )


def place_kernel(sources, capacity, me, ids_ref, gate_ref, tok_ref, gain_ref, go_ref, target_ref, *outs):
    rows = sources * capacity
    tok_rows, width = tok_ref.shape
    scaled, _ = normalize(tok_ref[...])
    normed = (scaled * gain_ref[...]).astype(BF16)
    ids = ids_ref[...]
    onehot = (lax.broadcasted_iota(jnp.int32, (sources, tok_rows), 0) == ids).astype(F32)
    earlier = lax.broadcasted_iota(jnp.int32, (tok_rows, tok_rows), 0) < lax.broadcasted_iota(
        jnp.int32, (tok_rows, tok_rows), 1
    )
    before = dot(onehot.astype(BF16), jnp.where(earlier, 1.0, 0.0).astype(BF16))
    rank = jnp.sum(before * onehot, axis=0, keepdims=True).astype(jnp.int32)
    kept = rank < capacity
    target_ref[...] = jnp.where(kept, ids * capacity + rank, -1)
    target = jnp.where(kept, jnp.bitwise_xor(ids, me[0]) * capacity + rank, -1)
    hit = lax.broadcasted_iota(jnp.int32, (rows, tok_rows), 0) == target
    pick = jnp.where(hit, 1.0, 0.0).astype(BF16)
    pick_gate = jnp.where(hit, gate_ref[...].astype(F32).reshape(1, tok_rows), 0.0).astype(BF16)
    placed_normed = dot(pick, normed).astype(BF16)
    placed_delta = dot(pick_gate, go_ref[...]).astype(BF16)
    for k in range(sources):
        block = slice(k * capacity, (k + 1) * capacity)
        outs[k][:, :width] = placed_normed[block]
        outs[k][:, width:] = placed_delta[block]


def gelu_parts(value):
    root = 0.7978845608028654
    square = value * value
    tan = jnp.tanh(root * (value + 0.044715 * value * square))
    half = 0.5 * (1.0 + tan)
    slope = half + 0.5 * value * (1.0 - tan * tan) * (root * (1.0 + 3.0 * 0.044715 * square))
    return value * half, slope


def grads_kernel(sources, capacity, pieces, order, w_in_ref, w_out_ref, *refs):
    blocks = refs[:sources]
    outs = refs[sources : sources + pieces]
    gpre_ref, extra_ref, x_ref, d_ref, xt_ref = refs[sources + pieces :]
    width, hidden = w_in_ref.shape
    piece_d, piece_f = width // pieces, hidden // pieces
    for k in range(sources):
        block = slice(k * capacity, (k + 1) * capacity)
        x_ref[block, :] = blocks[k][:, :width]
        d_ref[block, :] = blocks[k][:, width:]
    for j in range(pieces):
        start = pl.multiple_of(order[j] * piece_d, piece_d)
        xt_ref[j * piece_d : (j + 1) * piece_d, :] = x_ref[:, pl.ds(start, piece_d)].T
    total = jnp.zeros((sources * capacity, 1), F32)
    for j in range(pieces):
        part = pl.ds(pl.multiple_of(order[j] * piece_f, piece_f), piece_f)
        delta = d_ref[...]
        preact = dot(x_ref[...], w_in_ref[:, part])
        act_float, slope = gelu_parts(preact)
        act = act_float.astype(BF16)
        grad_act = dot(delta, w_out_ref[part, :], ((1,), (1,)))
        total += jnp.sum(act.astype(F32) * grad_act, axis=1, keepdims=True)
        grad_pre = (grad_act * slope).astype(BF16)
        gpre_ref[:, part] = grad_pre
        weight = dot(act.T, delta).astype(BF16)
        outs[j][piece_d:, :width] = weight[: piece_f // 2]
        outs[j][piece_d:, width:] = weight[piece_f // 2 :]
        weight = dot(xt_ref[...], grad_pre).astype(BF16)
        for i in range(pieces):
            outs[i][:piece_d, part] = weight[i * piece_d : (i + 1) * piece_d]
    high = total.astype(BF16).astype(F32)
    lane = lax.broadcasted_iota(jnp.int32, extra_ref.shape, 1)
    extra_ref[...] = jnp.where(lane == 0, high, jnp.where(lane == 1, total - high, 0.0)).astype(BF16)


def back_kernel(sources, capacity, me, gpre_ref, w_in_ref, extra_ref, out_ref):
    width = w_in_ref.shape[0]
    grad = dot(gpre_ref[...], w_in_ref[...], ((1,), (1,))).astype(BF16)
    for k in range(sources):
        block = slice(k * capacity, (k + 1) * capacity)
        source = jnp.bitwise_xor(me[0], k)
        out_ref[source, :, :width] = grad[block]
        out_ref[source, :, width:] = extra_ref[block, :]


def finish_kernel(target_ref, gate_ref, tok_ref, gain_ref, go_ref, back_ref, tokens_out, gate_out):
    rows = back_ref.shape[0]
    tok_rows, width = tok_ref.shape
    spots = jnp.broadcast_to(target_ref[...].astype(F32), (8, tok_rows)).T[:, :1].astype(jnp.int32)
    hit = lax.broadcasted_iota(jnp.int32, (tok_rows, rows), 1) == spots
    got = dot(jnp.where(hit, 1.0, 0.0).astype(BF16), back_ref[...])
    sums = got[:, width:].T
    gate_row = gate_ref[...].astype(F32).reshape(1, tok_rows)
    gate_out[...] = ((sums[0:1] + sums[1:2]) / gate_row).astype(BF16)
    scaled, spread = normalize(tok_ref[...])
    grad = got[:, :width] * gain_ref[...]
    mean = jnp.mean(grad, axis=-1, keepdims=True)
    cross = jnp.mean(grad * scaled, axis=-1, keepdims=True)
    branch = spread * (grad - mean - scaled * cross)
    tokens_out[...] = (go_ref[...].astype(F32) + branch).astype(BF16)


def swap_blocks(blocks):
    count = len(blocks)
    swapped = list(blocks)
    for k in reversed(range(1, count)):
        swapped[k] = lax.ppermute(blocks[k], "space", [(i, i ^ k) for i in range(count)])
    return swapped


def add(*terms):
    return functools.reduce(jnp.add, [t.astype(F32) for t in terms])


def line_sums(first, second, third, own, place):
    swapped = lax.ppermute(first, "dp", [(0, 1), (1, 0), (2, 3), (3, 2)])
    middle = lax.ppermute(second, "dp", [(1, 2), (2, 1)])
    across = lax.ppermute(second, "dp", [(0, 2), (3, 1)])
    inner = (place == 1) | (place == 2)
    passed = jnp.where(inner, add(third, swapped), third.astype(F32)).astype(BF16)
    last = lax.ppermute(passed, "dp", [(0, 1), (3, 2), (1, 3), (2, 0)])
    kept = jnp.where(inner, 0.0, swapped.astype(F32))
    return add(own, middle, across, kept, last)


def body(tokens, gain, w_in, w_out, expert_ids, gate, grad_out):
    sources = lax.axis_size("space")
    groups = lax.axis_size("dp")
    tok_rows, width = tokens.shape
    hidden = w_in.shape[2]
    capacity = ((tok_rows * 5 // 4 + sources - 1) // sources + 7) // 8 * 8
    rows = sources * capacity
    pieces = 4
    me = lax.axis_index("space").astype(jnp.int32).reshape(1)
    place = lax.axis_index("dp").astype(jnp.int32)
    ids_row = expert_ids.reshape(1, tok_rows)
    gain_row = gain.reshape(1, width)
    weight_in, weight_out = w_in[0], w_out[0]
    shape = jax.ShapeDtypeStruct
    io_bytes = 2 * (2 * tok_rows * width + 2 * rows * width)

    target, *sent = kernel_call(
        functools.partial(place_kernel, sources, capacity),
        "place",
        4 * rows * tok_rows * width,
        io_bytes,
        [shape((1, tok_rows), jnp.int32)] + [shape((capacity, 2 * width), BF16)] * sources,
        [smem] + [vmem] * 5,
    )(me, ids_row, gate, tokens, gain_row, grad_out)
    arrived = swap_blocks(sent)

    if groups == 4:
        first = jnp.where(place % 2 == 0, 3, 0)
        second = jnp.where(place < 2, 2, 1)
        order = jnp.stack([first, second, 6 - first - second - place, place]).astype(jnp.int32)
    else:
        order = jnp.arange(pieces, dtype=jnp.int32)
    *parts, gpre, extra = kernel_call(
        functools.partial(grads_kernel, sources, capacity, pieces),
        "grads",
        8 * rows * width * hidden,
        2 * (2 * rows * width + 4 * width * hidden + rows * hidden),
        [shape((width // pieces + hidden // pieces // 2, hidden), BF16)] * pieces
        + [shape((rows, hidden), BF16), shape((rows, LANES), BF16)],
        [smem] + [vmem] * (2 + sources),
        [
            pltpu.VMEM((rows, width), BF16),
            pltpu.VMEM((rows, width), BF16),
            pltpu.VMEM((width, rows), BF16),
        ],
        rows * hidden,
    )(order, weight_in, weight_out, *arrived)

    (returned,) = kernel_call(
        functools.partial(back_kernel, sources, capacity),
        "back",
        2 * rows * width * hidden,
        2 * (rows * hidden + width * hidden + rows * width),
        [shape((sources, capacity, width + LANES), BF16)],
        [smem] + [vmem] * 3,
    )(me, gpre, weight_in, extra)
    back = lax.all_to_all(returned, "space", split_axis=0, concat_axis=0, tiled=True)

    if groups == 4:
        grad_w_in, grad_w_out = split_piece(line_sums(*parts, place), width, pieces)
    else:
        parts_in, parts_out = zip(*[split_piece(part, width, pieces) for part in parts])
        grad_w_in, grad_w_out = (
            lax.psum_scatter(
                jnp.concatenate(part), "dp", scatter_dimension=0, tiled=True
            ).astype(F32)
            for part in (parts_in, parts_out)
        )
    grad_tokens, grad_gate = kernel_call(
        finish_kernel,
        "finish",
        2 * rows * tok_rows * width,
        io_bytes,
        [shape((tok_rows, width), BF16), shape((1, tok_rows), BF16)],
        [vmem] * 6,
    )(target, gate, tokens, gain_row, grad_out, back.reshape(rows, width + LANES))
    return (grad_tokens, grad_gate.reshape(tok_rows), grad_w_in[None], grad_w_out[None])


def split_piece(piece, width, pieces):
    piece_d = width // pieces
    lower = piece[piece_d:]
    return piece[:piece_d], jnp.concatenate([lower[:, :width], lower[:, width:]])


def solution(mesh):
    placed = (
        P(("space", "dp"), None),
        P(),
        P("space", None, None),
        P("space", None, None),
        P(("space", "dp"), None),
        P(("space", "dp")),
        P(("space", "dp"), None),
    )
    return jax.shard_map(
        body,
        mesh=mesh,
        in_specs=placed,
        out_specs=(
            P(("space", "dp"), None),
            P(("space", "dp")),
            P("space", "dp", None),
            P("space", "dp", None),
        ),
        check_vma=False,
    )
```

```python
import functools

import jax
import jax.numpy as jnp
from jax import lax
from jax.experimental import pallas as pl
from jax.experimental.pallas import tpu as pltpu
from jax.sharding import PartitionSpec as P

epsilon = 1e-05
F32 = jnp.float32
BF16 = jnp.bfloat16
LANES = 128
MIB = 1024 * 1024

vmem = pl.BlockSpec(memory_space=pltpu.VMEM)
smem = pl.BlockSpec(memory_space=pltpu.SMEM)
hbm = pl.BlockSpec(memory_space=pltpu.HBM)
anywhere = pl.BlockSpec(memory_space=pl.ANY)


def dot(left, right, contract=((1,), (0,))):
    return lax.dot_general(left, right, (contract, ((), ())), preferred_element_type=F32)


def normalize(tokens):
    values = tokens.astype(F32)
    center = values - jnp.mean(values, axis=-1, keepdims=True)
    spread = lax.rsqrt(jnp.mean(center * center, axis=-1, keepdims=True) + epsilon)
    return center * spread, spread


def kernel_call(kernel, name, flops, nbytes, outs, ins, scratch=(), places=None, vmem_mib=24):
    return pl.pallas_call(
        kernel,
        name=name,
        out_shape=outs,
        in_specs=ins,
        out_specs=places or [vmem] * len(outs),
        scratch_shapes=list(scratch),
        compiler_params=pltpu.CompilerParams(vmem_limit_bytes=vmem_mib * MIB),
        cost_estimate=pl.CostEstimate(flops=flops, bytes_accessed=nbytes, transcendentals=0),
    )


def start_copies(pairs, sems):
    copies = [pltpu.make_async_copy(src, dst, sems.at[i]) for i, (src, dst) in enumerate(pairs)]
    for copy in copies:
        copy.start()
    return copies


def place_kernel(sources, capacity, me, ids_hbm, gate_hbm, tok_hbm, gain_hbm, go_hbm, target_ref, *refs):
    outs = refs[:sources]
    ids_ref, gate_ref, tok_ref, gain_ref, go_ref, sent_ref, in_sems, out_sems = refs[sources:]
    rows = sources * capacity
    tok_rows, width = tok_ref.shape
    loads = start_copies(
        [(ids_hbm, ids_ref), (tok_hbm, tok_ref), (gain_hbm, gain_ref), (gate_hbm, gate_ref), (go_hbm, go_ref)],
        in_sems,
    )
    earlier = lax.broadcasted_iota(jnp.int32, (tok_rows, tok_rows), 0) < lax.broadcasted_iota(
        jnp.int32, (tok_rows, tok_rows), 1
    )
    earlier = jnp.where(earlier, 1.0, 0.0).astype(BF16)
    loads[0].wait()
    ids = ids_ref[...]
    onehot = (lax.broadcasted_iota(jnp.int32, (sources, tok_rows), 0) == ids).astype(F32)
    before = dot(onehot.astype(BF16), earlier)
    rank = jnp.sum(before * onehot, axis=0, keepdims=True).astype(jnp.int32)
    kept = rank < capacity
    target_ref[...] = jnp.where(kept, ids * capacity + rank, -1)
    target = jnp.where(kept, jnp.bitwise_xor(ids, me[0]) * capacity + rank, -1)
    hit = lax.broadcasted_iota(jnp.int32, (rows, tok_rows), 0) == target
    pick = jnp.where(hit, 1.0, 0.0).astype(BF16)
    loads[1].wait()
    loads[2].wait()
    scaled, _ = normalize(tok_ref[...])
    normed = (scaled * gain_ref[...]).astype(BF16)
    sent_ref[:, :width] = dot(pick, normed).astype(BF16)
    loads[3].wait()
    pick_gate = jnp.where(hit, gate_ref[...].astype(F32).reshape(1, tok_rows), 0.0).astype(BF16)
    loads[4].wait()
    sent_ref[:, width:] = dot(pick_gate, go_ref[...]).astype(BF16)
    spans = [pl.ds(j * capacity, capacity) for j in range(sources)]
    if capacity % 16:
        for j in range(sources):
            outs[j][...] = sent_ref[spans[j], :]
        return
    for copy in start_copies([(sent_ref.at[spans[j]], outs[j]) for j in range(sources)], out_sems):
        copy.wait()


def gelu_parts(value):
    root = 0.7978845608028654
    square = value * value
    tan = jnp.tanh(root * (value + 0.044715 * value * square))
    half = 0.5 * (1.0 + tan)
    slope = half + 0.5 * value * (1.0 - tan * tan) * (root * (1.0 + 3.0 * 0.044715 * square))
    return value * half, slope


def expert_chunk(rows_ref, w_in_ref, w_out_ref, part):
    width = w_in_ref.shape[0]
    delta = rows_ref[:, width:]
    preact = dot(rows_ref[:, :width], w_in_ref[:, part])
    act_float, slope = gelu_parts(preact)
    act = act_float.astype(BF16)
    grad_act = dot(delta, w_out_ref[part, :], ((1,), (1,)))
    weight = dot(act.T, delta).astype(BF16)
    total = jnp.sum(act.astype(F32) * grad_act, axis=1, keepdims=True)
    return weight, (grad_act * slope).astype(BF16), total


def early_kernel(sources, capacity, pieces, order, w_in_ref, w_out_ref, *refs):
    blocks = refs[:sources]
    first_ref, second_ref, rows_ref, gpre_ref, total_ref, sems = refs[sources:]
    piece_f = w_in_ref.shape[1] // pieces
    spans = [pl.ds(j * capacity, capacity) for j in range(sources)]
    if capacity % 16:
        for j in range(sources):
            rows_ref[spans[j], :] = blocks[j][...]
    else:
        for copy in start_copies([(blocks[j], rows_ref.at[spans[j]]) for j in range(sources)], sems):
            copy.wait()
    sums = []
    for j, out_ref in enumerate((first_ref, second_ref)):
        part = pl.ds(pl.multiple_of(order[j] * piece_f, piece_f), piece_f)
        out_ref[...], grad_pre, total = expert_chunk(rows_ref, w_in_ref, w_out_ref, part)
        gpre_ref[:, j * piece_f : (j + 1) * piece_f] = grad_pre
        sums.append(total)
    total_ref[...] = sums[0] + sums[1]


def late_kernel(
    pieces, order, w_in_ref, w_out_ref, rows_ref, half_ref, total_ref, third_ref, own_ref, *refs
):
    outs = refs[:pieces]
    gpre_ref, extra_ref, turned_ref = refs[pieces:]
    width, hidden = w_in_ref.shape
    piece_d, piece_f = width // pieces, hidden // pieces
    parts = [pl.ds(pl.multiple_of(order[j] * piece_f, piece_f), piece_f) for j in range(pieces)]
    total = total_ref[...]
    for j in range(2):
        gpre_ref[:, parts[j]] = half_ref[:, j * piece_f : (j + 1) * piece_f]
    for j, out_ref in enumerate((third_ref, own_ref)):
        out_ref[...], gpre_ref[:, parts[2 + j]], more = expert_chunk(
            rows_ref, w_in_ref, w_out_ref, parts[2 + j]
        )
        total = total + more
    for j in range(pieces):
        start = pl.multiple_of(order[j] * piece_d, piece_d)
        turned_ref[j * piece_d : (j + 1) * piece_d, :] = rows_ref[:, pl.ds(start, piece_d)].T
    for i in range(pieces):
        chunk = slice(i * piece_f, (i + 1) * piece_f)
        weight = dot(turned_ref[...], gpre_ref[:, chunk]).astype(BF16)
        for j in range(pieces):
            outs[j][:, chunk] = weight[j * piece_d : (j + 1) * piece_d]
    high = total.astype(BF16).astype(F32)
    lane = lax.broadcasted_iota(jnp.int32, extra_ref.shape, 1)
    extra_ref[...] = jnp.where(lane == 0, high, jnp.where(lane == 1, total - high, 0.0)).astype(BF16)


def back_kernel(sources, capacity, me, gpre_ref, w_in_ref, extra_ref, out_ref):
    width = w_in_ref.shape[0]
    grad = dot(gpre_ref[...], w_in_ref[...], ((1,), (1,))).astype(BF16)
    for j in range(sources):
        block = slice(j * capacity, (j + 1) * capacity)
        source = jnp.bitwise_xor(me[0], j)
        out_ref[source, :, :width] = grad[block]
        out_ref[source, :, width:] = extra_ref[block, :]


def finish_kernel(target_ref, gate_ref, tok_ref, gain_ref, go_ref, back_ref, tokens_out, gate_out):
    rows = back_ref.shape[0]
    tok_rows, width = tok_ref.shape
    spots = jnp.broadcast_to(target_ref[...].astype(F32), (8, tok_rows)).T[:, :1].astype(jnp.int32)
    hit = lax.broadcasted_iota(jnp.int32, (tok_rows, rows), 1) == spots
    got = dot(jnp.where(hit, 1.0, 0.0).astype(BF16), back_ref[...])
    sums = got[:, width:].T
    gate_row = gate_ref[...].astype(F32).reshape(1, tok_rows)
    gate_out[...] = ((sums[0:1] + sums[1:2]) / gate_row).astype(BF16).reshape(tok_rows)
    scaled, spread = normalize(tok_ref[...])
    grad = got[:, :width] * gain_ref[...]
    mean = jnp.mean(grad, axis=-1, keepdims=True)
    cross = jnp.mean(grad * scaled, axis=-1, keepdims=True)
    branch = spread * (grad - mean - scaled * cross)
    tokens_out[...] = (go_ref[...].astype(F32) + branch).astype(BF16)


def swap_blocks(blocks):
    count = len(blocks)
    return [
        blocks[j]
        if j == count - 2
        else lax.ppermute(blocks[j], "space", [(i, i ^ j ^ (count - 2)) for i in range(count)])
        for j in range(count)
    ]


def add(*terms):
    return functools.reduce(jnp.add, [t.astype(F32) for t in terms])


def line_sums(outs, ins, place, behind):
    inner = (place == 1) | (place == 2)
    sums, early = [], []
    for first, second, third, own in (outs, ins):
        if early:
            first, swapped = lax.optimization_barrier((first, swapped))
            second, behind, *early = lax.optimization_barrier((second, behind, *early))
            sums[0][1:4] = *early, jnp.where(inner, 0.0, swapped.astype(F32))
        swapped = lax.ppermute(first, "dp", [(0, 1), (1, 0), (2, 3), (3, 2)])
        middle = lax.ppermute(second, "dp", [(1, 2), (2, 1)])
        across = lax.ppermute(second, "dp", [(0, 2), (3, 1)])
        passed = jnp.where(inner, add(third, swapped), third.astype(F32)).astype(BF16)
        last = lax.ppermute(passed, "dp", [(0, 1), (3, 2), (1, 3), (2, 0)])
        early = [middle, across]
        kept = jnp.where(inner, 0.0, swapped.astype(F32))
        sums.append([own, middle, across, kept, last])
    return *[add(*terms) for terms in sums], behind


def body(tokens, gain, w_in, w_out, expert_ids, gate, grad_out):
    sources = lax.axis_size("space")
    groups = lax.axis_size("dp")
    tok_rows, width = tokens.shape
    hidden = w_in.shape[2]
    capacity = ((tok_rows * 5 // 4 + sources - 1) // sources + 7) // 8 * 8
    rows = sources * capacity
    pieces = 4
    me = (lax.axis_index("space").astype(jnp.int32) ^ (sources - 2)).reshape(1)
    place = lax.axis_index("dp").astype(jnp.int32)
    ids_row = expert_ids.reshape(1, tok_rows)
    gain_row = gain.reshape(1, width)
    weight_in, weight_out = w_in[0], w_out[0]
    shape = jax.ShapeDtypeStruct
    sems = pltpu.SemaphoreType.DMA
    block_place = vmem if capacity % 16 else anywhere
    io_bytes = 2 * (2 * tok_rows * width + 2 * rows * width)

    target, *sent = kernel_call(
        functools.partial(place_kernel, sources, capacity),
        "place",
        4 * rows * tok_rows * width,
        io_bytes,
        [shape((1, tok_rows), jnp.int32)] + [shape((capacity, 2 * width), BF16)] * sources,
        [smem] + [hbm] * 5,
        [
            pltpu.VMEM((1, tok_rows), jnp.int32),
            pltpu.VMEM((tok_rows,), BF16),
            pltpu.VMEM((tok_rows, width), BF16),
            pltpu.VMEM((1, width), F32),
            pltpu.VMEM((tok_rows, width), BF16),
            pltpu.VMEM((rows, 2 * width), BF16),
            sems((5,)),
            sems((sources,)),
        ],
        places=[vmem] + [block_place] * sources,
        vmem_mib=56,
    )(me, ids_row, gate, tokens, gain_row, grad_out)
    arrived = swap_blocks(sent)

    if groups == 4:
        first = jnp.where(place % 2 == 0, 3, 0)
        second = jnp.where(place < 2, 2, 1)
        order = jnp.stack([first, second, 6 - first - second - place, place]).astype(jnp.int32)
    else:
        order = jnp.arange(pieces, dtype=jnp.int32)
    piece_in = shape((width // pieces, hidden), BF16)
    piece_out = shape((hidden // pieces, width), BF16)
    first_out, second_out, got_rows, half, total = kernel_call(
        functools.partial(early_kernel, sources, capacity, pieces),
        "early",
        3 * rows * width * hidden,
        4 * rows * width + 4 * width * hidden,
        [
            piece_out,
            piece_out,
            shape((rows, 2 * width), BF16),
            shape((rows, hidden // pieces * 2), BF16),
            shape((rows, 1), F32),
        ],
        [smem] + [vmem] * 2 + [block_place] * sources,
        [sems((sources,))],
    )(order, weight_in, weight_out, *arrived)
    third_out, own_out, *parts_in, gpre, extra = kernel_call(
        functools.partial(late_kernel, pieces),
        "late",
        1,
        1,
        [piece_out] * 2
        + [piece_in] * pieces
        + [shape((rows, hidden), BF16), shape((rows, LANES), BF16)],
        [smem] + [vmem] * 5,
        [pltpu.VMEM((width, rows), BF16)],
    )(order, weight_in, weight_out, got_rows, half, total)
    parts_out = [first_out, second_out, third_out, own_out]

    (returned,) = kernel_call(
        functools.partial(back_kernel, sources, capacity),
        "back",
        1,
        1,
        [shape((sources, capacity, width + LANES), BF16)],
        [smem] + [vmem] * 3,
    )(me, gpre, weight_in, extra)
    if groups == 4:
        grad_w_out, grad_w_in, returned = line_sums(parts_out, parts_in, place, returned)
    else:
        grad_w_in, grad_w_out = (
            lax.psum_scatter(
                jnp.concatenate(part), "dp", scatter_dimension=0, tiled=True
            ).astype(F32)
            for part in (parts_in, parts_out)
        )
    back = lax.all_to_all(returned, "space", split_axis=0, concat_axis=0, tiled=True)
    grad_tokens, grad_gate = kernel_call(
        finish_kernel,
        "finish",
        1,
        1,
        [shape((tok_rows, width), BF16), shape((tok_rows,), BF16)],
        [vmem] * 6,
    )(target, gate, tokens, gain_row, grad_out, back.reshape(rows, width + LANES))
    return (grad_tokens, grad_gate, grad_w_in[None], grad_w_out[None])


def solution(mesh):
    placed = (
        P(("space", "dp"), None),
        P(),
        P("space", None, None),
        P("space", None, None),
        P(("space", "dp"), None),
        P(("space", "dp")),
        P(("space", "dp"), None),
    )
    return jax.shard_map(
        body,
        mesh=mesh,
        in_specs=placed,
        out_specs=(
            P(("space", "dp"), None),
            P(("space", "dp")),
            P("space", "dp", None),
            P("space", "dp", None),
        ),
        check_vma=False,
    )
```

```python
import functools

import jax
import jax.numpy as jnp
from jax import lax
from jax.experimental import pallas as pl
from jax.experimental.pallas import tpu as pltpu
from jax.sharding import PartitionSpec as P

epsilon = 1e-05
F32 = jnp.float32
BF16 = jnp.bfloat16
LANES = 128
LINE = 4
MIB = 1024 * 1024

vmem = pl.BlockSpec(memory_space=pltpu.VMEM)
smem = pl.BlockSpec(memory_space=pltpu.SMEM)
hbm = pl.BlockSpec(memory_space=pltpu.HBM)
anywhere = pl.BlockSpec(memory_space=pl.ANY)


def dot(left, right, contract=((1,), (0,))):
    return lax.dot_general(left, right, (contract, ((), ())), preferred_element_type=F32)


def normalize(tokens):
    values = tokens.astype(F32)
    center = values - jnp.mean(values, axis=-1, keepdims=True)
    spread = lax.rsqrt(jnp.mean(center * center, axis=-1, keepdims=True) + epsilon)
    return center * spread, spread


def kernel_call(kernel, name, flops, nbytes, outs, ins, scratch=(), places=None, vmem_mib=24):
    return pl.pallas_call(
        kernel,
        name=name,
        out_shape=outs,
        in_specs=ins,
        out_specs=places or [vmem] * len(outs),
        scratch_shapes=list(scratch),
        compiler_params=pltpu.CompilerParams(vmem_limit_bytes=vmem_mib * MIB),
        cost_estimate=pl.CostEstimate(flops=flops, bytes_accessed=nbytes, transcendentals=0),
    )


def start_copies(pairs, sems):
    copies = [pltpu.make_async_copy(src, dst, sems.at[i]) for i, (src, dst) in enumerate(pairs)]
    for copy in copies:
        copy.start()
    return copies


def block_base(me, sources):
    return jnp.bitwise_xor(me[0], sources - 2)


def place_kernel(
    sources, capacity, me, place, ids_hbm, gate_hbm, tok_hbm, gain_hbm, go_hbm, target_ref, *refs
):
    outs = refs[:sources]
    ids_ref, gate_ref, tok_ref, gain_ref, go_ref, sent_ref, in_sems, out_sems = refs[sources:]
    rows = sources * capacity
    tok_rows, width = tok_ref.shape
    loads = start_copies(
        [(ids_hbm, ids_ref), (tok_hbm, tok_ref), (gain_hbm, gain_ref), (gate_hbm, gate_ref), (go_hbm, go_ref)],
        in_sems,
    )
    mine = block_base(me, sources)
    earlier = lax.broadcasted_iota(jnp.int32, (tok_rows, tok_rows), 0) < lax.broadcasted_iota(
        jnp.int32, (tok_rows, tok_rows), 1
    )
    earlier = jnp.where(earlier, 1.0, 0.0).astype(BF16)
    for copy in loads:
        copy.wait()
    ids = ids_ref[...]
    onehot = (lax.broadcasted_iota(jnp.int32, (sources, tok_rows), 0) == ids).astype(F32)
    before = dot(onehot.astype(BF16), earlier)
    rank = jnp.sum(before * onehot, axis=0, keepdims=True).astype(jnp.int32)
    kept = rank < capacity
    target_ref[...] = jnp.where(kept, ids * capacity + rank, -1)
    target = jnp.where(kept, jnp.bitwise_xor(ids, mine) * capacity + rank, -1)
    hit = lax.broadcasted_iota(jnp.int32, (rows, tok_rows), 0) == target
    gate = gate_ref[...].astype(F32).reshape(1, tok_rows)
    scaled, _ = normalize(tok_ref[...])
    normed = (scaled * gain_ref[...]).astype(BF16)
    stores = []
    for part, (weight, values) in enumerate(((gate, go_ref[...]), (1.0, normed))):
        columns = pl.ds((1 - part) * width, width)
        sent_ref[:, columns] = dot(jnp.where(hit, weight, 0.0).astype(BF16), values).astype(BF16)
        spans = [pl.ds(j * capacity, capacity) for j in range(sources)]
        if capacity % 16:
            for j in range(sources):
                outs[j][:, columns] = sent_ref[spans[j], columns]
        else:
            stores += start_copies(
                [(sent_ref.at[spans[j], columns], outs[j].at[:, columns]) for j in range(sources)],
                out_sems.at[part],
            )
    for copy in stores:
        copy.wait()


def keep_kernel(block_ref, out_ref):
    out_ref[...] = block_ref[...]


def gelu_parts(value):
    root = 0.7978845608028654
    square = value * value
    tan = jnp.tanh(root * (value + 0.044715 * value * square))
    half = 0.5 * (1.0 + tan)
    slope = half + 0.5 * value * (1.0 - tan * tan) * (root * (1.0 + 3.0 * 0.044715 * square))
    return value * half, slope


def expert_chunk(rows_ref, w_in_ref, w_out_ref, part):
    width = w_in_ref.shape[0]
    delta = rows_ref[:, width:]
    preact = dot(rows_ref[:, :width], w_in_ref[:, part])
    act_float, slope = gelu_parts(preact)
    act = act_float.astype(BF16)
    grad_act = dot(delta, w_out_ref[part, :], ((1,), (1,)))
    weight = dot(act.T, delta).astype(BF16)
    total = jnp.sum(act.astype(F32) * grad_act, axis=1, keepdims=True)
    return weight, (grad_act * slope).astype(BF16), total


def shard_order(place):
    first = jnp.where(lax.rem(place, 2) == 0, 3, 0)
    second = jnp.where(place < 2, 2, 1)
    return [first, second, 6 - first - second - place, place]


def grads_kernel(sources, capacity, groups, place, w_in_ref, w_out_ref, *refs):
    blocks = refs[:sources]
    outs = refs[sources : sources + LINE]
    gpre_ref, extra_ref, rows_ref, turned_ref, sems = refs[sources + LINE :]
    width, hidden = w_in_ref.shape
    piece_d, piece_f = width // LINE, hidden // LINE
    order = shard_order(place[0]) if groups == LINE else list(range(LINE))
    spans = [pl.ds(j * capacity, capacity) for j in range(sources)]
    if capacity % 16:
        for j in range(sources):
            rows_ref[spans[j], :] = blocks[j][...]
    else:
        for copy in start_copies([(blocks[j], rows_ref.at[spans[j]]) for j in range(sources)], sems):
            copy.wait()
    for j in range(LINE):
        start = pl.multiple_of(order[j] * piece_d, piece_d)
        turned_ref[j * piece_d : (j + 1) * piece_d, :] = rows_ref[:, pl.ds(start, piece_d)].T
    total = jnp.zeros((sources * capacity, 1), F32)
    for j in range(LINE):
        part = pl.ds(pl.multiple_of(order[j] * piece_f, piece_f), piece_f)
        weight, grad_pre, more = expert_chunk(rows_ref, w_in_ref, w_out_ref, part)
        total += more
        gpre_ref[:, part] = grad_pre
        outs[j][piece_d:, :width] = weight[: piece_f // 2]
        outs[j][piece_d:, width:] = weight[piece_f // 2 :]
        weight = dot(turned_ref[...], grad_pre).astype(BF16)
        for i in range(LINE):
            outs[i][:piece_d, part] = weight[i * piece_d : (i + 1) * piece_d]
    high = total.astype(BF16).astype(F32)
    lane = lax.broadcasted_iota(jnp.int32, extra_ref.shape, 1)
    extra_ref[...] = jnp.where(lane == 0, high, jnp.where(lane == 1, total - high, 0.0)).astype(BF16)


def back_kernel(sources, capacity, me, gpre_ref, w_in_ref, extra_ref, out_ref):
    width = w_in_ref.shape[0]
    grad = dot(gpre_ref[...], w_in_ref[...], ((1,), (1,))).astype(BF16)
    for j in range(sources):
        block = slice(j * capacity, (j + 1) * capacity)
        source = jnp.bitwise_xor(block_base(me, sources), j)
        out_ref[source, :, :width] = grad[block]
        out_ref[source, :, width:] = extra_ref[block, :]


def finish_kernel(target_ref, gate_ref, tok_ref, gain_ref, go_ref, back_ref, tokens_out, gate_out):
    rows = back_ref.shape[0]
    tok_rows, width = tok_ref.shape
    spots = jnp.broadcast_to(target_ref[...].astype(F32), (8, tok_rows)).T[:, :1].astype(jnp.int32)
    hit = lax.broadcasted_iota(jnp.int32, (tok_rows, rows), 1) == spots
    got = dot(jnp.where(hit, 1.0, 0.0).astype(BF16), back_ref[...])
    sums = got[:, width:].T
    gate_row = gate_ref[...].astype(F32).reshape(1, tok_rows)
    gate_out[...] = ((sums[0:1] + sums[1:2]) / gate_row).astype(BF16).reshape(tok_rows)
    scaled, spread = normalize(tok_ref[...])
    grad = got[:, :width] * gain_ref[...]
    mean = jnp.mean(grad, axis=-1, keepdims=True)
    cross = jnp.mean(grad * scaled, axis=-1, keepdims=True)
    branch = spread * (grad - mean - scaled * cross)
    tokens_out[...] = (go_ref[...].astype(F32) + branch).astype(BF16)


def swap_blocks(blocks):
    count = len(blocks)
    return [
        blocks[j]
        if j == count - 2
        else lax.ppermute(blocks[j], "space", [(i, i ^ j ^ (count - 2)) for i in range(count)])
        for j in range(count)
    ]


def is_inner(place):
    return (place[0] == 1) | (place[0] == 2)


def pass_kernel(place, third_ref, swapped_ref, out_ref):
    swapped = jnp.where(is_inner(place), swapped_ref[...].astype(F32), 0.0)
    out_ref[...] = (third_ref[...].astype(F32) + swapped).astype(BF16)


def total_kernel(place, own_ref, middle_ref, across_ref, outer_ref, swapped_ref, last_ref, in_ref, out_ref):
    piece_d, half = in_ref.shape[0], out_ref.shape[0] // 2
    width = out_ref.shape[1]
    swapped = jnp.where(is_inner(place), 0.0, swapped_ref[...].astype(F32))
    total = own_ref[...].astype(F32) + swapped
    for ref in (middle_ref, across_ref, outer_ref, last_ref):
        total += ref[...].astype(F32)
    in_ref[...] = total[:piece_d]
    out_ref[:half, :] = total[piece_d:, :width]
    out_ref[half:, :] = total[piece_d:, width:]


def line_sums(place, first, second, third, own, width):
    swapped = lax.ppermute(first, "dp", [(0, 1), (1, 0), (2, 3), (3, 2)])
    middle = lax.ppermute(second, "dp", [(1, 2), (2, 1)])
    across = lax.ppermute(second, "dp", [(0, 2), (3, 1)])
    outer = lax.ppermute(third, "dp", [(0, 1), (3, 2)])
    (passed,) = kernel_call(
        pass_kernel,
        "pass",
        1,
        1,
        [jax.ShapeDtypeStruct(third.shape, BF16)],
        [smem] + [vmem] * 2,
        vmem_mib=56,
    )(place, third, swapped)
    last = lax.ppermute(passed, "dp", [(1, 3), (2, 0)])
    rows, hidden = own.shape
    piece_d = width // LINE
    return kernel_call(
        total_kernel,
        "total",
        1,
        1,
        [
            jax.ShapeDtypeStruct((piece_d, hidden), F32),
            jax.ShapeDtypeStruct((2 * (rows - piece_d), width), F32),
        ],
        [smem] + [vmem] * 6,
        vmem_mib=56,
    )(place, own, middle, across, outer, swapped, last)


def body(tokens, gain, w_in, w_out, expert_ids, gate, grad_out):
    sources = lax.axis_size("space")
    groups = lax.axis_size("dp")
    tok_rows, width = tokens.shape
    hidden = w_in.shape[2]
    capacity = ((tok_rows * 5 // 4 + sources - 1) // sources + 7) // 8 * 8
    rows = sources * capacity
    me = lax.axis_index("space").astype(jnp.int32).reshape(1)
    place = lax.axis_index("dp").astype(jnp.int32).reshape(1)
    ids_row = expert_ids.reshape(1, tok_rows)
    gain_row = gain.reshape(1, width)
    weight_in, weight_out = w_in[0], w_out[0]
    shape = jax.ShapeDtypeStruct
    sems = pltpu.SemaphoreType.DMA
    block_place = vmem if capacity % 16 else anywhere
    io_bytes = 2 * (2 * tok_rows * width + 2 * rows * width)

    target, *sent = kernel_call(
        functools.partial(place_kernel, sources, capacity),
        "place",
        4 * rows * tok_rows * width,
        io_bytes,
        [shape((1, tok_rows), jnp.int32)]
        + [shape((capacity, 2 * width), BF16)] * sources,
        [smem] * 2 + [hbm] * 5,
        [
            pltpu.VMEM((1, tok_rows), jnp.int32),
            pltpu.VMEM((tok_rows,), BF16),
            pltpu.VMEM((tok_rows, width), BF16),
            pltpu.VMEM((1, width), F32),
            pltpu.VMEM((tok_rows, width), BF16),
            pltpu.VMEM((rows, 2 * width), BF16),
            sems((5,)),
            sems((2, sources)),
        ],
        places=[vmem] + [block_place] * sources,
        vmem_mib=56,
    )(me, place, ids_row, gate, tokens, gain_row, grad_out)
    (kept,) = kernel_call(
        keep_kernel,
        "keep",
        1,
        1,
        [shape((capacity, 2 * width), BF16)],
        [vmem],
        vmem_mib=2,
    )(sent[sources - 2])
    arrived = swap_blocks(sent)
    arrived[sources - 2] = kept

    *parts, gpre, extra = kernel_call(
        functools.partial(grads_kernel, sources, capacity, groups),
        "grads",
        8 * rows * width * hidden,
        2 * (2 * rows * width + 4 * width * hidden + rows * hidden),
        [shape((width // LINE + hidden // LINE // 2, hidden), BF16)] * LINE
        + [shape((rows, hidden), BF16), shape((rows, LANES), BF16)],
        [smem] + [vmem] * 2 + [block_place] * sources,
        [
            pltpu.VMEM((rows, 2 * width), BF16),
            pltpu.VMEM((width, rows), BF16),
            sems((sources,)),
        ],
    )(place, weight_in, weight_out, *arrived)
    (returned,) = kernel_call(
        functools.partial(back_kernel, sources, capacity),
        "back",
        1,
        1,
        [shape((sources, capacity, width + LANES), BF16)],
        [smem] + [vmem] * 3,
    )(me, gpre, weight_in, extra)

    if groups == LINE:
        grad_w_in, grad_w_out = line_sums(place, *parts, width)
    else:
        parts_in, parts_out = zip(*[split_piece(part, width, LINE) for part in parts])
        grad_w_in, grad_w_out = (
            lax.psum_scatter(
                jnp.concatenate(part), "dp", scatter_dimension=0, tiled=True
            ).astype(F32)
            for part in (parts_in, parts_out)
        )
    back = lax.all_to_all(returned, "space", split_axis=0, concat_axis=0, tiled=True)
    grad_tokens, grad_gate = kernel_call(
        finish_kernel,
        "finish",
        1,
        1,
        [shape((tok_rows, width), BF16), shape((tok_rows,), BF16)],
        [vmem] * 6,
    )(target, gate, tokens, gain_row, grad_out, back.reshape(rows, width + LANES))
    return (grad_tokens, grad_gate, grad_w_in[None], grad_w_out[None])


def split_piece(piece, width, pieces):
    piece_d = width // pieces
    lower = piece[piece_d:]
    return piece[:piece_d], jnp.concatenate([lower[:, :width], lower[:, width:]])


def solution(mesh):
    placed = (
        P(("space", "dp"), None),
        P(),
        P("space", None, None),
        P("space", None, None),
        P(("space", "dp"), None),
        P(("space", "dp")),
        P(("space", "dp"), None),
    )
    return jax.shard_map(
        body,
        mesh=mesh,
        in_specs=placed,
        out_specs=(
            P(("space", "dp"), None),
            P(("space", "dp")),
            P("space", "dp", None),
            P("space", "dp", None),
        ),
        check_vma=False,
    )
```

```python
import functools

import jax
import jax.numpy as jnp
from jax import lax
from jax.experimental import pallas as pl
from jax.experimental.pallas import tpu as pltpu
from jax.sharding import PartitionSpec as P

epsilon = 1e-05
F32 = jnp.float32
BF16 = jnp.bfloat16
LANES = 128
LINE = 4
MIB = 1024 * 1024

vmem = pl.BlockSpec(memory_space=pltpu.VMEM)
smem = pl.BlockSpec(memory_space=pltpu.SMEM)
hbm = pl.BlockSpec(memory_space=pltpu.HBM)
anywhere = pl.BlockSpec(memory_space=pl.ANY)


def dot(left, right, contract=((1,), (0,))):
    return lax.dot_general(left, right, (contract, ((), ())), preferred_element_type=F32)


def normalize(tokens):
    values = tokens.astype(F32)
    center = values - jnp.mean(values, axis=-1, keepdims=True)
    spread = lax.rsqrt(jnp.mean(center * center, axis=-1, keepdims=True) + epsilon)
    return center * spread, spread


def kernel_call(kernel, name, flops, nbytes, outs, ins, scratch=(), places=None, vmem_mib=24):
    return pl.pallas_call(
        kernel,
        name=name,
        out_shape=outs,
        in_specs=ins,
        out_specs=places or [vmem] * len(outs),
        scratch_shapes=list(scratch),
        compiler_params=pltpu.CompilerParams(vmem_limit_bytes=vmem_mib * MIB),
        cost_estimate=pl.CostEstimate(flops=flops, bytes_accessed=nbytes, transcendentals=0),
    )


def start_copies(pairs, sems):
    copies = [pltpu.make_async_copy(src, dst, sems.at[i]) for i, (src, dst) in enumerate(pairs)]
    for copy in copies:
        copy.start()
    return copies


def block_base(me, sources):
    return jnp.bitwise_xor(me[0], sources - 2)


def place_kernel(
    sources, capacity, me, place, ids_hbm, gate_hbm, tok_hbm, gain_hbm, go_hbm, target_ref, *refs
):
    outs = refs[:sources]
    ids_ref, gate_ref, tok_ref, gain_ref, go_ref, sent_ref, in_sems, out_sems = refs[sources:]
    rows = sources * capacity
    tok_rows, width = tok_ref.shape
    loads = start_copies(
        [(ids_hbm, ids_ref), (tok_hbm, tok_ref), (gain_hbm, gain_ref), (gate_hbm, gate_ref), (go_hbm, go_ref)],
        in_sems,
    )
    mine = block_base(me, sources)
    earlier = lax.broadcasted_iota(jnp.int32, (tok_rows, tok_rows), 0) < lax.broadcasted_iota(
        jnp.int32, (tok_rows, tok_rows), 1
    )
    earlier = jnp.where(earlier, 1.0, 0.0).astype(BF16)
    for copy in loads:
        copy.wait()
    ids = ids_ref[...]
    onehot = (lax.broadcasted_iota(jnp.int32, (sources, tok_rows), 0) == ids).astype(F32)
    before = dot(onehot.astype(BF16), earlier)
    rank = jnp.sum(before * onehot, axis=0, keepdims=True).astype(jnp.int32)
    kept = rank < capacity
    target_ref[...] = jnp.where(kept, ids * capacity + rank, -1)
    target = jnp.where(kept, jnp.bitwise_xor(ids, mine) * capacity + rank, -1)
    hit = lax.broadcasted_iota(jnp.int32, (rows, tok_rows), 0) == target
    gate = gate_ref[...].astype(F32).reshape(1, tok_rows)
    scaled, _ = normalize(tok_ref[...])
    normed = (scaled * gain_ref[...]).astype(BF16)
    stores = []
    for part, (weight, values) in enumerate(((gate, go_ref[...]), (1.0, normed))):
        columns = pl.ds((1 - part) * width, width)
        sent_ref[:, columns] = dot(jnp.where(hit, weight, 0.0).astype(BF16), values).astype(BF16)
        spans = [pl.ds(j * capacity, capacity) for j in range(sources)]
        if capacity % 16:
            for j in range(sources):
                outs[j][:, columns] = sent_ref[spans[j], columns]
        else:
            stores += start_copies(
                [(sent_ref.at[spans[j], columns], outs[j].at[:, columns]) for j in range(sources)],
                out_sems.at[part],
            )
    for copy in stores:
        copy.wait()


def keep_kernel(block_ref, out_ref):
    out_ref[...] = block_ref[...]


def gelu_parts(value):
    root = 0.7978845608028654
    cubic = root * 0.044715
    square = value * value
    tan = jnp.tanh(value * (root + cubic * square))
    half = 0.5 + 0.5 * tan
    act = value * half
    return act, half + act * (1.0 - tan) * (root + 3.0 * cubic * square)


def shard_order(place):
    first = jnp.where(lax.rem(place, 2) == 0, 3, 0)
    second = jnp.where(place < 2, 2, 1)
    return [first, second, 6 - first - second - place, place]


def expert_work(order, blocks, w_in_ref, w_out_ref, gpre_ref, extra_ref, rows_ref, turned_ref, put):
    capacity = blocks[0].shape[0]
    width, hidden = w_in_ref.shape
    piece_d, piece_f = width // LINE, hidden // LINE
    for j, block in enumerate(blocks):
        rows_ref[j * capacity : (j + 1) * capacity, :] = block[...]
    for j in range(LINE):
        start = pl.multiple_of(order[j] * piece_d, piece_d)
        turned_ref[j * piece_d : (j + 1) * piece_d, :] = rows_ref[:, pl.ds(start, piece_d)].T
    total = jnp.zeros(extra_ref.shape, F32)
    for j in range(LINE):
        part = pl.ds(pl.multiple_of(order[j] * piece_f, piece_f), piece_f)
        delta = rows_ref[:, width:]
        act, slope = gelu_parts(dot(rows_ref[:, :width], w_in_ref[:, part]))
        grad_act = dot(delta, w_out_ref[part, :], ((1,), (1,)))
        products = act * grad_act
        for lane in range(0, piece_f, LANES):
            total += products[:, lane : lane + LANES]
        grad_pre = (grad_act * slope).astype(BF16)
        gpre_ref[:, part] = grad_pre
        put(j, part, dot(turned_ref[...], grad_pre), dot(act.astype(BF16).T, delta))
    total = jnp.sum(total, axis=1, keepdims=True)
    high = total.astype(BF16).astype(F32)
    lane = lax.broadcasted_iota(jnp.int32, extra_ref.shape, 1)
    extra_ref[...] = jnp.where(lane == 0, high, jnp.where(lane == 1, total - high, 0.0)).astype(BF16)


def sooner_kernel(count, groups, place, w_in_ref, w_out_ref, *refs):
    blocks = refs[:count]
    sum_in_ref, sum_out_ref, gpre_ref, extra_ref, rows_ref, turned_ref = refs[count:]
    piece_f = w_in_ref.shape[1] // LINE

    def put(j, part, weight_in, weight_out):
        sum_in_ref[:, part] = weight_in
        sum_out_ref[j * piece_f : (j + 1) * piece_f, :] = weight_out

    order = shard_order(place[0]) if groups == LINE else list(range(LINE))
    expert_work(order, blocks, w_in_ref, w_out_ref, gpre_ref, extra_ref, rows_ref, turned_ref, put)


def later_kernel(count, groups, place, w_in_ref, w_out_ref, sum_in_ref, sum_out_ref, *refs):
    blocks = refs[:count]
    outs = refs[count : count + LINE]
    gpre_ref, extra_ref, rows_ref, turned_ref = refs[count + LINE :]
    width, hidden = w_in_ref.shape
    piece_d, piece_f = width // LINE, hidden // LINE

    def put(j, part, weight_in, weight_out):
        weight = (sum_out_ref[j * piece_f : (j + 1) * piece_f, :] + weight_out).astype(BF16)
        outs[j][piece_d:, :width] = weight[: piece_f // 2]
        outs[j][piece_d:, width:] = weight[piece_f // 2 :]
        weight = (sum_in_ref[:, part] + weight_in).astype(BF16)
        for i in range(LINE):
            outs[i][:piece_d, part] = weight[i * piece_d : (i + 1) * piece_d]

    order = shard_order(place[0]) if groups == LINE else list(range(LINE))
    expert_work(order, blocks, w_in_ref, w_out_ref, gpre_ref, extra_ref, rows_ref, turned_ref, put)


def back_kernel(sources, capacity, sets, me, w_in_ref, *refs):
    out_ref = refs[-1]
    width = w_in_ref.shape[0]
    for members, gpre_ref, extra_ref in zip(sets, refs[0:-1:2], refs[1:-1:2]):
        grad = dot(gpre_ref[...], w_in_ref[...], ((1,), (1,))).astype(BF16)
        for i, j in enumerate(members):
            block = slice(i * capacity, (i + 1) * capacity)
            source = jnp.bitwise_xor(block_base(me, sources), j)
            out_ref[source, :, :width] = grad[block]
            out_ref[source, :, width:] = extra_ref[block, :]


def finish_kernel(target_ref, gate_ref, tok_ref, gain_ref, go_ref, back_ref, tokens_out, gate_out):
    rows = back_ref.shape[0]
    tok_rows, width = tok_ref.shape
    spots = jnp.broadcast_to(target_ref[...].astype(F32), (8, tok_rows)).T[:, :1].astype(jnp.int32)
    hit = lax.broadcasted_iota(jnp.int32, (tok_rows, rows), 1) == spots
    got = dot(jnp.where(hit, 1.0, 0.0).astype(BF16), back_ref[...])
    sums = got[:, width:].T
    gate_row = gate_ref[...].astype(F32).reshape(1, tok_rows)
    gate_out[...] = ((sums[0:1] + sums[1:2]) / gate_row).astype(BF16).reshape(tok_rows)
    scaled, spread = normalize(tok_ref[...])
    grad = got[:, :width] * gain_ref[...]
    mean = jnp.mean(grad, axis=-1, keepdims=True)
    cross = jnp.mean(grad * scaled, axis=-1, keepdims=True)
    branch = spread * (grad - mean - scaled * cross)
    tokens_out[...] = (go_ref[...].astype(F32) + branch).astype(BF16)


def swap_blocks(blocks):
    count = len(blocks)
    return [
        blocks[j]
        if j == count - 2
        else lax.ppermute(blocks[j], "space", [(i, i ^ j ^ (count - 2)) for i in range(count)])
        for j in range(count)
    ]


def is_inner(place):
    return (place[0] == 1) | (place[0] == 2)


def pass_kernel(place, third_ref, swapped_ref, own_ref, out_ref, sum_ref):
    swapped = swapped_ref[...].astype(F32)
    onward = jnp.where(is_inner(place), swapped, 0.0)
    out_ref[...] = (third_ref[...].astype(F32) + onward).astype(BF16)
    sum_ref[...] = own_ref[...].astype(F32) + (swapped - onward)


def most_kernel(sum_ref, middle_ref, across_ref, outer_ref, out_ref):
    total = sum_ref[...]
    for ref in (middle_ref, across_ref, outer_ref):
        total += ref[...].astype(F32)
    out_ref[...] = total


def total_kernel(sum_ref, last_ref, in_ref, out_ref):
    piece_d, half = in_ref.shape[0], out_ref.shape[0] // 2
    width = out_ref.shape[1]
    total = sum_ref[...] + last_ref[...].astype(F32)
    in_ref[...] = total[:piece_d]
    out_ref[:half, :] = total[piece_d:, :width]
    out_ref[half:, :] = total[piece_d:, width:]


def line_sums(place, first, second, third, own, width, behind):
    swapped = lax.ppermute(first, "dp", [(0, 1), (1, 0), (2, 3), (3, 2)])
    middle = lax.ppermute(second, "dp", [(1, 2), (2, 1)])
    across = lax.ppermute(second, "dp", [(0, 2), (3, 1)])
    swapped, behind = lax.optimization_barrier((swapped, behind))
    outer = lax.ppermute(third, "dp", [(0, 1), (3, 2)])
    rows, hidden = own.shape
    piece_d = width // LINE
    whole = jax.ShapeDtypeStruct(own.shape, F32)
    passed, some = kernel_call(
        pass_kernel,
        "pass",
        1,
        1,
        [jax.ShapeDtypeStruct(own.shape, BF16), whole],
        [smem] + [vmem] * 3,
    )(place, third, swapped, own)
    last = lax.ppermute(passed, "dp", [(1, 3), (2, 0)])
    (most,) = kernel_call(
        most_kernel, "most", 1, 1, [whole], [vmem] * 4, vmem_mib=56
    )(some, middle, across, outer)
    sums = kernel_call(
        total_kernel,
        "total",
        1,
        1,
        [
            jax.ShapeDtypeStruct((piece_d, hidden), F32),
            jax.ShapeDtypeStruct((2 * (rows - piece_d), width), F32),
        ],
        [vmem] * 2,
        vmem_mib=56,
    )(most, last)
    return *sums, behind


def body(tokens, gain, w_in, w_out, expert_ids, gate, grad_out):
    sources = lax.axis_size("space")
    groups = lax.axis_size("dp")
    tok_rows, width = tokens.shape
    hidden = w_in.shape[2]
    capacity = ((tok_rows * 5 // 4 + sources - 1) // sources + 7) // 8 * 8
    rows = sources * capacity
    me = lax.axis_index("space").astype(jnp.int32).reshape(1)
    place = lax.axis_index("dp").astype(jnp.int32).reshape(1)
    ids_row = expert_ids.reshape(1, tok_rows)
    gain_row = gain.reshape(1, width)
    weight_in, weight_out = w_in[0], w_out[0]
    shape = jax.ShapeDtypeStruct
    sems = pltpu.SemaphoreType.DMA
    block_place = vmem if capacity % 16 else anywhere
    io_bytes = 2 * (2 * tok_rows * width + 2 * rows * width)

    target, *sent = kernel_call(
        functools.partial(place_kernel, sources, capacity),
        "place",
        4 * rows * tok_rows * width,
        io_bytes,
        [shape((1, tok_rows), jnp.int32)]
        + [shape((capacity, 2 * width), BF16)] * sources,
        [smem] * 2 + [hbm] * 5,
        [
            pltpu.VMEM((1, tok_rows), jnp.int32),
            pltpu.VMEM((tok_rows,), BF16),
            pltpu.VMEM((tok_rows, width), BF16),
            pltpu.VMEM((1, width), F32),
            pltpu.VMEM((tok_rows, width), BF16),
            pltpu.VMEM((rows, 2 * width), BF16),
            sems((5,)),
            sems((2, sources)),
        ],
        places=[vmem] + [block_place] * sources,
        vmem_mib=56,
    )(me, place, ids_row, gate, tokens, gain_row, grad_out)
    (kept,) = kernel_call(
        keep_kernel,
        "keep",
        1,
        1,
        [shape((capacity, 2 * width), BF16)],
        [vmem],
        vmem_mib=2,
    )(sent[sources - 2])
    arrived = swap_blocks(sent)
    arrived[sources - 2] = kept

    late_set = list(range(3 * sources // 8, 6 * sources // 8))
    soon_set = [j for j in range(sources) if j not in late_set]

    def work(kernel, name, members, outs, *sums):
        count, span = len(members), len(members) * capacity
        return kernel_call(
            functools.partial(kernel, count, groups),
            name,
            8 * span * width * hidden,
            2 * (2 * span * width + 4 * width * hidden + span * hidden),
            outs + [shape((span, hidden), BF16), shape((span, LANES), BF16)],
            [smem] + [vmem] * (2 + len(sums) + count),
            [pltpu.VMEM((span, 2 * width), BF16), pltpu.VMEM((width, span), BF16)],
        )(place, weight_in, weight_out, *sums, *[arrived[j] for j in members])

    *sums, soon_gpre, soon_extra = work(
        sooner_kernel, "sooner", soon_set, [shape((width, hidden), F32), shape((hidden, width), F32)]
    )
    piece = shape((width // LINE + hidden // LINE // 2, hidden), BF16)
    *parts, late_gpre, late_extra = work(later_kernel, "later", late_set, [piece] * LINE, *sums)
    (returned,) = kernel_call(
        functools.partial(back_kernel, sources, capacity, (soon_set, late_set)),
        "back",
        1,
        1,
        [shape((sources, capacity, width + LANES), BF16)],
        [smem] + [vmem] * 5,
    )(me, weight_in, soon_gpre, soon_extra, late_gpre, late_extra)

    if groups == LINE:
        grad_w_in, grad_w_out, returned = line_sums(place, *parts, width, returned)
    else:
        parts_in, parts_out = zip(*[split_piece(part, width, LINE) for part in parts])
        grad_w_in, grad_w_out = (
            lax.psum_scatter(
                jnp.concatenate(part), "dp", scatter_dimension=0, tiled=True
            ).astype(F32)
            for part in (parts_in, parts_out)
        )
    back = lax.all_to_all(returned, "space", split_axis=0, concat_axis=0, tiled=True)
    grad_tokens, grad_gate = kernel_call(
        finish_kernel,
        "finish",
        1,
        1,
        [shape((tok_rows, width), BF16), shape((tok_rows,), BF16)],
        [vmem] * 6,
    )(target, gate, tokens, gain_row, grad_out, back.reshape(rows, width + LANES))
    return (grad_tokens, grad_gate, grad_w_in[None], grad_w_out[None])


def split_piece(piece, width, pieces):
    piece_d = width // pieces
    lower = piece[piece_d:]
    return piece[:piece_d], jnp.concatenate([lower[:, :width], lower[:, width:]])


def solution(mesh):
    placed = (
        P(("space", "dp"), None),
        P(),
        P("space", None, None),
        P("space", None, None),
        P(("space", "dp"), None),
        P(("space", "dp")),
        P(("space", "dp"), None),
    )
    return jax.shard_map(
        body,
        mesh=mesh,
        in_specs=placed,
        out_specs=(
            P(("space", "dp"), None),
            P(("space", "dp")),
            P("space", "dp", None),
            P("space", "dp", None),
        ),
        check_vma=False,
    )
```

```python
import functools

import jax
import jax.numpy as jnp
from jax import lax
from jax.experimental import pallas as pl
from jax.experimental.pallas import tpu as pltpu
from jax.sharding import PartitionSpec as P

epsilon = 1e-05
F32 = jnp.float32
BF16 = jnp.bfloat16
LANES = 128
LINE = 4
MIB = 1024 * 1024

vmem = pl.BlockSpec(memory_space=pltpu.VMEM)
smem = pl.BlockSpec(memory_space=pltpu.SMEM)
hbm = pl.BlockSpec(memory_space=pltpu.HBM)
anywhere = pl.BlockSpec(memory_space=pl.ANY)


def dot(left, right, contract=((1,), (0,))):
    return lax.dot_general(left, right, (contract, ((), ())), preferred_element_type=F32)


def normalize(tokens):
    values = tokens.astype(F32)
    center = values - jnp.mean(values, axis=-1, keepdims=True)
    spread = lax.rsqrt(jnp.mean(center * center, axis=-1, keepdims=True) + epsilon)
    return center * spread, spread


def kernel_call(kernel, name, flops, nbytes, outs, ins, scratch=(), places=None, vmem_mib=24):
    return pl.pallas_call(
        kernel,
        name=name,
        out_shape=outs,
        in_specs=ins,
        out_specs=places or [vmem] * len(outs),
        scratch_shapes=list(scratch),
        compiler_params=pltpu.CompilerParams(vmem_limit_bytes=vmem_mib * MIB),
        cost_estimate=pl.CostEstimate(flops=flops, bytes_accessed=nbytes, transcendentals=0),
    )


def start_copies(pairs, sems):
    copies = [pltpu.make_async_copy(src, dst, sems.at[i]) for i, (src, dst) in enumerate(pairs)]
    for copy in copies:
        copy.start()
    return copies


def place_kernel(
    sources, capacity, me, place, ids_hbm, gate_hbm, tok_hbm, gain_hbm, go_hbm, target_ref, *refs
):
    outs = refs[:sources]
    ids_ref, gate_ref, tok_ref, gain_ref, go_ref, sent_ref, in_sems, out_sems = refs[sources:]
    rows = sources * capacity
    tok_rows, width = tok_ref.shape
    loads = start_copies(
        [(ids_hbm, ids_ref), (tok_hbm, tok_ref), (gain_hbm, gain_ref), (gate_hbm, gate_ref), (go_hbm, go_ref)],
        in_sems,
    )
    mine = jnp.bitwise_xor(me[0], sources - 2)
    earlier = lax.broadcasted_iota(jnp.int32, (tok_rows, tok_rows), 0) < lax.broadcasted_iota(
        jnp.int32, (tok_rows, tok_rows), 1
    )
    earlier = jnp.where(earlier, 1.0, 0.0).astype(BF16)
    for copy in loads:
        copy.wait()
    ids = ids_ref[...]
    onehot = (lax.broadcasted_iota(jnp.int32, (sources, tok_rows), 0) == ids).astype(F32)
    before = dot(onehot.astype(BF16), earlier)
    rank = jnp.sum(before * onehot, axis=0, keepdims=True).astype(jnp.int32)
    kept = rank < capacity
    target = jnp.where(kept, jnp.bitwise_xor(ids, mine) * capacity + rank, -1)
    target_ref[...] = target
    hit = lax.broadcasted_iota(jnp.int32, (rows, tok_rows), 0) == target
    gate = gate_ref[...].astype(F32).reshape(1, tok_rows)
    scaled, _ = normalize(tok_ref[...])
    normed = (scaled * gain_ref[...]).astype(BF16)
    stores = []
    for part, (weight, values) in enumerate(((gate, go_ref[...]), (1.0, normed))):
        columns = pl.ds((1 - part) * width, width)
        sent_ref[:, columns] = dot(jnp.where(hit, weight, 0.0).astype(BF16), values).astype(BF16)
        spans = [pl.ds(j * capacity, capacity) for j in range(sources)]
        if capacity % 16:
            for j in range(sources):
                outs[j][:, columns] = sent_ref[spans[j], columns]
        else:
            stores += start_copies(
                [(sent_ref.at[spans[j], columns], outs[j].at[:, columns]) for j in range(sources)],
                out_sems.at[part],
            )
    for copy in stores:
        copy.wait()


def keep_kernel(block_ref, out_ref):
    out_ref[...] = block_ref[...]


def gelu_parts(value):
    root = 0.7978845608028654
    cubic = root * 0.044715
    square = value * value
    tan = jnp.tanh(value * (root + cubic * square))
    half = 0.5 + 0.5 * tan
    act = value * half
    return act, half + act * (1.0 - tan) * (root + 3.0 * cubic * square)


def shard_order(place):
    first = jnp.where(lax.rem(place, 2) == 0, 3, 0)
    second = jnp.where(place < 2, 2, 1)
    return [first, second, 6 - first - second - place, place]


def expert_work(order, blocks, w_in_ref, w_out_ref, gpre_ref, extra_ref, rows_ref, turned_ref, put):
    capacity = blocks[0].shape[0]
    width, hidden = w_in_ref.shape
    piece_d, piece_f = width // LINE, hidden // LINE
    for j, block in enumerate(blocks):
        rows_ref[j * capacity : (j + 1) * capacity, :] = block[...]
    for j in range(LINE):
        start = pl.multiple_of(order[j] * piece_d, piece_d)
        turned_ref[j * piece_d : (j + 1) * piece_d, :] = rows_ref[:, pl.ds(start, piece_d)].T
    total = jnp.zeros(extra_ref.shape, F32)
    for j in range(LINE):
        part = pl.ds(pl.multiple_of(order[j] * piece_f, piece_f), piece_f)
        delta = rows_ref[:, width:]
        act, slope = gelu_parts(dot(rows_ref[:, :width], w_in_ref[:, part]))
        grad_act = dot(delta, w_out_ref[part, :], ((1,), (1,)))
        products = act * grad_act
        for lane in range(0, piece_f, LANES):
            total += products[:, lane : lane + LANES]
        grad_pre = (grad_act * slope).astype(BF16)
        gpre_ref[:, part] = grad_pre
        put(j, part, dot(turned_ref[...], grad_pre), dot(act.astype(BF16).T, delta))
    total = jnp.sum(total, axis=1, keepdims=True)
    high = total.astype(BF16).astype(F32)
    lane = lax.broadcasted_iota(jnp.int32, extra_ref.shape, 1)
    extra_ref[...] = jnp.where(lane == 0, high, jnp.where(lane == 1, total - high, 0.0)).astype(BF16)


def sooner_kernel(count, groups, place, w_in_ref, w_out_ref, *refs):
    blocks = refs[:count]
    sum_in_ref, sum_out_ref, gpre_ref, extra_ref, rows_ref, turned_ref = refs[count:]
    piece_f = w_in_ref.shape[1] // LINE

    def put(j, part, weight_in, weight_out):
        sum_in_ref[:, part] = weight_in
        sum_out_ref[j * piece_f : (j + 1) * piece_f, :] = weight_out

    order = shard_order(place[0]) if groups == LINE else list(range(LINE))
    expert_work(order, blocks, w_in_ref, w_out_ref, gpre_ref, extra_ref, rows_ref, turned_ref, put)


def later_kernel(count, groups, place, w_in_ref, w_out_ref, sum_in_ref, sum_out_ref, *refs):
    blocks = refs[:count]
    outs = refs[count : count + LINE]
    gpre_ref, extra_ref, rows_ref, turned_ref = refs[count + LINE :]
    width, hidden = w_in_ref.shape
    piece_d, piece_f = width // LINE, hidden // LINE

    def put(j, part, weight_in, weight_out):
        weight = (sum_out_ref[j * piece_f : (j + 1) * piece_f, :] + weight_out).astype(BF16)
        outs[j][piece_d:, :width] = weight[: piece_f // 2]
        outs[j][piece_d:, width:] = weight[piece_f // 2 :]
        weight = (sum_in_ref[:, part] + weight_in).astype(BF16)
        for i in range(LINE):
            outs[i][:piece_d, part] = weight[i * piece_d : (i + 1) * piece_d]

    order = shard_order(place[0]) if groups == LINE else list(range(LINE))
    expert_work(order, blocks, w_in_ref, w_out_ref, gpre_ref, extra_ref, rows_ref, turned_ref, put)


def back_kernel(capacity, sets, w_in_ref, *refs):
    inputs, outs = refs[:4], refs[4:]
    width = w_in_ref.shape[0]
    for members, gpre_ref, extra_ref in zip(sets, inputs[::2], inputs[1::2]):
        grad = dot(gpre_ref[...], w_in_ref[...], ((1,), (1,))).astype(BF16)
        for i, j in enumerate(members):
            block = slice(i * capacity, (i + 1) * capacity)
            outs[j][:, :width] = grad[block]
            outs[j][:, width:] = extra_ref[block, :]


def finish_kernel(target_ref, gate_ref, tok_ref, gain_ref, go_ref, *refs):
    *blocks, tokens_out, gate_out, back_ref = refs
    rows, capacity = back_ref.shape[0], blocks[0].shape[0]
    for j, block in enumerate(blocks):
        back_ref[j * capacity : (j + 1) * capacity, :] = block[...]
    tok_rows, width = tok_ref.shape
    spots = jnp.broadcast_to(target_ref[...].astype(F32), (8, tok_rows)).T[:, :1].astype(jnp.int32)
    hit = lax.broadcasted_iota(jnp.int32, (tok_rows, rows), 1) == spots
    got = dot(jnp.where(hit, 1.0, 0.0).astype(BF16), back_ref[...])
    sums = got[:, width:].T
    gate_row = gate_ref[...].astype(F32).reshape(1, tok_rows)
    gate_out[...] = ((sums[0:1] + sums[1:2]) / gate_row).astype(BF16).reshape(tok_rows)
    scaled, spread = normalize(tok_ref[...])
    grad = got[:, :width] * gain_ref[...]
    mean = jnp.mean(grad, axis=-1, keepdims=True)
    cross = jnp.mean(grad * scaled, axis=-1, keepdims=True)
    branch = spread * (grad - mean - scaled * cross)
    tokens_out[...] = (go_ref[...].astype(F32) + branch).astype(BF16)


def swap_blocks(blocks):
    count = len(blocks)
    return [
        blocks[j]
        if j == count - 2
        else lax.ppermute(blocks[j], "space", [(i, i ^ j ^ (count - 2)) for i in range(count)])
        for j in range(count)
    ]


def is_inner(place):
    return (place[0] == 1) | (place[0] == 2)


def pass_kernel(place, third_ref, own_ref, swapped_ref, middle_ref, across_ref, out_ref, sum_ref):
    swapped = swapped_ref[...].astype(F32)
    onward = jnp.where(is_inner(place), swapped, 0.0)
    out_ref[...] = (third_ref[...].astype(F32) + onward).astype(BF16)
    total = own_ref[...].astype(F32) + (swapped - onward)
    for ref in (middle_ref, across_ref):
        total += ref[...].astype(F32)
    sum_ref[...] = total


def total_kernel(sum_ref, last_ref, in_ref, out_ref):
    piece_d, half = in_ref.shape[0], out_ref.shape[0] // 2
    width = out_ref.shape[1]
    total = sum_ref[...] + last_ref[...].astype(F32)
    in_ref[...] = total[:piece_d]
    out_ref[:half, :] = total[piece_d:, :width]
    out_ref[half:, :] = total[piece_d:, width:]


def line_sums(place, first, second, third, own, width, ahead):
    rows, hidden = own.shape
    piece_d = width // LINE
    swapped = lax.ppermute(first, "dp", [(0, 1), (1, 0), (2, 3), (3, 2)])
    middle = lax.ppermute(second, "dp", [(1, 2), (2, 1)])
    across = lax.ppermute(second, "dp", [(0, 2), (3, 1)])
    third, *ahead = lax.optimization_barrier((third, *ahead))
    passed, most = kernel_call(
        pass_kernel,
        "pass",
        1,
        1,
        [jax.ShapeDtypeStruct(own.shape, BF16), jax.ShapeDtypeStruct(own.shape, F32)],
        [smem] + [vmem] * 5,
    )(place, third, own, swapped, middle, across)
    last = lax.ppermute(passed, "dp", [(0, 1), (3, 2), (1, 3), (2, 0)])
    sums = kernel_call(
        total_kernel,
        "total",
        1,
        1,
        [
            jax.ShapeDtypeStruct((piece_d, hidden), F32),
            jax.ShapeDtypeStruct((2 * (rows - piece_d), width), F32),
        ],
        [vmem] * 2,
    )(most, last)
    return *sums, ahead


def body(tokens, gain, w_in, w_out, expert_ids, gate, grad_out):
    sources = lax.axis_size("space")
    groups = lax.axis_size("dp")
    tok_rows, width = tokens.shape
    hidden = w_in.shape[2]
    capacity = ((tok_rows * 5 // 4 + sources - 1) // sources + 7) // 8 * 8
    rows = sources * capacity
    me = lax.axis_index("space").astype(jnp.int32).reshape(1)
    place = lax.axis_index("dp").astype(jnp.int32).reshape(1)
    ids_row = expert_ids.reshape(1, tok_rows)
    gain_row = gain.reshape(1, width)
    weight_in, weight_out = w_in[0], w_out[0]
    shape = jax.ShapeDtypeStruct
    sems = pltpu.SemaphoreType.DMA
    block_place = vmem if capacity % 16 else anywhere
    io_bytes = 2 * (2 * tok_rows * width + 2 * rows * width)

    target, *sent = kernel_call(
        functools.partial(place_kernel, sources, capacity),
        "place",
        4 * rows * tok_rows * width,
        io_bytes,
        [shape((1, tok_rows), jnp.int32)]
        + [shape((capacity, 2 * width), BF16)] * sources,
        [smem] * 2 + [hbm] * 5,
        [
            pltpu.VMEM((1, tok_rows), jnp.int32),
            pltpu.VMEM((tok_rows,), BF16),
            pltpu.VMEM((tok_rows, width), BF16),
            pltpu.VMEM((1, width), F32),
            pltpu.VMEM((tok_rows, width), BF16),
            pltpu.VMEM((rows, 2 * width), BF16),
            sems((5,)),
            sems((2, sources)),
        ],
        places=[vmem] + [block_place] * sources,
        vmem_mib=56,
    )(me, place, ids_row, gate, tokens, gain_row, grad_out)
    (kept,) = kernel_call(
        keep_kernel,
        "keep",
        1,
        1,
        [shape((capacity, 2 * width), BF16)],
        [vmem],
        vmem_mib=2,
    )(sent[sources - 2])
    arrived = swap_blocks(sent)
    arrived[sources - 2] = kept

    late_set = list(range(3 * sources // 8, 6 * sources // 8))
    soon_set = [j for j in range(sources) if j not in late_set]

    def work(kernel, name, members, outs, *sums):
        count, span = len(members), len(members) * capacity
        return kernel_call(
            functools.partial(kernel, count, groups),
            name,
            8 * span * width * hidden,
            2 * (2 * span * width + 4 * width * hidden + span * hidden),
            outs + [shape((span, hidden), BF16), shape((span, LANES), BF16)],
            [smem] + [vmem] * (2 + len(sums) + count),
            [pltpu.VMEM((span, 2 * width), BF16), pltpu.VMEM((width, span), BF16)],
        )(place, weight_in, weight_out, *sums, *[arrived[j] for j in members])

    *sums, soon_gpre, soon_extra = work(
        sooner_kernel, "sooner", soon_set, [shape((width, hidden), F32), shape((hidden, width), F32)]
    )
    piece = shape((width // LINE + hidden // LINE // 2, hidden), BF16)
    *parts, late_gpre, late_extra = work(later_kernel, "later", late_set, [piece] * LINE, *sums)
    returned = kernel_call(
        functools.partial(back_kernel, capacity, (soon_set, late_set)),
        "back",
        1,
        1,
        [shape((capacity, width + LANES), BF16)] * sources,
        [vmem] * 5,
    )(weight_in, soon_gpre, soon_extra, late_gpre, late_extra)

    back = swap_blocks(returned)
    if groups == LINE:
        grad_w_in, grad_w_out, back[: sources // 2] = line_sums(
            place, *parts, width, back[: sources // 2]
        )
    else:
        parts_in, parts_out = zip(*[split_piece(part, width, LINE) for part in parts])
        grad_w_in, grad_w_out = (
            lax.psum_scatter(
                jnp.concatenate(part), "dp", scatter_dimension=0, tiled=True
            ).astype(F32)
            for part in (parts_in, parts_out)
        )
    grad_tokens, grad_gate = kernel_call(
        finish_kernel,
        "finish",
        1,
        1,
        [shape((tok_rows, width), BF16), shape((tok_rows,), BF16)],
        [vmem] * (5 + sources),
        [pltpu.VMEM((rows, width + LANES), BF16)],
    )(target, gate, tokens, gain_row, grad_out, *back)
    return (grad_tokens, grad_gate, grad_w_in[None], grad_w_out[None])


def split_piece(piece, width, pieces):
    piece_d = width // pieces
    lower = piece[piece_d:]
    return piece[:piece_d], jnp.concatenate([lower[:, :width], lower[:, width:]])


def solution(mesh):
    placed = (
        P(("space", "dp"), None),
        P(),
        P("space", None, None),
        P("space", None, None),
        P(("space", "dp"), None),
        P(("space", "dp")),
        P(("space", "dp"), None),
    )
    return jax.shard_map(
        body,
        mesh=mesh,
        in_specs=placed,
        out_specs=(
            P(("space", "dp"), None),
            P(("space", "dp")),
            P("space", "dp", None),
            P("space", "dp", None),
        ),
        check_vma=False,
    )
```

```python
import functools

import jax
import jax.numpy as jnp
from jax import lax
from jax.experimental import pallas as pl
from jax.experimental.pallas import tpu as pltpu
from jax.sharding import PartitionSpec as P

epsilon = 1e-05
F32 = jnp.float32
BF16 = jnp.bfloat16
LANES = 128
LINE = 4
MIB = 1024 * 1024

vmem = pl.BlockSpec(memory_space=pltpu.VMEM)
smem = pl.BlockSpec(memory_space=pltpu.SMEM)
hbm = pl.BlockSpec(memory_space=pltpu.HBM)
anywhere = pl.BlockSpec(memory_space=pl.ANY)


def dot(left, right, contract=((1,), (0,))):
    return lax.dot_general(left, right, (contract, ((), ())), preferred_element_type=F32)


def normalize(tokens):
    values = tokens.astype(F32)
    center = values - jnp.mean(values, axis=-1, keepdims=True)
    spread = lax.rsqrt(jnp.mean(center * center, axis=-1, keepdims=True) + epsilon)
    return center * spread, spread


def kernel_call(kernel, name, flops, nbytes, outs, ins, scratch=(), places=None, vmem_mib=24):
    return pl.pallas_call(
        kernel,
        name=name,
        out_shape=outs,
        in_specs=ins,
        out_specs=places or [vmem] * len(outs),
        scratch_shapes=list(scratch),
        compiler_params=pltpu.CompilerParams(vmem_limit_bytes=vmem_mib * MIB),
        cost_estimate=pl.CostEstimate(flops=flops, bytes_accessed=nbytes, transcendentals=0),
    )


def start_copies(pairs, sems):
    copies = [pltpu.make_async_copy(src, dst, sems.at[i]) for i, (src, dst) in enumerate(pairs)]
    for copy in copies:
        copy.start()
    return copies


def place_kernel(
    sources, capacity, me, place, ids_hbm, gate_hbm, tok_hbm, gain_hbm, go_hbm, target_ref, *refs
):
    outs = refs[:sources]
    wide_ref, ids_ref, gate_ref, tok_ref, gain_ref, go_ref, sent_ref, in_sems, out_sems = refs[sources:]
    rows = sources * capacity
    tok_rows, width = tok_ref.shape
    loads = start_copies(
        [(ids_hbm, ids_ref), (tok_hbm, tok_ref), (gain_hbm, gain_ref), (gate_hbm, gate_ref), (go_hbm, go_ref)],
        in_sems,
    )
    earlier = lax.broadcasted_iota(jnp.int32, (LANES, LANES), 0) < lax.broadcasted_iota(
        jnp.int32, (LANES, LANES), 1
    )
    earlier = jnp.where(earlier, 1.0, 0.0).astype(BF16)
    loads[0].wait()
    chunks = range(0, tok_rows, LANES)
    wide_ref[...] = jnp.full_like(wide_ref, -1)
    wide_ref[:, :tok_rows] = ids_ref[...]
    ids = [wide_ref[:, c : c + LANES] for c in chunks]
    expert = lax.broadcasted_iota(jnp.int32, (sources, LANES), 0)
    onehots = [jnp.where(expert == chunk, 1.0, 0.0) for chunk in ids]
    within = dot(jnp.concatenate(onehots).astype(BF16), earlier)
    base = jnp.zeros((sources, 1), F32)
    for i, (c, chunk, onehot) in enumerate(zip(chunks, ids, onehots)):
        before = within[i * sources : (i + 1) * sources] + base
        base += jnp.sum(onehot, axis=1, keepdims=True)
        rank = jnp.sum(before * onehot, axis=0, keepdims=True).astype(jnp.int32)
        away = jnp.bitwise_xor(chunk, me[0])
        block = jnp.zeros_like(away)
        for j, k in enumerate(block_order(sources)):
            block = jnp.where(away == k, j, block)
        end = min(LANES, tok_rows - c)
        target = jnp.where(rank < capacity, block * capacity + rank, -1)
        target_ref[:, c : c + end] = target[:, :end]
    target = target_ref[...]
    for copy in loads[1:]:
        copy.wait()
    hit = lax.broadcasted_iota(jnp.int32, (rows, tok_rows), 0) == target
    gate = gate_ref[...].astype(F32).reshape(1, tok_rows)
    scaled, _ = normalize(tok_ref[...])
    normed = (scaled * gain_ref[...]).astype(BF16)
    stores = []
    for part, (weight, values) in enumerate(((gate, go_ref[...]), (1.0, normed))):
        columns = pl.ds((1 - part) * width, width)
        sent_ref[:, columns] = dot(jnp.where(hit, weight, 0.0).astype(BF16), values).astype(BF16)
        spans = [pl.ds(j * capacity, capacity) for j in range(sources)]
        if capacity % 16:
            for j in range(sources):
                outs[j][:, columns] = sent_ref[spans[j], columns]
        else:
            stores += start_copies(
                [(sent_ref.at[spans[j], columns], outs[j].at[:, columns]) for j in range(sources)],
                out_sems.at[part],
            )
    for copy in stores:
        copy.wait()


def keep_kernel(block_ref, out_ref):
    out_ref[...] = block_ref[...]


def gelu_parts(value):
    root = 0.7978845608028654
    cubic = root * 0.044715
    square = value * value
    tan = jnp.tanh(value * (root + cubic * square))
    half = 0.5 + 0.5 * tan
    act = value * half
    return act, half + act * (1.0 - tan) * (root + 3.0 * cubic * square)


def shard_order(place):
    first = jnp.where(lax.rem(place, 2) == 0, 3, 0)
    second = jnp.where(place < 2, 2, 1)
    return [first, second, 6 - first - second - place, place]


def expert_work(order, blocks, w_in_ref, w_out_ref, gpre_ref, extra_ref, rows_ref, turned_ref, put):
    capacity = blocks[0].shape[0]
    width, hidden = w_in_ref.shape
    piece_d, piece_f = width // LINE, hidden // LINE
    for j, block in enumerate(blocks):
        rows_ref[j * capacity : (j + 1) * capacity, :] = block[...]
    for j in range(LINE):
        start = pl.multiple_of(order[j] * piece_d, piece_d)
        turned_ref[j * piece_d : (j + 1) * piece_d, :] = rows_ref[:, pl.ds(start, piece_d)].T
    total = jnp.zeros(extra_ref.shape, F32)
    for j in range(LINE):
        part = pl.ds(pl.multiple_of(order[j] * piece_f, piece_f), piece_f)
        delta = rows_ref[:, width:]
        act, slope = gelu_parts(dot(rows_ref[:, :width], w_in_ref[:, part]))
        grad_act = dot(delta, w_out_ref[part, :], ((1,), (1,)))
        products = act * grad_act
        for lane in range(0, piece_f, LANES):
            total += products[:, lane : lane + LANES]
        grad_pre = (grad_act * slope).astype(BF16)
        gpre_ref[:, part] = grad_pre
        put(j, part, dot(turned_ref[...], grad_pre), dot(act.astype(BF16).T, delta))
    total = jnp.sum(total, axis=1, keepdims=True)
    high = total.astype(BF16).astype(F32)
    lane = lax.broadcasted_iota(jnp.int32, extra_ref.shape, 1)
    extra_ref[...] = jnp.where(lane == 0, high, jnp.where(lane == 1, total - high, 0.0)).astype(BF16)


def sooner_kernel(count, groups, place, w_in_ref, w_out_ref, *refs):
    blocks = refs[:count]
    sum_in_ref, sum_out_ref, gpre_ref, extra_ref, rows_ref, turned_ref = refs[count:]
    piece_f = w_in_ref.shape[1] // LINE

    def put(j, part, weight_in, weight_out):
        sum_in_ref[:, part] = weight_in
        sum_out_ref[j * piece_f : (j + 1) * piece_f, :] = weight_out

    order = shard_order(place[0]) if groups == LINE else list(range(LINE))
    expert_work(order, blocks, w_in_ref, w_out_ref, gpre_ref, extra_ref, rows_ref, turned_ref, put)


def later_kernel(count, groups, place, w_in_ref, w_out_ref, sum_in_ref, sum_out_ref, *refs):
    blocks = refs[:count]
    outs = refs[count : count + LINE]
    gpre_ref, extra_ref, rows_ref, turned_ref = refs[count + LINE :]
    width, hidden = w_in_ref.shape
    piece_d, piece_f = width // LINE, hidden // LINE

    def put(j, part, weight_in, weight_out):
        weight = (sum_out_ref[j * piece_f : (j + 1) * piece_f, :] + weight_out).astype(BF16)
        outs[j][piece_d:, :width] = weight[: piece_f // 2]
        outs[j][piece_d:, width:] = weight[piece_f // 2 :]
        weight = (sum_in_ref[:, part] + weight_in).astype(BF16)
        for i in range(LINE):
            outs[i][:piece_d, part] = weight[i * piece_d : (i + 1) * piece_d]

    order = shard_order(place[0]) if groups == LINE else list(range(LINE))
    expert_work(order, blocks, w_in_ref, w_out_ref, gpre_ref, extra_ref, rows_ref, turned_ref, put)


def back_kernel(capacity, sets, w_in_ref, *refs):
    inputs, outs = refs[:4], refs[4:]
    width = w_in_ref.shape[0]
    for members, gpre_ref, extra_ref in zip(sets, inputs[::2], inputs[1::2]):
        grad = dot(gpre_ref[...], w_in_ref[...], ((1,), (1,))).astype(BF16)
        for i, j in enumerate(members):
            block = slice(i * capacity, (i + 1) * capacity)
            outs[j][:, :width] = grad[block]
            outs[j][:, width:] = extra_ref[block, :]


def finish_kernel(target_ref, gate_ref, tok_ref, gain_ref, go_ref, *refs):
    *blocks, tokens_out, gate_out, back_ref = refs
    rows, capacity = back_ref.shape[0], blocks[0].shape[0]
    for j, block in enumerate(blocks):
        back_ref[j * capacity : (j + 1) * capacity, :] = block[...]
    tok_rows, width = tok_ref.shape
    spots = jnp.broadcast_to(target_ref[...].astype(F32), (8, tok_rows)).T[:, :1].astype(jnp.int32)
    hit = lax.broadcasted_iota(jnp.int32, (tok_rows, rows), 1) == spots
    got = dot(jnp.where(hit, 1.0, 0.0).astype(BF16), back_ref[...])
    sums = got[:, width:].T
    gate_row = gate_ref[...].astype(F32).reshape(1, tok_rows)
    gate_out[...] = ((sums[0:1] + sums[1:2]) / gate_row).astype(BF16).reshape(tok_rows)
    scaled, spread = normalize(tok_ref[...])
    grad = got[:, :width] * gain_ref[...]
    mean = jnp.mean(grad, axis=-1, keepdims=True)
    cross = jnp.mean(grad * scaled, axis=-1, keepdims=True)
    branch = spread * (grad - mean - scaled * cross)
    tokens_out[...] = (go_ref[...].astype(F32) + branch).astype(BF16)


def block_order(sources):
    same = sorted(range(2, sources, 2), key=lambda k: (k.bit_count(), -k))
    return same + list(range(sources - 1, 1, -2)) + [1, 0]


def swap_blocks(blocks):
    count = len(blocks)
    return [
        lax.ppermute(block, "space", [(i, i ^ k) for i in range(count)]) if k else block
        for block, k in zip(blocks, block_order(count))
    ]


def is_inner(place):
    return (place[0] == 1) | (place[0] == 2)


def pass_kernel(place, third_ref, own_ref, swapped_ref, across_ref, middle_ref, out_ref, sum_ref):
    swapped = swapped_ref[...].astype(F32)
    onward = jnp.where(is_inner(place), swapped, 0.0)
    out_ref[...] = (third_ref[...].astype(F32) + onward).astype(BF16)
    total = own_ref[...].astype(F32) + (swapped - onward)
    for ref in (across_ref, middle_ref):
        total += ref[...].astype(F32)
    sum_ref[...] = total


def total_kernel(sum_ref, last_ref, in_ref, out_ref):
    piece_d, half = in_ref.shape[0], out_ref.shape[0] // 2
    width = out_ref.shape[1]
    total = sum_ref[...] + last_ref[...].astype(F32)
    in_ref[...] = total[:piece_d]
    out_ref[:half, :] = total[piece_d:, :width]
    out_ref[half:, :] = total[piece_d:, width:]


def line_sums(place, first, second, third, own, width, ahead):
    rows, hidden = own.shape
    piece_d = width // LINE
    swapped = lax.ppermute(first, "dp", [(0, 1), (1, 0), (2, 3), (3, 2)])
    across = lax.ppermute(second, "dp", [(0, 2), (3, 1)])
    middle = lax.ppermute(second, "dp", [(1, 2), (2, 1)])
    third, *ahead = lax.optimization_barrier((third, *ahead))
    passed, most = kernel_call(
        pass_kernel,
        "pass",
        1,
        1,
        [jax.ShapeDtypeStruct(own.shape, BF16), jax.ShapeDtypeStruct(own.shape, F32)],
        [smem] + [vmem] * 5,
    )(place, third, own, swapped, across, middle)
    last = lax.ppermute(passed, "dp", [(0, 1), (3, 2), (1, 3), (2, 0)])
    sums = kernel_call(
        total_kernel,
        "total",
        1,
        1,
        [
            jax.ShapeDtypeStruct((piece_d, hidden), F32),
            jax.ShapeDtypeStruct((2 * (rows - piece_d), width), F32),
        ],
        [vmem] * 2,
    )(most, last)
    return *sums, ahead


def body(tokens, gain, w_in, w_out, expert_ids, gate, grad_out):
    sources = lax.axis_size("space")
    groups = lax.axis_size("dp")
    tok_rows, width = tokens.shape
    hidden = w_in.shape[2]
    capacity = ((tok_rows * 5 // 4 + sources - 1) // sources + 7) // 8 * 8
    rows = sources * capacity
    me = lax.axis_index("space").astype(jnp.int32).reshape(1)
    place = lax.axis_index("dp").astype(jnp.int32).reshape(1)
    ids_row = expert_ids.reshape(1, tok_rows)
    gain_row = gain.reshape(1, width)
    weight_in, weight_out = w_in[0], w_out[0]
    shape = jax.ShapeDtypeStruct
    sems = pltpu.SemaphoreType.DMA
    block_place = vmem if capacity % 16 else anywhere
    io_bytes = 2 * (2 * tok_rows * width + 2 * rows * width)

    target, *sent = kernel_call(
        functools.partial(place_kernel, sources, capacity),
        "place",
        4 * rows * tok_rows * width,
        io_bytes,
        [shape((1, tok_rows), jnp.int32)]
        + [shape((capacity, 2 * width), BF16)] * sources,
        [smem] * 2 + [hbm] * 5,
        [
            pltpu.VMEM((1, pl.cdiv(tok_rows, LANES) * LANES), jnp.int32),
            pltpu.VMEM((1, tok_rows), jnp.int32),
            pltpu.VMEM((tok_rows,), BF16),
            pltpu.VMEM((tok_rows, width), BF16),
            pltpu.VMEM((1, width), F32),
            pltpu.VMEM((tok_rows, width), BF16),
            pltpu.VMEM((rows, 2 * width), BF16),
            sems((5,)),
            sems((2, sources)),
        ],
        places=[vmem] + [block_place] * sources,
        vmem_mib=56,
    )(me, place, ids_row, gate, tokens, gain_row, grad_out)
    (kept,) = kernel_call(
        keep_kernel,
        "keep",
        1,
        1,
        [shape((capacity, 2 * width), BF16)],
        [vmem],
        vmem_mib=2,
    )(sent[-1])
    arrived = swap_blocks(sent)
    arrived[-1] = kept

    late_set = list(range(3 * sources // 8, 6 * sources // 8))
    soon_set = [j for j in range(sources) if j not in late_set]

    def work(kernel, name, members, outs, *sums):
        count, span = len(members), len(members) * capacity
        return kernel_call(
            functools.partial(kernel, count, groups),
            name,
            8 * span * width * hidden,
            2 * (2 * span * width + 4 * width * hidden + span * hidden),
            outs + [shape((span, hidden), BF16), shape((span, LANES), BF16)],
            [smem] + [vmem] * (2 + len(sums) + count),
            [pltpu.VMEM((span, 2 * width), BF16), pltpu.VMEM((width, span), BF16)],
        )(place, weight_in, weight_out, *sums, *[arrived[j] for j in members])

    *sums, soon_gpre, soon_extra = work(
        sooner_kernel, "sooner", soon_set, [shape((width, hidden), F32), shape((hidden, width), F32)]
    )
    piece = shape((width // LINE + hidden // LINE // 2, hidden), BF16)
    *parts, late_gpre, late_extra = work(later_kernel, "later", late_set, [piece] * LINE, *sums)
    returned = kernel_call(
        functools.partial(back_kernel, capacity, (soon_set, late_set)),
        "back",
        1,
        1,
        [shape((capacity, width + LANES), BF16)] * sources,
        [vmem] * 5,
    )(weight_in, soon_gpre, soon_extra, late_gpre, late_extra)

    back = swap_blocks(returned)
    if groups == LINE:
        grad_w_in, grad_w_out, back[: sources // 2] = line_sums(
            place, *parts, width, back[: sources // 2]
        )
    else:
        parts_in, parts_out = zip(*[split_piece(part, width, LINE) for part in parts])
        grad_w_in, grad_w_out = (
            lax.psum_scatter(
                jnp.concatenate(part), "dp", scatter_dimension=0, tiled=True
            ).astype(F32)
            for part in (parts_in, parts_out)
        )
    grad_tokens, grad_gate = kernel_call(
        finish_kernel,
        "finish",
        1,
        1,
        [shape((tok_rows, width), BF16), shape((tok_rows,), BF16)],
        [vmem] * (5 + sources),
        [pltpu.VMEM((rows, width + LANES), BF16)],
    )(target, gate, tokens, gain_row, grad_out, *back)
    return (grad_tokens, grad_gate, grad_w_in[None], grad_w_out[None])


def split_piece(piece, width, pieces):
    piece_d = width // pieces
    lower = piece[piece_d:]
    return piece[:piece_d], jnp.concatenate([lower[:, :width], lower[:, width:]])


def solution(mesh):
    placed = (
        P(("space", "dp"), None),
        P(),
        P("space", None, None),
        P("space", None, None),
        P(("space", "dp"), None),
        P(("space", "dp")),
        P(("space", "dp"), None),
    )
    return jax.shard_map(
        body,
        mesh=mesh,
        in_specs=placed,
        out_specs=(
            P(("space", "dp"), None),
            P(("space", "dp")),
            P("space", "dp", None),
            P("space", "dp", None),
        ),
        check_vma=False,
    )
```

```python
import functools

import jax
import jax.numpy as jnp
from jax import lax
from jax.experimental import pallas as pl
from jax.experimental.pallas import tpu as pltpu
from jax.sharding import PartitionSpec as P

epsilon = 1e-05
F32 = jnp.float32
BF16 = jnp.bfloat16
LANES = 128
LINE = 4
MIB = 1024 * 1024

vmem = pl.BlockSpec(memory_space=pltpu.VMEM)
smem = pl.BlockSpec(memory_space=pltpu.SMEM)
hbm = pl.BlockSpec(memory_space=pltpu.HBM)
anywhere = pl.BlockSpec(memory_space=pl.ANY)


def dot(left, right, contract=((1,), (0,))):
    return lax.dot_general(left, right, (contract, ((), ())), preferred_element_type=F32)


def normalize(tokens):
    values = tokens.astype(F32)
    center = values - jnp.mean(values, axis=-1, keepdims=True)
    spread = lax.rsqrt(jnp.mean(center * center, axis=-1, keepdims=True) + epsilon)
    return center * spread, spread


def kernel_call(kernel, name, flops, nbytes, outs, ins, scratch=(), places=None, vmem_mib=24):
    return pl.pallas_call(
        kernel,
        name=name,
        out_shape=outs,
        in_specs=ins,
        out_specs=places or [vmem] * len(outs),
        scratch_shapes=list(scratch),
        compiler_params=pltpu.CompilerParams(vmem_limit_bytes=vmem_mib * MIB),
        cost_estimate=pl.CostEstimate(flops=flops, bytes_accessed=nbytes, transcendentals=0),
    )


def start_copies(pairs, sems):
    copies = [pltpu.make_async_copy(src, dst, sems.at[i]) for i, (src, dst) in enumerate(pairs)]
    for copy in copies:
        copy.start()
    return copies


def place_kernel(
    sources, capacity, me, place, ids_hbm, gate_hbm, tok_hbm, gain_hbm, go_hbm, target_ref, *refs
):
    outs = refs[:sources]
    wide_ref, ids_ref, gate_ref, tok_ref, gain_ref, go_ref, sent_ref, in_sems, out_sems = refs[sources:]
    rows = sources * capacity
    tok_rows, width = tok_ref.shape
    loads = start_copies(
        [(ids_hbm, ids_ref), (tok_hbm, tok_ref), (gain_hbm, gain_ref), (gate_hbm, gate_ref), (go_hbm, go_ref)],
        in_sems,
    )
    earlier = lax.broadcasted_iota(jnp.int32, (LANES, LANES), 0) < lax.broadcasted_iota(
        jnp.int32, (LANES, LANES), 1
    )
    earlier = jnp.where(earlier, 1.0, 0.0).astype(BF16)
    loads[0].wait()
    chunks = range(0, tok_rows, LANES)
    wide_ref[...] = jnp.full_like(wide_ref, -1)
    wide_ref[:, :tok_rows] = ids_ref[...]
    ids = [wide_ref[:, c : c + LANES] for c in chunks]
    expert = lax.broadcasted_iota(jnp.int32, (sources, LANES), 0)
    onehots = [jnp.where(expert == chunk, 1.0, 0.0) for chunk in ids]
    within = dot(jnp.concatenate(onehots).astype(BF16), earlier)
    base = jnp.zeros((sources, 1), F32)
    for i, (c, chunk, onehot) in enumerate(zip(chunks, ids, onehots)):
        before = within[i * sources : (i + 1) * sources] + base
        base += jnp.sum(onehot, axis=1, keepdims=True)
        rank = jnp.sum(before * onehot, axis=0, keepdims=True).astype(jnp.int32)
        away = jnp.bitwise_xor(chunk, me[0])
        block = jnp.zeros_like(away)
        for j, k in enumerate(block_order(sources)):
            block = jnp.where(away == k, j, block)
        end = min(LANES, tok_rows - c)
        target = jnp.where(rank < capacity, block * capacity + rank, -1)
        target_ref[:, c : c + end] = target[:, :end]
    target = target_ref[...]
    for copy in loads[1:]:
        copy.wait()
    hit = lax.broadcasted_iota(jnp.int32, (rows, tok_rows), 0) == target
    gate = gate_ref[...].astype(F32).reshape(1, tok_rows)
    scaled, _ = normalize(tok_ref[...])
    normed = (scaled * gain_ref[...]).astype(BF16)
    stores = []
    for part, (weight, values) in enumerate(((gate, go_ref[...]), (1.0, normed))):
        columns = pl.ds((1 - part) * width, width)
        sent_ref[:, columns] = dot(jnp.where(hit, weight, 0.0).astype(BF16), values).astype(BF16)
        spans = [pl.ds(j * capacity, capacity) for j in range(sources)]
        if capacity % 16:
            for j in range(sources):
                outs[j][:, columns] = sent_ref[spans[j], columns]
        else:
            stores += start_copies(
                [(sent_ref.at[spans[j], columns], outs[j].at[:, columns]) for j in range(sources)],
                out_sems.at[part],
            )
    for copy in stores:
        copy.wait()


def keep_kernel(block_ref, out_ref):
    out_ref[...] = block_ref[...]


def gelu_parts(value):
    root = 0.7978845608028654
    cubic = root * 0.044715
    square = value * value
    tan = jnp.tanh(value * (root + cubic * square))
    half = 0.5 + 0.5 * tan
    act = value * half
    return act, half + act * (1.0 - tan) * (root + 3.0 * cubic * square)


def shard_order(place):
    second = jnp.where(place < 2, 2 - 2 * place, 7 - 2 * place)
    return [3 - place, second, 3 - second, place]


def expert_work(order, blocks, w_in_ref, w_out_ref, gpre_ref, extra_ref, rows_ref, turned_ref, put):
    capacity = blocks[0].shape[0]
    width, hidden = w_in_ref.shape
    piece_d, piece_f = width // LINE, hidden // LINE
    for j, block in enumerate(blocks):
        rows_ref[j * capacity : (j + 1) * capacity, :] = block[...]
    for j in range(LINE):
        start = pl.multiple_of(order[j] * piece_d, piece_d)
        turned_ref[j * piece_d : (j + 1) * piece_d, :] = rows_ref[:, pl.ds(start, piece_d)].T
    total = jnp.zeros(extra_ref.shape, F32)
    for j in range(LINE):
        part = pl.ds(pl.multiple_of(order[j] * piece_f, piece_f), piece_f)
        delta = rows_ref[:, width:]
        act, slope = gelu_parts(dot(rows_ref[:, :width], w_in_ref[:, part]))
        grad_act = dot(delta, w_out_ref[part, :], ((1,), (1,)))
        products = act * grad_act
        for lane in range(0, piece_f, LANES):
            total += products[:, lane : lane + LANES]
        grad_pre = (grad_act * slope).astype(BF16)
        gpre_ref[:, part] = grad_pre
        put(j, part, dot(turned_ref[...], grad_pre), dot(act.astype(BF16).T, delta))
    total = jnp.sum(total, axis=1, keepdims=True)
    high = total.astype(BF16).astype(F32)
    lane = lax.broadcasted_iota(jnp.int32, extra_ref.shape, 1)
    extra_ref[...] = jnp.where(lane == 0, high, jnp.where(lane == 1, total - high, 0.0)).astype(BF16)


def sooner_kernel(count, groups, place, w_in_ref, w_out_ref, *refs):
    blocks = refs[:count]
    sum_in_ref, sum_out_ref, gpre_ref, extra_ref, rows_ref, turned_ref = refs[count:]
    piece_f = w_in_ref.shape[1] // LINE

    def put(j, part, weight_in, weight_out):
        sum_in_ref[:, part] = weight_in
        sum_out_ref[j * piece_f : (j + 1) * piece_f, :] = weight_out

    order = shard_order(place[0]) if groups == LINE else list(range(LINE))
    expert_work(order, blocks, w_in_ref, w_out_ref, gpre_ref, extra_ref, rows_ref, turned_ref, put)


def later_kernel(count, groups, place, w_in_ref, w_out_ref, sum_in_ref, sum_out_ref, *refs):
    blocks = refs[:count]
    outs = refs[count : count + LINE]
    gpre_ref, extra_ref, rows_ref, turned_ref = refs[count + LINE :]
    width, hidden = w_in_ref.shape
    piece_d, piece_f = width // LINE, hidden // LINE

    def put(j, part, weight_in, weight_out):
        weight = (sum_out_ref[j * piece_f : (j + 1) * piece_f, :] + weight_out).astype(BF16)
        outs[j][piece_d:, :width] = weight[: piece_f // 2]
        outs[j][piece_d:, width:] = weight[piece_f // 2 :]
        weight = (sum_in_ref[:, part] + weight_in).astype(BF16)
        for i in range(LINE):
            outs[i][:piece_d, part] = weight[i * piece_d : (i + 1) * piece_d]

    order = shard_order(place[0]) if groups == LINE else list(range(LINE))
    expert_work(order, blocks, w_in_ref, w_out_ref, gpre_ref, extra_ref, rows_ref, turned_ref, put)


def back_kernel(capacity, sets, w_in_ref, *refs):
    inputs, outs = refs[:4], refs[4:]
    width = w_in_ref.shape[0]
    for members, gpre_ref, extra_ref in zip(sets, inputs[::2], inputs[1::2]):
        grad = dot(gpre_ref[...], w_in_ref[...], ((1,), (1,))).astype(BF16)
        for i, j in enumerate(members):
            block = slice(i * capacity, (i + 1) * capacity)
            outs[j][:, :width] = grad[block]
            outs[j][:, width:] = extra_ref[block, :]


def finish_kernel(target_ref, gate_ref, tok_ref, gain_ref, go_ref, *refs):
    *blocks, tokens_out, gate_out, back_ref = refs
    rows, capacity = back_ref.shape[0], blocks[0].shape[0]
    for j, block in enumerate(blocks):
        back_ref[j * capacity : (j + 1) * capacity, :] = block[...]
    tok_rows, width = tok_ref.shape
    spots = jnp.broadcast_to(target_ref[...].astype(F32), (8, tok_rows)).T[:, :1].astype(jnp.int32)
    hit = lax.broadcasted_iota(jnp.int32, (tok_rows, rows), 1) == spots
    got = dot(jnp.where(hit, 1.0, 0.0).astype(BF16), back_ref[...])
    sums = got[:, width:].T
    gate_row = gate_ref[...].astype(F32).reshape(1, tok_rows)
    gate_out[...] = ((sums[0:1] + sums[1:2]) / gate_row).astype(BF16).reshape(tok_rows)
    scaled, spread = normalize(tok_ref[...])
    grad = got[:, :width] * gain_ref[...]
    mean = jnp.mean(grad, axis=-1, keepdims=True)
    cross = jnp.mean(grad * scaled, axis=-1, keepdims=True)
    branch = spread * (grad - mean - scaled * cross)
    tokens_out[...] = (go_ref[...].astype(F32) + branch).astype(BF16)


def block_order(sources):
    same = sorted(range(2, sources, 2), key=lambda k: (k.bit_count(), -k))
    return same + list(range(sources - 1, 1, -2)) + [1, 0]


def swap_blocks(blocks, order):
    devices = range(lax.axis_size("space"))
    return [
        lax.ppermute(block, "space", [(i, i ^ k) for i in devices]) if k else block
        for block, k in zip(blocks, order)
    ]


def pass_kernel(place, up_ref, down_ref, third_ref, own_ref, out_ref, sum_ref):
    up, down = up_ref[...].astype(F32), down_ref[...].astype(F32)
    low = place[0] == 1
    out_ref[...] = (third_ref[...].astype(F32) + jnp.where(low, up, down)).astype(BF16)
    sum_ref[...] = own_ref[...].astype(F32) + jnp.where(low, down, up)


def total_kernel(sum_ref, cycle_ref, last_ref, in_ref, out_ref):
    piece_d, half = in_ref.shape[0], out_ref.shape[0] // 2
    width = out_ref.shape[1]
    total = sum_ref[...] + cycle_ref[...].astype(F32) + last_ref[...].astype(F32)
    in_ref[...] = total[:piece_d]
    out_ref[:half, :] = total[piece_d:, :width]
    out_ref[half:, :] = total[piece_d:, width:]


def line_sums(place, first, second, third, own, width, returned):
    rows, hidden = own.shape
    piece_d = width // LINE
    half = len(returned) // 2
    order = block_order(len(returned))
    up = lax.ppermute(first, "dp", [(0, 1), (1, 2)])
    down = lax.ppermute(first, "dp", [(3, 2), (2, 1)])
    cycle = lax.ppermute(second, "dp", [(0, 2), (1, 0), (2, 3), (3, 1)])
    back = swap_blocks(returned[:half], order[:half])
    third, *back = lax.optimization_barrier((third, *back))
    passed, most = kernel_call(
        pass_kernel,
        "pass",
        1,
        1,
        [jax.ShapeDtypeStruct(own.shape, BF16), jax.ShapeDtypeStruct(own.shape, F32)],
        [smem] + [vmem] * 4,
    )(place, up, down, third, own)
    last = lax.ppermute(passed, "dp", [(0, 1), (3, 2), (1, 3), (2, 0)])
    cycle, *rest = lax.optimization_barrier((cycle, *returned[half:]))
    back += swap_blocks(rest, order[half:])
    sums = kernel_call(
        total_kernel,
        "total",
        1,
        1,
        [
            jax.ShapeDtypeStruct((piece_d, hidden), F32),
            jax.ShapeDtypeStruct((2 * (rows - piece_d), width), F32),
        ],
        [vmem] * 3,
    )(most, cycle, last)
    return *sums, back


def body(tokens, gain, w_in, w_out, expert_ids, gate, grad_out):
    sources = lax.axis_size("space")
    groups = lax.axis_size("dp")
    tok_rows, width = tokens.shape
    hidden = w_in.shape[2]
    capacity = ((tok_rows * 5 // 4 + sources - 1) // sources + 7) // 8 * 8
    rows = sources * capacity
    me = lax.axis_index("space").astype(jnp.int32).reshape(1)
    place = lax.axis_index("dp").astype(jnp.int32).reshape(1)
    ids_row = expert_ids.reshape(1, tok_rows)
    gain_row = gain.reshape(1, width)
    weight_in, weight_out = w_in[0], w_out[0]
    shape = jax.ShapeDtypeStruct
    sems = pltpu.SemaphoreType.DMA
    block_place = vmem if capacity % 16 else anywhere
    io_bytes = 2 * (2 * tok_rows * width + 2 * rows * width)

    target, *sent = kernel_call(
        functools.partial(place_kernel, sources, capacity),
        "place",
        4 * rows * tok_rows * width,
        io_bytes,
        [shape((1, tok_rows), jnp.int32)]
        + [shape((capacity, 2 * width), BF16)] * sources,
        [smem] * 2 + [hbm] * 5,
        [
            pltpu.VMEM((1, pl.cdiv(tok_rows, LANES) * LANES), jnp.int32),
            pltpu.VMEM((1, tok_rows), jnp.int32),
            pltpu.VMEM((tok_rows,), BF16),
            pltpu.VMEM((tok_rows, width), BF16),
            pltpu.VMEM((1, width), F32),
            pltpu.VMEM((tok_rows, width), BF16),
            pltpu.VMEM((rows, 2 * width), BF16),
            sems((5,)),
            sems((2, sources)),
        ],
        places=[vmem] + [block_place] * sources,
        vmem_mib=56,
    )(me, place, ids_row, gate, tokens, gain_row, grad_out)
    (kept,) = kernel_call(
        keep_kernel,
        "keep",
        1,
        1,
        [shape((capacity, 2 * width), BF16)],
        [vmem],
        vmem_mib=2,
    )(sent[-1])
    arrived = swap_blocks(sent, block_order(sources))
    arrived[-1] = kept

    late_set = list(range(3 * sources // 8, 6 * sources // 8))
    soon_set = [j for j in range(sources) if j not in late_set]

    def work(kernel, name, members, outs, *sums):
        count, span = len(members), len(members) * capacity
        return kernel_call(
            functools.partial(kernel, count, groups),
            name,
            8 * span * width * hidden,
            2 * (2 * span * width + 4 * width * hidden + span * hidden),
            outs + [shape((span, hidden), BF16), shape((span, LANES), BF16)],
            [smem] + [vmem] * (2 + len(sums) + count),
            [pltpu.VMEM((span, 2 * width), BF16), pltpu.VMEM((width, span), BF16)],
        )(place, weight_in, weight_out, *sums, *[arrived[j] for j in members])

    *sums, soon_gpre, soon_extra = work(
        sooner_kernel, "sooner", soon_set, [shape((width, hidden), F32), shape((hidden, width), F32)]
    )
    piece = shape((width // LINE + hidden // LINE // 2, hidden), BF16)
    *parts, late_gpre, late_extra = work(later_kernel, "later", late_set, [piece] * LINE, *sums)
    returned = kernel_call(
        functools.partial(back_kernel, capacity, (soon_set, late_set)),
        "back",
        1,
        1,
        [shape((capacity, width + LANES), BF16)] * sources,
        [vmem] * 5,
    )(weight_in, soon_gpre, soon_extra, late_gpre, late_extra)

    if groups == LINE:
        grad_w_in, grad_w_out, back = line_sums(place, *parts, width, returned)
    else:
        back = swap_blocks(returned, block_order(sources))
        parts_in, parts_out = zip(*[split_piece(part, width, LINE) for part in parts])
        grad_w_in, grad_w_out = (
            lax.psum_scatter(
                jnp.concatenate(part), "dp", scatter_dimension=0, tiled=True
            ).astype(F32)
            for part in (parts_in, parts_out)
        )
    grad_tokens, grad_gate = kernel_call(
        finish_kernel,
        "finish",
        1,
        1,
        [shape((tok_rows, width), BF16), shape((tok_rows,), BF16)],
        [vmem] * (5 + sources),
        [pltpu.VMEM((rows, width + LANES), BF16)],
    )(target, gate, tokens, gain_row, grad_out, *back)
    return (grad_tokens, grad_gate, grad_w_in[None], grad_w_out[None])


def split_piece(piece, width, pieces):
    piece_d = width // pieces
    lower = piece[piece_d:]
    return piece[:piece_d], jnp.concatenate([lower[:, :width], lower[:, width:]])


def solution(mesh):
    placed = (
        P(("space", "dp"), None),
        P(),
        P("space", None, None),
        P("space", None, None),
        P(("space", "dp"), None),
        P(("space", "dp")),
        P(("space", "dp"), None),
    )
    return jax.shard_map(
        body,
        mesh=mesh,
        in_specs=placed,
        out_specs=(
            P(("space", "dp"), None),
            P(("space", "dp")),
            P("space", "dp", None),
            P("space", "dp", None),
        ),
        check_vma=False,
    )
```

```python
import functools

import jax
import jax.numpy as jnp
from jax import lax
from jax.experimental import pallas as pl
from jax.experimental.pallas import tpu as pltpu
from jax.sharding import PartitionSpec as P

epsilon = 1e-05
F32 = jnp.float32
BF16 = jnp.bfloat16
LANES = 128
LINE = 4
MIB = 1024 * 1024

vmem = pl.BlockSpec(memory_space=pltpu.VMEM)
smem = pl.BlockSpec(memory_space=pltpu.SMEM)
hbm = pl.BlockSpec(memory_space=pltpu.HBM)
anywhere = pl.BlockSpec(memory_space=pl.ANY)


def dot(left, right, contract=((1,), (0,))):
    return lax.dot_general(left, right, (contract, ((), ())), preferred_element_type=F32)


def normalize(tokens):
    values = tokens.astype(F32)
    center = values - jnp.mean(values, axis=-1, keepdims=True)
    spread = lax.rsqrt(jnp.mean(center * center, axis=-1, keepdims=True) + epsilon)
    return center * spread, spread


def kernel_call(kernel, name, flops, nbytes, outs, ins, scratch=(), places=None, vmem_mib=24):
    return pl.pallas_call(
        kernel,
        name=name,
        out_shape=outs,
        in_specs=ins,
        out_specs=places or [vmem] * len(outs),
        scratch_shapes=list(scratch),
        compiler_params=pltpu.CompilerParams(vmem_limit_bytes=vmem_mib * MIB),
        cost_estimate=pl.CostEstimate(flops=flops, bytes_accessed=nbytes, transcendentals=0),
    )


def start_copies(pairs, sems):
    copies = [pltpu.make_async_copy(src, dst, sems.at[i]) for i, (src, dst) in enumerate(pairs)]
    for copy in copies:
        copy.start()
    return copies


def put_blocks(first, target, gate, tok_ref, gain_ref, go_ref, sent_ref, outs, sems):
    capacity, width = outs[0].shape[0], tok_ref.shape[1]
    count = len(outs)
    hit = lax.broadcasted_iota(jnp.int32, (count * capacity, target.shape[1]), 0) == (
        target - first * capacity
    )
    gate = gate.astype(F32).reshape(target.shape)
    scaled, _ = normalize(tok_ref[...])
    normed = (scaled * gain_ref[...]).astype(BF16)
    spans = [pl.ds(j * capacity, capacity) for j in range(count)]
    stores = []
    for part, (weight, values) in enumerate(((gate, go_ref[...]), (1.0, normed))):
        columns = pl.ds((1 - part) * width, width)
        sent_ref[:, columns] = dot(jnp.where(hit, weight, 0.0).astype(BF16), values).astype(BF16)
        if capacity % 16:
            for j in range(count):
                outs[j][:, columns] = sent_ref[spans[j], columns]
        else:
            stores += start_copies(
                [(sent_ref.at[spans[j], columns], outs[j].at[:, columns]) for j in range(count)],
                sems.at[part],
            )
    for copy in stores:
        copy.wait()


def place_kernel(
    sources, capacity, me, place, ids_hbm, gate_hbm, tok_hbm, gain_hbm, go_hbm, target_ref, *refs
):
    *outs, wide_ref, ids_ref, gate_ref, tok_ref, gain_ref, go_ref, sent_ref, in_sems, out_sems = refs
    tok_rows = tok_ref.shape[0]
    loads = start_copies(
        [(ids_hbm, ids_ref), (tok_hbm, tok_ref), (gain_hbm, gain_ref), (gate_hbm, gate_ref), (go_hbm, go_ref)],
        in_sems,
    )
    earlier = lax.broadcasted_iota(jnp.int32, (LANES, LANES), 0) < lax.broadcasted_iota(
        jnp.int32, (LANES, LANES), 1
    )
    earlier = jnp.where(earlier, 1.0, 0.0).astype(BF16)
    loads[0].wait()
    chunks = range(0, tok_rows, LANES)
    wide_ref[...] = jnp.full_like(wide_ref, -1)
    wide_ref[:, :tok_rows] = ids_ref[...]
    ids = [wide_ref[:, c : c + LANES] for c in chunks]
    expert = lax.broadcasted_iota(jnp.int32, (sources, LANES), 0)
    onehots = [jnp.where(expert == chunk, 1.0, 0.0) for chunk in ids]
    within = dot(jnp.concatenate(onehots).astype(BF16), earlier)
    base = jnp.zeros((sources, 1), F32)
    for i, (c, chunk, onehot) in enumerate(zip(chunks, ids, onehots)):
        before = within[i * sources : (i + 1) * sources] + base
        base += jnp.sum(onehot, axis=1, keepdims=True)
        rank = jnp.sum(before * onehot, axis=0, keepdims=True).astype(jnp.int32)
        away = jnp.bitwise_xor(chunk, me[0])
        block = jnp.zeros_like(away)
        for j, k in enumerate(block_order(sources)):
            block = jnp.where(away == k, j, block)
        end = min(LANES, tok_rows - c)
        target = jnp.where(rank < capacity, block * capacity + rank, -1)
        target_ref[:, c : c + end] = target[:, :end]
    for copy in loads[1:]:
        copy.wait()
    put_blocks(0, target_ref[...], gate_ref[...], tok_ref, gain_ref, go_ref, sent_ref, outs, out_sems)


def rest_kernel(first, target_ref, gate_ref, tok_ref, gain_ref, go_ref, *refs):
    *outs, sent_ref, sems = refs
    put_blocks(first, target_ref[...], gate_ref[...], tok_ref, gain_ref, go_ref, sent_ref, outs, sems)


def keep_kernel(block_ref, out_ref):
    out_ref[...] = block_ref[...]


def gelu_parts(value):
    root = 0.7978845608028654
    cubic = root * 0.044715
    square = value * value
    tan = jnp.tanh(value * (root + cubic * square))
    half = 0.5 + 0.5 * tan
    act = value * half
    return act, half + act * (1.0 - tan) * (root + 3.0 * cubic * square)


def shard_order(place):
    first = jnp.where(lax.rem(place, 2) == 0, 3, 0)
    second = jnp.where(place < 2, 2, 1)
    return [first, second, 6 - first - second - place, place]


def expert_work(order, blocks, w_in_ref, w_out_ref, gpre_ref, extra_ref, rows_ref, turned_ref, put):
    capacity = blocks[0].shape[0]
    width, hidden = w_in_ref.shape
    piece_d, piece_f = width // LINE, hidden // LINE
    for j, block in enumerate(blocks):
        rows_ref[j * capacity : (j + 1) * capacity, :] = block[...]
    for j in range(LINE):
        start = pl.multiple_of(order[j] * piece_d, piece_d)
        turned_ref[j * piece_d : (j + 1) * piece_d, :] = rows_ref[:, pl.ds(start, piece_d)].T
    total = jnp.zeros(extra_ref.shape, F32)
    for j in range(LINE):
        part = pl.ds(pl.multiple_of(order[j] * piece_f, piece_f), piece_f)
        delta = rows_ref[:, width:]
        act, slope = gelu_parts(dot(rows_ref[:, :width], w_in_ref[:, part]))
        grad_act = dot(delta, w_out_ref[part, :], ((1,), (1,)))
        products = act * grad_act
        for lane in range(0, piece_f, LANES):
            total += products[:, lane : lane + LANES]
        grad_pre = (grad_act * slope).astype(BF16)
        gpre_ref[:, part] = grad_pre
        put(j, part, dot(turned_ref[...], grad_pre), dot(act.astype(BF16).T, delta))
    total = jnp.sum(total, axis=1, keepdims=True)
    high = total.astype(BF16).astype(F32)
    lane = lax.broadcasted_iota(jnp.int32, extra_ref.shape, 1)
    extra_ref[...] = jnp.where(lane == 0, high, jnp.where(lane == 1, total - high, 0.0)).astype(BF16)


def sooner_kernel(count, groups, place, w_in_ref, w_out_ref, *refs):
    blocks = refs[:count]
    sum_in_ref, sum_out_ref, gpre_ref, extra_ref, rows_ref, turned_ref = refs[count:]
    piece_f = w_in_ref.shape[1] // LINE

    def put(j, part, weight_in, weight_out):
        sum_in_ref[:, part] = weight_in
        sum_out_ref[j * piece_f : (j + 1) * piece_f, :] = weight_out

    order = shard_order(place[0]) if groups == LINE else list(range(LINE))
    expert_work(order, blocks, w_in_ref, w_out_ref, gpre_ref, extra_ref, rows_ref, turned_ref, put)


def later_kernel(count, groups, place, w_in_ref, w_out_ref, sum_in_ref, sum_out_ref, *refs):
    blocks = refs[:count]
    outs = refs[count : count + LINE]
    gpre_ref, extra_ref, rows_ref, turned_ref = refs[count + LINE :]
    width, hidden = w_in_ref.shape
    piece_d, piece_f = width // LINE, hidden // LINE

    def put(j, part, weight_in, weight_out):
        weight = (sum_out_ref[j * piece_f : (j + 1) * piece_f, :] + weight_out).astype(BF16)
        outs[j][piece_d:, :width] = weight[: piece_f // 2]
        outs[j][piece_d:, width:] = weight[piece_f // 2 :]
        weight = (sum_in_ref[:, part] + weight_in).astype(BF16)
        for i in range(LINE):
            outs[i][:piece_d, part] = weight[i * piece_d : (i + 1) * piece_d]

    order = shard_order(place[0]) if groups == LINE else list(range(LINE))
    expert_work(order, blocks, w_in_ref, w_out_ref, gpre_ref, extra_ref, rows_ref, turned_ref, put)


def back_kernel(capacity, sets, w_in_ref, *refs):
    inputs, outs = refs[:4], refs[4:]
    width = w_in_ref.shape[0]
    for members, gpre_ref, extra_ref in zip(sets, inputs[::2], inputs[1::2]):
        grad = dot(gpre_ref[...], w_in_ref[...], ((1,), (1,))).astype(BF16)
        for i, j in enumerate(members):
            block = slice(i * capacity, (i + 1) * capacity)
            outs[j][:, :width] = grad[block]
            outs[j][:, width:] = extra_ref[block, :]


def finish_kernel(target_ref, gate_ref, tok_ref, gain_ref, go_ref, *refs):
    *blocks, tokens_out, gate_out, back_ref = refs
    rows, capacity = back_ref.shape[0], blocks[0].shape[0]
    for j, block in enumerate(blocks):
        back_ref[j * capacity : (j + 1) * capacity, :] = block[...]
    tok_rows, width = tok_ref.shape
    spots = jnp.broadcast_to(target_ref[...].astype(F32), (8, tok_rows)).T[:, :1].astype(jnp.int32)
    hit = lax.broadcasted_iota(jnp.int32, (tok_rows, rows), 1) == spots
    got = dot(jnp.where(hit, 1.0, 0.0).astype(BF16), back_ref[...])
    sums = got[:, width:].T
    gate_row = gate_ref[...].astype(F32).reshape(1, tok_rows)
    gate_out[...] = ((sums[0:1] + sums[1:2]) / gate_row).astype(BF16).reshape(tok_rows)
    scaled, spread = normalize(tok_ref[...])
    grad = got[:, :width] * gain_ref[...]
    mean = jnp.mean(grad, axis=-1, keepdims=True)
    cross = jnp.mean(grad * scaled, axis=-1, keepdims=True)
    branch = spread * (grad - mean - scaled * cross)
    tokens_out[...] = (go_ref[...].astype(F32) + branch).astype(BF16)


def block_order(sources):
    same = sorted(range(2, sources, 2), key=lambda k: (k.bit_count(), -k))
    return same + list(range(sources - 1, 1, -2)) + [1, 0]


def swap_blocks(blocks, order):
    devices = range(lax.axis_size("space"))
    return [
        lax.ppermute(block, "space", [(i, i ^ k) for i in devices]) if k else block
        for block, k in zip(blocks, order)
    ]


def start_kernel(own_ref, middle_ref, out_ref):
    out_ref[...] = own_ref[...].astype(F32) + middle_ref[...].astype(F32)


def pass_kernel(place, swapped_ref, third_ref, sum_ref, out_ref, more_ref):
    swapped = swapped_ref[...].astype(F32)
    onward = jnp.where((place[0] == 1) | (place[0] == 2), swapped, 0.0)
    out_ref[...] = (third_ref[...].astype(F32) + onward).astype(BF16)
    more_ref[...] = sum_ref[...] + (swapped - onward)


def total_kernel(sum_ref, across_ref, last_ref, in_ref, out_ref):
    piece_d, half = in_ref.shape[0], out_ref.shape[0] // 2
    width = out_ref.shape[1]
    total = sum_ref[...] + across_ref[...].astype(F32) + last_ref[...].astype(F32)
    in_ref[...] = total[:piece_d]
    out_ref[:half, :] = total[piece_d:, :width]
    out_ref[half:, :] = total[piece_d:, width:]


def line_sums(place, first, second, third, own, width, returned):
    rows, hidden = own.shape
    piece_d = width // LINE
    half = len(returned) // 2
    order = block_order(len(returned))
    middle = lax.ppermute(second, "dp", [(1, 2), (2, 1)])
    swapped = lax.ppermute(first, "dp", [(0, 1), (1, 0), (2, 3), (3, 2)])
    across = lax.ppermute(second, "dp", [(0, 2), (3, 1)])
    back = swap_blocks(returned[:half], order[:half])
    third, *back = lax.optimization_barrier((third, *back))
    (some,) = kernel_call(
        start_kernel, "start", 1, 1, [jax.ShapeDtypeStruct(own.shape, F32)], [vmem] * 2
    )(own, middle)
    passed, most = kernel_call(
        pass_kernel,
        "pass",
        1,
        1,
        [jax.ShapeDtypeStruct(own.shape, BF16), jax.ShapeDtypeStruct(own.shape, F32)],
        [smem] + [vmem] * 3,
    )(place, swapped, third, some)
    last = lax.ppermute(passed, "dp", [(0, 1), (3, 2), (1, 3), (2, 0)])
    across, *rest = lax.optimization_barrier((across, *returned[half:]))
    back += swap_blocks(rest, order[half:])
    sums = kernel_call(
        total_kernel,
        "total",
        1,
        1,
        [
            jax.ShapeDtypeStruct((piece_d, hidden), F32),
            jax.ShapeDtypeStruct((2 * (rows - piece_d), width), F32),
        ],
        [vmem] * 3,
    )(most, across, last)
    return *sums, back


def body(tokens, gain, w_in, w_out, expert_ids, gate, grad_out):
    sources = lax.axis_size("space")
    groups = lax.axis_size("dp")
    tok_rows, width = tokens.shape
    hidden = w_in.shape[2]
    capacity = ((tok_rows * 5 // 4 + sources - 1) // sources + 7) // 8 * 8
    rows = sources * capacity
    me = lax.axis_index("space").astype(jnp.int32).reshape(1)
    place = lax.axis_index("dp").astype(jnp.int32).reshape(1)
    ids_row = expert_ids.reshape(1, tok_rows)
    gain_row = gain.reshape(1, width)
    weight_in, weight_out = w_in[0], w_out[0]
    shape = jax.ShapeDtypeStruct
    sems = pltpu.SemaphoreType.DMA
    block_place = vmem if capacity % 16 else anywhere
    io_bytes = 2 * (2 * tok_rows * width + 2 * rows * width)

    soon = sources // 2
    blocks = [shape((capacity, 2 * width), BF16)] * soon
    target, *sent = kernel_call(
        functools.partial(place_kernel, sources, capacity),
        "place",
        2 * rows * tok_rows * width,
        io_bytes,
        [shape((1, tok_rows), jnp.int32)] + blocks,
        [smem] * 2 + [hbm] * 5,
        [
            pltpu.VMEM((1, pl.cdiv(tok_rows, LANES) * LANES), jnp.int32),
            pltpu.VMEM((1, tok_rows), jnp.int32),
            pltpu.VMEM((tok_rows,), BF16),
            pltpu.VMEM((tok_rows, width), BF16),
            pltpu.VMEM((1, width), F32),
            pltpu.VMEM((tok_rows, width), BF16),
            pltpu.VMEM((soon * capacity, 2 * width), BF16),
            sems((5,)),
            sems((2, soon)),
        ],
        places=[vmem] + [block_place] * soon,
        vmem_mib=56,
    )(me, place, ids_row, gate, tokens, gain_row, grad_out)
    sent += kernel_call(
        functools.partial(rest_kernel, soon),
        "rest",
        1,
        1,
        blocks,
        [vmem] * 5,
        [pltpu.VMEM((soon * capacity, 2 * width), BF16), sems((2, soon))],
        places=[block_place] * soon,
        vmem_mib=16,
    )(target, gate, tokens, gain_row, grad_out)
    (kept,) = kernel_call(
        keep_kernel,
        "keep",
        1,
        1,
        [shape((capacity, 2 * width), BF16)],
        [vmem],
        vmem_mib=2,
    )(sent[-1])
    arrived = swap_blocks(sent, block_order(sources))
    arrived[-1] = kept

    late_set = list(range(sources // 2, 3 * sources // 4))
    soon_set = [j for j in range(sources) if j not in late_set]

    def work(kernel, name, members, outs, *sums):
        count, span = len(members), len(members) * capacity
        return kernel_call(
            functools.partial(kernel, count, groups),
            name,
            8 * span * width * hidden,
            2 * (2 * span * width + 4 * width * hidden + span * hidden),
            outs + [shape((span, hidden), BF16), shape((span, LANES), BF16)],
            [smem] + [vmem] * (2 + len(sums) + count),
            [pltpu.VMEM((span, 2 * width), BF16), pltpu.VMEM((width, span), BF16)],
        )(place, weight_in, weight_out, *sums, *[arrived[j] for j in members])

    *sums, soon_gpre, soon_extra = work(
        sooner_kernel, "sooner", soon_set, [shape((width, hidden), F32), shape((hidden, width), F32)]
    )
    piece = shape((width // LINE + hidden // LINE // 2, hidden), BF16)
    *parts, late_gpre, late_extra = work(later_kernel, "later", late_set, [piece] * LINE, *sums)
    returned = kernel_call(
        functools.partial(back_kernel, capacity, (soon_set, late_set)),
        "back",
        1,
        1,
        [shape((capacity, width + LANES), BF16)] * sources,
        [vmem] * 5,
    )(weight_in, soon_gpre, soon_extra, late_gpre, late_extra)

    if groups == LINE:
        grad_w_in, grad_w_out, back = line_sums(place, *parts, width, returned)
    else:
        back = swap_blocks(returned, block_order(sources))
        parts_in, parts_out = zip(*[split_piece(part, width, LINE) for part in parts])
        grad_w_in, grad_w_out = (
            lax.psum_scatter(
                jnp.concatenate(part), "dp", scatter_dimension=0, tiled=True
            ).astype(F32)
            for part in (parts_in, parts_out)
        )
    grad_tokens, grad_gate = kernel_call(
        finish_kernel,
        "finish",
        1,
        1,
        [shape((tok_rows, width), BF16), shape((tok_rows,), BF16)],
        [vmem] * (5 + sources),
        [pltpu.VMEM((rows, width + LANES), BF16)],
    )(target, gate, tokens, gain_row, grad_out, *back)
    return (grad_tokens, grad_gate, grad_w_in[None], grad_w_out[None])


def split_piece(piece, width, pieces):
    piece_d = width // pieces
    lower = piece[piece_d:]
    return piece[:piece_d], jnp.concatenate([lower[:, :width], lower[:, width:]])


def solution(mesh):
    placed = (
        P(("space", "dp"), None),
        P(),
        P("space", None, None),
        P("space", None, None),
        P(("space", "dp"), None),
        P(("space", "dp")),
        P(("space", "dp"), None),
    )
    return jax.shard_map(
        body,
        mesh=mesh,
        in_specs=placed,
        out_specs=(
            P(("space", "dp"), None),
            P(("space", "dp")),
            P("space", "dp", None),
            P("space", "dp", None),
        ),
        check_vma=False,
    )
```

```python
import functools

import jax
import jax.numpy as jnp
from jax import lax
from jax.experimental import pallas as pl
from jax.experimental.pallas import tpu as pltpu
from jax.sharding import PartitionSpec as P

epsilon = 1e-05
F32 = jnp.float32
BF16 = jnp.bfloat16
LANES = 128
LINE = 4
MIB = 1024 * 1024

vmem = pl.BlockSpec(memory_space=pltpu.VMEM)
smem = pl.BlockSpec(memory_space=pltpu.SMEM)
hbm = pl.BlockSpec(memory_space=pltpu.HBM)
anywhere = pl.BlockSpec(memory_space=pl.ANY)


def dot(left, right, contract=((1,), (0,))):
    return lax.dot_general(left, right, (contract, ((), ())), preferred_element_type=F32)


def normalize(tokens):
    values = tokens.astype(F32)
    center = values - jnp.mean(values, axis=-1, keepdims=True)
    spread = lax.rsqrt(jnp.mean(center * center, axis=-1, keepdims=True) + epsilon)
    return center * spread, spread


def kernel_call(kernel, name, flops, nbytes, outs, ins, scratch=(), places=None, vmem_mib=24):
    return pl.pallas_call(
        kernel,
        name=name,
        out_shape=outs,
        in_specs=ins,
        out_specs=places or [vmem] * len(outs),
        scratch_shapes=list(scratch),
        compiler_params=pltpu.CompilerParams(vmem_limit_bytes=vmem_mib * MIB),
        cost_estimate=pl.CostEstimate(flops=flops, bytes_accessed=nbytes, transcendentals=0),
    )


def start_copies(pairs, sems):
    copies = [pltpu.make_async_copy(src, dst, sems.at[i]) for i, (src, dst) in enumerate(pairs)]
    for copy in copies:
        copy.start()
    return copies


def put_blocks(first, target, gate, tok_ref, gain_ref, go_ref, sent_ref, outs, sems):
    capacity, width = outs[0].shape[0], tok_ref.shape[1]
    count = len(outs)
    hit = lax.broadcasted_iota(jnp.int32, (count * capacity, target.shape[1]), 0) == (
        target - first * capacity
    )
    gate = gate.astype(F32).reshape(target.shape)
    scaled, _ = normalize(tok_ref[...])
    normed = (scaled * gain_ref[...]).astype(BF16)
    spans = [pl.ds(j * capacity, capacity) for j in range(count)]
    stores = []
    for part, (weight, values) in enumerate(((gate, go_ref[...]), (1.0, normed))):
        columns = pl.ds((1 - part) * width, width)
        sent_ref[:, columns] = dot(jnp.where(hit, weight, 0.0).astype(BF16), values).astype(BF16)
        if capacity % 16:
            for j in range(count):
                outs[j][:, columns] = sent_ref[spans[j], columns]
        else:
            stores += start_copies(
                [(sent_ref.at[spans[j], columns], outs[j].at[:, columns]) for j in range(count)],
                sems.at[part],
            )
    for copy in stores:
        copy.wait()


def place_kernel(
    sources, capacity, me, place, ids_hbm, gate_hbm, tok_hbm, gain_hbm, go_hbm, target_ref, *refs
):
    *outs, wide_ref, ids_ref, gate_ref, tok_ref, gain_ref, go_ref, sent_ref, in_sems, out_sems = refs
    tok_rows = tok_ref.shape[0]
    loads = start_copies(
        [(ids_hbm, ids_ref), (tok_hbm, tok_ref), (gain_hbm, gain_ref), (gate_hbm, gate_ref), (go_hbm, go_ref)],
        in_sems,
    )
    earlier = lax.broadcasted_iota(jnp.int32, (LANES, LANES), 0) < lax.broadcasted_iota(
        jnp.int32, (LANES, LANES), 1
    )
    earlier = jnp.where(earlier, 1.0, 0.0).astype(BF16)
    loads[0].wait()
    chunks = range(0, tok_rows, LANES)
    wide_ref[...] = jnp.full_like(wide_ref, -1)
    wide_ref[:, :tok_rows] = ids_ref[...]
    ids = [wide_ref[:, c : c + LANES] for c in chunks]
    expert = lax.broadcasted_iota(jnp.int32, (sources, LANES), 0)
    onehots = [jnp.where(expert == chunk, 1.0, 0.0) for chunk in ids]
    within = dot(jnp.concatenate(onehots).astype(BF16), earlier)
    base = jnp.zeros((sources, 1), F32)
    for i, (c, chunk, onehot) in enumerate(zip(chunks, ids, onehots)):
        before = within[i * sources : (i + 1) * sources] + base
        base += jnp.sum(onehot, axis=1, keepdims=True)
        rank = jnp.sum(before * onehot, axis=0, keepdims=True).astype(jnp.int32)
        away = jnp.bitwise_xor(chunk, me[0])
        block = jnp.zeros_like(away)
        for j, k in enumerate(block_order(sources)):
            block = jnp.where(away == k, j, block)
        end = min(LANES, tok_rows - c)
        target = jnp.where(rank < capacity, block * capacity + rank, -1)
        target_ref[:, c : c + end] = target[:, :end]
    for copy in loads[1:]:
        copy.wait()
    put_blocks(0, target_ref[...], gate_ref[...], tok_ref, gain_ref, go_ref, sent_ref, outs, out_sems)


def rest_kernel(first, target_ref, gate_ref, tok_ref, gain_ref, go_ref, *refs):
    *outs, sent_ref, sems = refs
    put_blocks(first, target_ref[...], gate_ref[...], tok_ref, gain_ref, go_ref, sent_ref, outs, sems)


def keep_kernel(block_ref, out_ref):
    out_ref[...] = block_ref[...]


def gelu_parts(value):
    root = 0.7978845608028654
    cubic = root * 0.044715
    square = value * value
    tan = jnp.tanh(value * (root + cubic * square))
    half = 0.5 + 0.5 * tan
    act = value * half
    return act, half + act * (1.0 - tan) * (root + 3.0 * cubic * square)


def shard_order(place):
    first = jnp.where(lax.rem(place, 2) == 0, 3, 0)
    second = jnp.where(place < 2, 2, 1)
    return [first, second, 6 - first - second - place, place]


def expert_work(order, blocks, w_in_ref, w_out_ref, gpre_ref, extra_ref, rows_ref, turned_ref, put):
    capacity = blocks[0].shape[0]
    width, hidden = w_in_ref.shape
    piece_d, piece_f = width // LINE, hidden // LINE
    for j, block in enumerate(blocks):
        rows_ref[j * capacity : (j + 1) * capacity, :] = block[...]
    for j in range(LINE):
        start = pl.multiple_of(order[j] * piece_d, piece_d)
        turned_ref[j * piece_d : (j + 1) * piece_d, :] = rows_ref[:, pl.ds(start, piece_d)].T
    total = jnp.zeros(extra_ref.shape, F32)
    for j in range(LINE):
        part = pl.ds(pl.multiple_of(order[j] * piece_f, piece_f), piece_f)
        delta = rows_ref[:, width:]
        act, slope = gelu_parts(dot(rows_ref[:, :width], w_in_ref[:, part]))
        grad_act = dot(delta, w_out_ref[part, :], ((1,), (1,)))
        products = act * grad_act
        for lane in range(0, piece_f, LANES):
            total += products[:, lane : lane + LANES]
        grad_pre = (grad_act * slope).astype(BF16)
        gpre_ref[:, part] = grad_pre
        put(j, part, dot(turned_ref[...], grad_pre), dot(act.astype(BF16).T, delta))
    total = jnp.sum(total, axis=1, keepdims=True)
    high = total.astype(BF16).astype(F32)
    lane = lax.broadcasted_iota(jnp.int32, extra_ref.shape, 1)
    extra_ref[...] = jnp.where(lane == 0, high, jnp.where(lane == 1, total - high, 0.0)).astype(BF16)


def sooner_kernel(count, groups, place, w_in_ref, w_out_ref, *refs):
    blocks = refs[:count]
    sum_in_ref, sum_out_ref, gpre_ref, extra_ref, rows_ref, turned_ref = refs[count:]
    piece_f = w_in_ref.shape[1] // LINE

    def put(j, part, weight_in, weight_out):
        sum_in_ref[:, part] = weight_in
        sum_out_ref[j * piece_f : (j + 1) * piece_f, :] = weight_out

    order = shard_order(place[0]) if groups == LINE else list(range(LINE))
    expert_work(order, blocks, w_in_ref, w_out_ref, gpre_ref, extra_ref, rows_ref, turned_ref, put)


def next_kernel(count, groups, place, w_in_ref, w_out_ref, old_in_ref, old_out_ref, *refs):
    blocks = refs[:count]
    sum_in_ref, sum_out_ref, gpre_ref, extra_ref, rows_ref, turned_ref = refs[count:]
    piece_f = w_in_ref.shape[1] // LINE

    def put(j, part, weight_in, weight_out):
        chunk = slice(j * piece_f, (j + 1) * piece_f)
        sum_in_ref[:, part] = old_in_ref[:, part] + weight_in
        sum_out_ref[chunk, :] = old_out_ref[chunk, :] + weight_out

    order = shard_order(place[0]) if groups == LINE else list(range(LINE))
    expert_work(order, blocks, w_in_ref, w_out_ref, gpre_ref, extra_ref, rows_ref, turned_ref, put)


def later_kernel(count, groups, place, w_in_ref, w_out_ref, sum_in_ref, sum_out_ref, *refs):
    blocks = refs[:count]
    outs = refs[count : count + LINE]
    gpre_ref, extra_ref, rows_ref, turned_ref = refs[count + LINE :]
    width, hidden = w_in_ref.shape
    piece_d, piece_f = width // LINE, hidden // LINE

    def put(j, part, weight_in, weight_out):
        weight = (sum_out_ref[j * piece_f : (j + 1) * piece_f, :] + weight_out).astype(BF16)
        outs[j][piece_d:, :width] = weight[: piece_f // 2]
        outs[j][piece_d:, width:] = weight[piece_f // 2 :]
        weight = (sum_in_ref[:, part] + weight_in).astype(BF16)
        for i in range(LINE):
            outs[i][:piece_d, part] = weight[i * piece_d : (i + 1) * piece_d]

    order = shard_order(place[0]) if groups == LINE else list(range(LINE))
    expert_work(order, blocks, w_in_ref, w_out_ref, gpre_ref, extra_ref, rows_ref, turned_ref, put)


def back_kernel(capacity, sets, w_in_ref, *refs):
    inputs, outs = refs[: 2 * len(sets)], refs[2 * len(sets) :]
    width = w_in_ref.shape[0]
    for members, gpre_ref, extra_ref in zip(sets, inputs[::2], inputs[1::2]):
        grad = dot(gpre_ref[...], w_in_ref[...], ((1,), (1,))).astype(BF16)
        for i, j in enumerate(members):
            block = slice(i * capacity, (i + 1) * capacity)
            outs[j][:, :width] = grad[block]
            outs[j][:, width:] = extra_ref[block, :]


def finish_kernel(target_ref, gate_ref, tok_ref, gain_ref, go_ref, *refs):
    *blocks, tokens_out, gate_out, back_ref = refs
    rows, capacity = back_ref.shape[0], blocks[0].shape[0]
    for j, block in enumerate(blocks):
        back_ref[j * capacity : (j + 1) * capacity, :] = block[...]
    tok_rows, width = tok_ref.shape
    spots = jnp.broadcast_to(target_ref[...].astype(F32), (8, tok_rows)).T[:, :1].astype(jnp.int32)
    hit = lax.broadcasted_iota(jnp.int32, (tok_rows, rows), 1) == spots
    got = dot(jnp.where(hit, 1.0, 0.0).astype(BF16), back_ref[...])
    sums = got[:, width:].T
    gate_row = gate_ref[...].astype(F32).reshape(1, tok_rows)
    gate_out[...] = ((sums[0:1] + sums[1:2]) / gate_row).astype(BF16).reshape(tok_rows)
    scaled, spread = normalize(tok_ref[...])
    grad = got[:, :width] * gain_ref[...]
    mean = jnp.mean(grad, axis=-1, keepdims=True)
    cross = jnp.mean(grad * scaled, axis=-1, keepdims=True)
    branch = spread * (grad - mean - scaled * cross)
    tokens_out[...] = (go_ref[...].astype(F32) + branch).astype(BF16)


def block_order(sources):
    same = sorted(range(2, sources, 2), key=lambda k: (k.bit_count(), -k))
    return same + list(range(sources - 1, 1, -2)) + [1, 0]


def swap_blocks(blocks, order):
    devices = range(lax.axis_size("space"))
    return [
        lax.ppermute(block, "space", [(i, i ^ k) for i in devices]) if k else block
        for block, k in zip(blocks, order)
    ]


def pass_kernel(place, swapped_ref, middle_ref, third_ref, own_ref, out_ref, sum_ref):
    inner = (place[0] == 1) | (place[0] == 2)
    swapped, middle = swapped_ref[...].astype(F32), middle_ref[...].astype(F32)
    out_ref[...] = (third_ref[...].astype(F32) + jnp.where(inner, swapped, 0.0)).astype(BF16)
    sum_ref[...] = own_ref[...].astype(F32) + jnp.where(inner, middle, swapped)


def total_kernel(sum_ref, across_ref, last_ref, in_ref, out_ref):
    piece_d, half = in_ref.shape[0], out_ref.shape[0] // 2
    width = out_ref.shape[1]
    total = sum_ref[...] + across_ref[...].astype(F32) + last_ref[...].astype(F32)
    in_ref[...] = total[:piece_d]
    out_ref[:half, :] = total[piece_d:, :width]
    out_ref[half:, :] = total[piece_d:, width:]


def line_sums(place, first, second, third, own, width, returned):
    rows, hidden = own.shape
    piece_d = width // LINE
    half = len(returned) // 2
    order = block_order(len(returned))
    middle = lax.ppermute(second, "dp", [(0, 0), (1, 2), (2, 1), (3, 3)])
    swapped = lax.ppermute(first, "dp", [(0, 1), (1, 0), (2, 3), (3, 2)])
    across = lax.ppermute(second, "dp", [(0, 2), (3, 1)])
    back = swap_blocks(returned[:half], order[:half])
    third, *back = lax.optimization_barrier((third, *back))
    passed, most = kernel_call(
        pass_kernel,
        "pass",
        1,
        1,
        [jax.ShapeDtypeStruct(own.shape, BF16), jax.ShapeDtypeStruct(own.shape, F32)],
        [smem] + [vmem] * 4,
    )(place, swapped, middle, third, own)
    last = lax.ppermute(passed, "dp", [(0, 1), (3, 2), (1, 3), (2, 0)])
    across, *rest = lax.optimization_barrier((across, *returned[half:]))
    back += swap_blocks(rest, order[half:])
    sums = kernel_call(
        total_kernel,
        "total",
        1,
        1,
        [
            jax.ShapeDtypeStruct((piece_d, hidden), F32),
            jax.ShapeDtypeStruct((2 * (rows - piece_d), width), F32),
        ],
        [vmem] * 3,
    )(most, across, last)
    return *sums, back


def body(tokens, gain, w_in, w_out, expert_ids, gate, grad_out):
    sources = lax.axis_size("space")
    groups = lax.axis_size("dp")
    tok_rows, width = tokens.shape
    hidden = w_in.shape[2]
    capacity = ((tok_rows * 5 // 4 + sources - 1) // sources + 7) // 8 * 8
    rows = sources * capacity
    me = lax.axis_index("space").astype(jnp.int32).reshape(1)
    place = lax.axis_index("dp").astype(jnp.int32).reshape(1)
    ids_row = expert_ids.reshape(1, tok_rows)
    gain_row = gain.reshape(1, width)
    weight_in, weight_out = w_in[0], w_out[0]
    shape = jax.ShapeDtypeStruct
    sems = pltpu.SemaphoreType.DMA
    block_place = vmem if capacity % 16 else anywhere
    io_bytes = 2 * (2 * tok_rows * width + 2 * rows * width)

    soon = sources // 2
    blocks = [shape((capacity, 2 * width), BF16)] * soon
    target, *sent = kernel_call(
        functools.partial(place_kernel, sources, capacity),
        "place",
        2 * rows * tok_rows * width,
        io_bytes,
        [shape((1, tok_rows), jnp.int32)] + blocks,
        [smem] * 2 + [hbm] * 5,
        [
            pltpu.VMEM((1, pl.cdiv(tok_rows, LANES) * LANES), jnp.int32),
            pltpu.VMEM((1, tok_rows), jnp.int32),
            pltpu.VMEM((tok_rows,), BF16),
            pltpu.VMEM((tok_rows, width), BF16),
            pltpu.VMEM((1, width), F32),
            pltpu.VMEM((tok_rows, width), BF16),
            pltpu.VMEM((soon * capacity, 2 * width), BF16),
            sems((5,)),
            sems((2, soon)),
        ],
        places=[vmem] + [block_place] * soon,
        vmem_mib=56,
    )(me, place, ids_row, gate, tokens, gain_row, grad_out)
    sent += kernel_call(
        functools.partial(rest_kernel, soon),
        "rest",
        1,
        1,
        blocks,
        [vmem] * 5,
        [pltpu.VMEM((soon * capacity, 2 * width), BF16), sems((2, soon))],
        places=[block_place] * soon,
        vmem_mib=16,
    )(target, gate, tokens, gain_row, grad_out)
    (kept,) = kernel_call(
        keep_kernel,
        "keep",
        1,
        1,
        [shape((capacity, 2 * width), BF16)],
        [vmem],
        vmem_mib=2,
    )(sent[-1])
    arrived = swap_blocks(sent, block_order(sources))
    arrived[-1] = kept

    next_set = list(range(3 * sources // 8, sources // 2))
    late_set = list(range(sources // 2, 3 * sources // 4))
    soon_set = [j for j in range(sources) if j not in next_set + late_set]

    def work(kernel, name, members, outs, *sums):
        count, span = len(members), len(members) * capacity
        return kernel_call(
            functools.partial(kernel, count, groups),
            name,
            8 * span * width * hidden,
            2 * (2 * span * width + 4 * width * hidden + span * hidden),
            outs + [shape((span, hidden), BF16), shape((span, LANES), BF16)],
            [smem] + [vmem] * (2 + len(sums) + count),
            [pltpu.VMEM((span, 2 * width), BF16), pltpu.VMEM((width, span), BF16)],
        )(place, weight_in, weight_out, *sums, *[arrived[j] for j in members])

    sums_shape = [shape((width, hidden), F32), shape((hidden, width), F32)]
    *sums, soon_gpre, soon_extra = work(sooner_kernel, "sooner", soon_set, sums_shape)
    *sums, next_gpre, next_extra = work(next_kernel, "next", next_set, sums_shape, *sums)
    piece = shape((width // LINE + hidden // LINE // 2, hidden), BF16)
    *parts, late_gpre, late_extra = work(later_kernel, "later", late_set, [piece] * LINE, *sums)
    returned = kernel_call(
        functools.partial(back_kernel, capacity, (soon_set, next_set, late_set)),
        "back",
        1,
        1,
        [shape((capacity, width + LANES), BF16)] * sources,
        [vmem] * 7,
    )(weight_in, soon_gpre, soon_extra, next_gpre, next_extra, late_gpre, late_extra)

    if groups == LINE:
        grad_w_in, grad_w_out, back = line_sums(place, *parts, width, returned)
    else:
        back = swap_blocks(returned, block_order(sources))
        parts_in, parts_out = zip(*[split_piece(part, width, LINE) for part in parts])
        grad_w_in, grad_w_out = (
            lax.psum_scatter(
                jnp.concatenate(part), "dp", scatter_dimension=0, tiled=True
            ).astype(F32)
            for part in (parts_in, parts_out)
        )
    grad_tokens, grad_gate = kernel_call(
        finish_kernel,
        "finish",
        1,
        1,
        [shape((tok_rows, width), BF16), shape((tok_rows,), BF16)],
        [vmem] * (5 + sources),
        [pltpu.VMEM((rows, width + LANES), BF16)],
    )(target, gate, tokens, gain_row, grad_out, *back)
    return (grad_tokens, grad_gate, grad_w_in[None], grad_w_out[None])


def split_piece(piece, width, pieces):
    piece_d = width // pieces
    lower = piece[piece_d:]
    return piece[:piece_d], jnp.concatenate([lower[:, :width], lower[:, width:]])


def solution(mesh):
    placed = (
        P(("space", "dp"), None),
        P(),
        P("space", None, None),
        P("space", None, None),
        P(("space", "dp"), None),
        P(("space", "dp")),
        P(("space", "dp"), None),
    )
    return jax.shard_map(
        body,
        mesh=mesh,
        in_specs=placed,
        out_specs=(
            P(("space", "dp"), None),
            P(("space", "dp")),
            P("space", "dp", None),
            P("space", "dp", None),
        ),
        check_vma=False,
    )
```

```python
import functools

import jax
import jax.numpy as jnp
from jax import lax
from jax.experimental import pallas as pl
from jax.experimental.pallas import tpu as pltpu
from jax.sharding import PartitionSpec as P

epsilon = 1e-05
F32 = jnp.float32
BF16 = jnp.bfloat16
LANES = 128
LINE = 4
MIB = 1024 * 1024

vmem = pl.BlockSpec(memory_space=pltpu.VMEM)
smem = pl.BlockSpec(memory_space=pltpu.SMEM)
hbm = pl.BlockSpec(memory_space=pltpu.HBM)
anywhere = pl.BlockSpec(memory_space=pl.ANY)


def dot(left, right, contract=((1,), (0,))):
    return lax.dot_general(left, right, (contract, ((), ())), preferred_element_type=F32)


def normalize(tokens):
    values = tokens.astype(F32)
    center = values - jnp.mean(values, axis=-1, keepdims=True)
    spread = lax.rsqrt(jnp.mean(center * center, axis=-1, keepdims=True) + epsilon)
    return center * spread, spread


def kernel_call(kernel, name, flops, nbytes, outs, ins, scratch=(), places=None, vmem_mib=24):
    return pl.pallas_call(
        kernel,
        name=name,
        out_shape=outs,
        in_specs=ins,
        out_specs=places or [vmem] * len(outs),
        scratch_shapes=list(scratch),
        compiler_params=pltpu.CompilerParams(vmem_limit_bytes=vmem_mib * MIB),
        cost_estimate=pl.CostEstimate(flops=flops, bytes_accessed=nbytes, transcendentals=0),
    )


def start_copies(pairs, sems):
    copies = [pltpu.make_async_copy(src, dst, sems.at[i]) for i, (src, dst) in enumerate(pairs)]
    for copy in copies:
        copy.start()
    return copies


def put_blocks(first, target, gate, tok_ref, gain_ref, go_ref, sent_ref, outs, sems):
    capacity, width = outs[0].shape[0], tok_ref.shape[1]
    count = len(outs)
    hit = lax.broadcasted_iota(jnp.int32, (count * capacity, target.shape[1]), 0) == (
        target - first * capacity
    )
    gate = gate.astype(F32).reshape(target.shape)
    scaled, _ = normalize(tok_ref[...])
    normed = (scaled * gain_ref[...]).astype(BF16)
    spans = [pl.ds(j * capacity, capacity) for j in range(count)]
    stores = []
    for part, (weight, values) in enumerate(((gate, go_ref[...]), (1.0, normed))):
        columns = pl.ds((1 - part) * width, width)
        sent_ref[:, columns] = dot(jnp.where(hit, weight, 0.0).astype(BF16), values).astype(BF16)
        if capacity % 16:
            for j in range(count):
                outs[j][:, columns] = sent_ref[spans[j], columns]
        else:
            stores += start_copies(
                [(sent_ref.at[spans[j], columns], outs[j].at[:, columns]) for j in range(count)],
                sems.at[part],
            )
    for copy in stores:
        copy.wait()


def place_kernel(
    sources, capacity, me, place, ids_hbm, gate_hbm, tok_hbm, gain_hbm, go_hbm, target_ref, *refs
):
    *outs, wide_ref, ids_ref, gate_ref, tok_ref, gain_ref, go_ref, sent_ref, in_sems, out_sems = refs
    tok_rows = tok_ref.shape[0]
    loads = start_copies(
        [(ids_hbm, ids_ref), (tok_hbm, tok_ref), (gain_hbm, gain_ref), (gate_hbm, gate_ref), (go_hbm, go_ref)],
        in_sems,
    )
    earlier = lax.broadcasted_iota(jnp.int32, (LANES, LANES), 0) < lax.broadcasted_iota(
        jnp.int32, (LANES, LANES), 1
    )
    earlier = jnp.where(earlier, 1.0, 0.0).astype(BF16)
    loads[0].wait()
    chunks = range(0, tok_rows, LANES)
    wide_ref[...] = jnp.full_like(wide_ref, -1)
    wide_ref[:, :tok_rows] = ids_ref[...]
    ids = [wide_ref[:, c : c + LANES] for c in chunks]
    expert = lax.broadcasted_iota(jnp.int32, (sources, LANES), 0)
    onehots = [jnp.where(expert == chunk, 1.0, 0.0) for chunk in ids]
    within = dot(jnp.concatenate(onehots).astype(BF16), earlier)
    base = jnp.zeros((sources, 1), F32)
    for i, (c, chunk, onehot) in enumerate(zip(chunks, ids, onehots)):
        before = within[i * sources : (i + 1) * sources] + base
        base += jnp.sum(onehot, axis=1, keepdims=True)
        rank = jnp.sum(before * onehot, axis=0, keepdims=True).astype(jnp.int32)
        away = jnp.bitwise_xor(chunk, me[0])
        block = jnp.zeros_like(away)
        for j, k in enumerate(block_order(sources)):
            block = jnp.where(away == k, j, block)
        end = min(LANES, tok_rows - c)
        target = jnp.where(rank < capacity, block * capacity + rank, -1)
        target_ref[:, c : c + end] = target[:, :end]
    for copy in loads[1:]:
        copy.wait()
    put_blocks(0, target_ref[...], gate_ref[...], tok_ref, gain_ref, go_ref, sent_ref, outs, out_sems)


def rest_kernel(first, target_ref, gate_ref, tok_ref, gain_ref, go_ref, *refs):
    *outs, sent_ref, sems = refs
    put_blocks(first, target_ref[...], gate_ref[...], tok_ref, gain_ref, go_ref, sent_ref, outs, sems)


def keep_kernel(block_ref, out_ref):
    out_ref[...] = block_ref[...]


def gelu_parts(value):
    root = 0.7978845608028654
    cubic = root * 0.044715
    square = value * value
    tan = jnp.tanh(value * (root + cubic * square))
    half = 0.5 + 0.5 * tan
    act = value * half
    return act, half + act * (1.0 - tan) * (root + 3.0 * cubic * square)


def shard_order(place):
    first = jnp.where(lax.rem(place, 2) == 0, 3, 0)
    second = jnp.where(place < 2, 2, 1)
    return [first, second, 6 - first - second - place, place]


def expert_work(order, blocks, w_in_ref, w_out_ref, gpre_ref, extra_ref, rows_ref, turned_ref, put):
    capacity = blocks[0].shape[0]
    width, hidden = w_in_ref.shape
    piece_d, piece_f = width // LINE, hidden // LINE
    for j, block in enumerate(blocks):
        rows_ref[j * capacity : (j + 1) * capacity, :] = block[...]
    for j in range(LINE):
        start = pl.multiple_of(order[j] * piece_d, piece_d)
        turned_ref[j * piece_d : (j + 1) * piece_d, :] = rows_ref[:, pl.ds(start, piece_d)].T
    total = jnp.zeros(extra_ref.shape, F32)
    for j in range(LINE):
        part = pl.ds(pl.multiple_of(order[j] * piece_f, piece_f), piece_f)
        delta = rows_ref[:, width:]
        act, slope = gelu_parts(dot(rows_ref[:, :width], w_in_ref[:, part]))
        grad_act = dot(delta, w_out_ref[part, :], ((1,), (1,)))
        products = act * grad_act
        for lane in range(0, piece_f, LANES):
            total += products[:, lane : lane + LANES]
        grad_pre = (grad_act * slope).astype(BF16)
        gpre_ref[:, part] = grad_pre
        put(j, part, dot(turned_ref[...], grad_pre), dot(act.astype(BF16).T, delta))
    total = jnp.sum(total, axis=1, keepdims=True)
    high = total.astype(BF16).astype(F32)
    lane = lax.broadcasted_iota(jnp.int32, extra_ref.shape, 1)
    extra_ref[...] = jnp.where(lane == 0, high, jnp.where(lane == 1, total - high, 0.0)).astype(BF16)


def sooner_kernel(count, groups, place, w_in_ref, w_out_ref, *refs):
    blocks = refs[:count]
    sum_in_ref, sum_out_ref, gpre_ref, extra_ref, rows_ref, turned_ref = refs[count:]
    piece_f = w_in_ref.shape[1] // LINE

    def put(j, part, weight_in, weight_out):
        sum_in_ref[:, part] = weight_in
        sum_out_ref[j * piece_f : (j + 1) * piece_f, :] = weight_out

    order = shard_order(place[0]) if groups == LINE else list(range(LINE))
    expert_work(order, blocks, w_in_ref, w_out_ref, gpre_ref, extra_ref, rows_ref, turned_ref, put)


def next_kernel(count, groups, place, w_in_ref, w_out_ref, old_in_ref, old_out_ref, *refs):
    blocks = refs[:count]
    sum_in_ref, sum_out_ref, gpre_ref, extra_ref, rows_ref, turned_ref = refs[count:]
    piece_f = w_in_ref.shape[1] // LINE

    def put(j, part, weight_in, weight_out):
        chunk = slice(j * piece_f, (j + 1) * piece_f)
        sum_in_ref[:, part] = old_in_ref[:, part] + weight_in
        sum_out_ref[chunk, :] = old_out_ref[chunk, :] + weight_out

    order = shard_order(place[0]) if groups == LINE else list(range(LINE))
    expert_work(order, blocks, w_in_ref, w_out_ref, gpre_ref, extra_ref, rows_ref, turned_ref, put)


def later_kernel(count, groups, place, w_in_ref, w_out_ref, sum_in_ref, sum_out_ref, *refs):
    blocks = refs[:count]
    outs = refs[count : count + LINE]
    gpre_ref, extra_ref, rows_ref, turned_ref = refs[count + LINE :]
    width, hidden = w_in_ref.shape
    piece_d, piece_f = width // LINE, hidden // LINE

    def put(j, part, weight_in, weight_out):
        weight = (sum_out_ref[j * piece_f : (j + 1) * piece_f, :] + weight_out).astype(BF16)
        outs[j][piece_d:, :width] = weight[: piece_f // 2]
        outs[j][piece_d:, width:] = weight[piece_f // 2 :]
        weight = (sum_in_ref[:, part] + weight_in).astype(BF16)
        for i in range(LINE):
            outs[i][:piece_d, part] = weight[i * piece_d : (i + 1) * piece_d]

    order = shard_order(place[0]) if groups == LINE else list(range(LINE))
    expert_work(order, blocks, w_in_ref, w_out_ref, gpre_ref, extra_ref, rows_ref, turned_ref, put)


def back_kernel(capacity, sets, w_in_ref, *refs):
    inputs, outs = refs[: 2 * len(sets)], refs[2 * len(sets) :]
    width = w_in_ref.shape[0]
    for members, gpre_ref, extra_ref in zip(sets, inputs[::2], inputs[1::2]):
        grad = dot(gpre_ref[...], w_in_ref[...], ((1,), (1,))).astype(BF16)
        for i, j in enumerate(members):
            block = slice(i * capacity, (i + 1) * capacity)
            outs[j][:, :width] = grad[block]
            outs[j][:, width:] = extra_ref[block, :]


def finish_kernel(target_ref, gate_ref, tok_ref, gain_ref, go_ref, *refs):
    *blocks, tokens_out, gate_out, back_ref = refs
    rows, capacity = back_ref.shape[0], blocks[0].shape[0]
    for j, block in enumerate(blocks):
        back_ref[j * capacity : (j + 1) * capacity, :] = block[...]
    tok_rows, width = tok_ref.shape
    spots = jnp.broadcast_to(target_ref[...].astype(F32), (8, tok_rows)).T[:, :1].astype(jnp.int32)
    hit = lax.broadcasted_iota(jnp.int32, (tok_rows, rows), 1) == spots
    got = dot(jnp.where(hit, 1.0, 0.0).astype(BF16), back_ref[...])
    sums = got[:, width:].T
    gate_row = gate_ref[...].astype(F32).reshape(1, tok_rows)
    gate_out[...] = ((sums[0:1] + sums[1:2]) / gate_row).astype(BF16).reshape(tok_rows)
    scaled, spread = normalize(tok_ref[...])
    grad = got[:, :width] * gain_ref[...]
    mean = jnp.mean(grad, axis=-1, keepdims=True)
    cross = jnp.mean(grad * scaled, axis=-1, keepdims=True)
    branch = spread * (grad - mean - scaled * cross)
    tokens_out[...] = (go_ref[...].astype(F32) + branch).astype(BF16)


def block_order(sources):
    same = sorted(range(2, sources, 2), key=lambda k: (k.bit_count(), -k))
    return same + list(range(sources - 1, 1, -2)) + [1, 0]


def swap_blocks(blocks, order):
    devices = range(lax.axis_size("space"))
    return [
        lax.ppermute(block, "space", [(i, i ^ k) for i in devices]) if k else block
        for block, k in zip(blocks, order)
    ]


def pass_kernel(place, swapped_ref, middle_ref, third_ref, own_ref, out_ref, sum_ref):
    inner = (place[0] == 1) | (place[0] == 2)
    swapped, middle = swapped_ref[...].astype(F32), middle_ref[...].astype(F32)
    out_ref[...] = (third_ref[...].astype(F32) + jnp.where(inner, swapped, 0.0)).astype(BF16)
    sum_ref[...] = own_ref[...].astype(F32) + jnp.where(inner, middle, swapped)


def total_kernel(sum_ref, across_ref, last_ref, in_ref, out_ref):
    piece_d, half = in_ref.shape[0], out_ref.shape[0] // 2
    width = out_ref.shape[1]
    total = sum_ref[...] + across_ref[...].astype(F32) + last_ref[...].astype(F32)
    in_ref[...] = total[:piece_d]
    out_ref[:half, :] = total[piece_d:, :width]
    out_ref[half:, :] = total[piece_d:, width:]


def line_sums(place, first, second, third, own, width, returned):
    rows, hidden = own.shape
    piece_d = width // LINE
    ahead = 3 * len(returned) // 8
    order = block_order(len(returned))
    middle = lax.ppermute(second, "dp", [(0, 0), (1, 2), (2, 1), (3, 3)])
    swapped = lax.ppermute(first, "dp", [(0, 1), (1, 0), (2, 3), (3, 2)])
    back = swap_blocks(returned[:ahead], order[:ahead])
    second, back[0] = lax.optimization_barrier((second, back[0]))
    across = lax.ppermute(second, "dp", [(0, 2), (3, 1)])
    third, *back = lax.optimization_barrier((third, *back))
    passed, most = kernel_call(
        pass_kernel,
        "pass",
        1,
        1,
        [jax.ShapeDtypeStruct(own.shape, BF16), jax.ShapeDtypeStruct(own.shape, F32)],
        [smem] + [vmem] * 4,
    )(place, swapped, middle, third, own)
    last = lax.ppermute(passed, "dp", [(0, 1), (3, 2), (1, 3), (2, 0)])
    across, *rest = lax.optimization_barrier((across, *returned[ahead:]))
    back += swap_blocks(rest, order[ahead:])
    sums = kernel_call(
        total_kernel,
        "total",
        1,
        1,
        [
            jax.ShapeDtypeStruct((piece_d, hidden), F32),
            jax.ShapeDtypeStruct((2 * (rows - piece_d), width), F32),
        ],
        [vmem] * 3,
    )(most, across, last)
    return *sums, back


def body(tokens, gain, w_in, w_out, expert_ids, gate, grad_out):
    sources = lax.axis_size("space")
    groups = lax.axis_size("dp")
    tok_rows, width = tokens.shape
    hidden = w_in.shape[2]
    capacity = ((tok_rows * 5 // 4 + sources - 1) // sources + 7) // 8 * 8
    rows = sources * capacity
    me = lax.axis_index("space").astype(jnp.int32).reshape(1)
    place = lax.axis_index("dp").astype(jnp.int32).reshape(1)
    ids_row = expert_ids.reshape(1, tok_rows)
    gain_row = gain.reshape(1, width)
    weight_in, weight_out = w_in[0], w_out[0]
    shape = jax.ShapeDtypeStruct
    sems = pltpu.SemaphoreType.DMA
    block_place = vmem if capacity % 16 else anywhere
    io_bytes = 2 * (2 * tok_rows * width + 2 * rows * width)

    soon = sources // 2
    blocks = [shape((capacity, 2 * width), BF16)] * soon
    target, *sent = kernel_call(
        functools.partial(place_kernel, sources, capacity),
        "place",
        2 * rows * tok_rows * width,
        io_bytes,
        [shape((1, tok_rows), jnp.int32)] + blocks,
        [smem] * 2 + [hbm] * 5,
        [
            pltpu.VMEM((1, pl.cdiv(tok_rows, LANES) * LANES), jnp.int32),
            pltpu.VMEM((1, tok_rows), jnp.int32),
            pltpu.VMEM((tok_rows,), BF16),
            pltpu.VMEM((tok_rows, width), BF16),
            pltpu.VMEM((1, width), F32),
            pltpu.VMEM((tok_rows, width), BF16),
            pltpu.VMEM((soon * capacity, 2 * width), BF16),
            sems((5,)),
            sems((2, soon)),
        ],
        places=[vmem] + [block_place] * soon,
        vmem_mib=56,
    )(me, place, ids_row, gate, tokens, gain_row, grad_out)
    sent += kernel_call(
        functools.partial(rest_kernel, soon),
        "rest",
        1,
        1,
        blocks,
        [vmem] * 5,
        [pltpu.VMEM((soon * capacity, 2 * width), BF16), sems((2, soon))],
        places=[block_place] * soon,
        vmem_mib=16,
    )(target, gate, tokens, gain_row, grad_out)
    (kept,) = kernel_call(
        keep_kernel,
        "keep",
        1,
        1,
        [shape((capacity, 2 * width), BF16)],
        [vmem],
        vmem_mib=2,
    )(sent[-1])
    arrived = swap_blocks(sent, block_order(sources))
    arrived[-1] = kept

    next_set = list(range(3 * sources // 8, sources // 2))
    late_set = list(range(sources // 2, 3 * sources // 4))
    soon_set = [j for j in range(sources) if j not in next_set + late_set]

    def work(kernel, name, members, outs, *sums):
        count, span = len(members), len(members) * capacity
        return kernel_call(
            functools.partial(kernel, count, groups),
            name,
            8 * span * width * hidden,
            2 * (2 * span * width + 4 * width * hidden + span * hidden),
            outs + [shape((span, hidden), BF16), shape((span, LANES), BF16)],
            [smem] + [vmem] * (2 + len(sums) + count),
            [pltpu.VMEM((span, 2 * width), BF16), pltpu.VMEM((width, span), BF16)],
        )(place, weight_in, weight_out, *sums, *[arrived[j] for j in members])

    sums_shape = [shape((width, hidden), F32), shape((hidden, width), F32)]
    *sums, soon_gpre, soon_extra = work(sooner_kernel, "sooner", soon_set, sums_shape)
    *sums, next_gpre, next_extra = work(next_kernel, "next", next_set, sums_shape, *sums)
    piece = shape((width // LINE + hidden // LINE // 2, hidden), BF16)
    *parts, late_gpre, late_extra = work(later_kernel, "later", late_set, [piece] * LINE, *sums)
    returned = kernel_call(
        functools.partial(back_kernel, capacity, (soon_set, next_set, late_set)),
        "back",
        1,
        1,
        [shape((capacity, width + LANES), BF16)] * sources,
        [vmem] * 7,
    )(weight_in, soon_gpre, soon_extra, next_gpre, next_extra, late_gpre, late_extra)

    if groups == LINE:
        grad_w_in, grad_w_out, back = line_sums(place, *parts, width, returned)
    else:
        back = swap_blocks(returned, block_order(sources))
        parts_in, parts_out = zip(*[split_piece(part, width, LINE) for part in parts])
        grad_w_in, grad_w_out = (
            lax.psum_scatter(
                jnp.concatenate(part), "dp", scatter_dimension=0, tiled=True
            ).astype(F32)
            for part in (parts_in, parts_out)
        )
    grad_tokens, grad_gate = kernel_call(
        finish_kernel,
        "finish",
        1,
        1,
        [shape((tok_rows, width), BF16), shape((tok_rows,), BF16)],
        [vmem] * (5 + sources),
        [pltpu.VMEM((rows, width + LANES), BF16)],
    )(target, gate, tokens, gain_row, grad_out, *back)
    return (grad_tokens, grad_gate, grad_w_in[None], grad_w_out[None])


def split_piece(piece, width, pieces):
    piece_d = width // pieces
    lower = piece[piece_d:]
    return piece[:piece_d], jnp.concatenate([lower[:, :width], lower[:, width:]])


def solution(mesh):
    placed = (
        P(("space", "dp"), None),
        P(),
        P("space", None, None),
        P("space", None, None),
        P(("space", "dp"), None),
        P(("space", "dp")),
        P(("space", "dp"), None),
    )
    return jax.shard_map(
        body,
        mesh=mesh,
        in_specs=placed,
        out_specs=(
            P(("space", "dp"), None),
            P(("space", "dp")),
            P("space", "dp", None),
            P("space", "dp", None),
        ),
        check_vma=False,
    )
```

```python
import functools

import jax
import jax.numpy as jnp
from jax import lax
from jax.experimental import pallas as pl
from jax.experimental.pallas import tpu as pltpu
from jax.sharding import PartitionSpec as P

epsilon = 1e-05
F32 = jnp.float32
BF16 = jnp.bfloat16
LANES = 128
LINE = 4
MIB = 1024 * 1024

vmem = pl.BlockSpec(memory_space=pltpu.VMEM)
smem = pl.BlockSpec(memory_space=pltpu.SMEM)
hbm = pl.BlockSpec(memory_space=pltpu.HBM)
anywhere = pl.BlockSpec(memory_space=pl.ANY)


def dot(left, right, contract=((1,), (0,))):
    return lax.dot_general(left, right, (contract, ((), ())), preferred_element_type=F32)


def normalize(tokens):
    values = tokens.astype(F32)
    center = values - jnp.mean(values, axis=-1, keepdims=True)
    spread = lax.rsqrt(jnp.mean(center * center, axis=-1, keepdims=True) + epsilon)
    return center * spread, spread


def kernel_call(kernel, name, flops, nbytes, outs, ins, scratch=(), places=None, vmem_mib=24):
    return pl.pallas_call(
        kernel,
        name=name,
        out_shape=outs,
        in_specs=ins,
        out_specs=places or [vmem] * len(outs),
        scratch_shapes=list(scratch),
        compiler_params=pltpu.CompilerParams(vmem_limit_bytes=vmem_mib * MIB),
        cost_estimate=pl.CostEstimate(flops=flops, bytes_accessed=nbytes, transcendentals=0),
    )


def start_copies(pairs, sems):
    copies = [pltpu.make_async_copy(src, dst, sems.at[i]) for i, (src, dst) in enumerate(pairs)]
    for copy in copies:
        copy.start()
    return copies


def put_blocks(first, target, gate, tok_ref, gain_ref, go_ref, sent_ref, outs, sems):
    capacity, width = outs[0].shape[0], tok_ref.shape[1]
    count = len(outs)
    hit = lax.broadcasted_iota(jnp.int32, (count * capacity, target.shape[1]), 0) == (
        target - first * capacity
    )
    gate = gate.astype(F32).reshape(target.shape)
    scaled, _ = normalize(tok_ref[...])
    normed = (scaled * gain_ref[...]).astype(BF16)
    spans = [pl.ds(j * capacity, capacity) for j in range(count)]
    stores = []
    for part, (weight, values) in enumerate(((gate, go_ref[...]), (1.0, normed))):
        columns = pl.ds((1 - part) * width, width)
        sent_ref[:, columns] = dot(jnp.where(hit, weight, 0.0).astype(BF16), values).astype(BF16)
        if capacity % 16:
            for j in range(count):
                outs[j][:, columns] = sent_ref[spans[j], columns]
        else:
            stores += start_copies(
                [(sent_ref.at[spans[j], columns], outs[j].at[:, columns]) for j in range(count)],
                sems.at[part],
            )
    for copy in stores:
        copy.wait()


def place_kernel(
    sources, capacity, me, place, ids_hbm, gate_hbm, tok_hbm, gain_hbm, go_hbm, target_ref, *refs
):
    *outs, wide_ref, ids_ref, gate_ref, tok_ref, gain_ref, go_ref, sent_ref, in_sems, out_sems = refs
    tok_rows = tok_ref.shape[0]
    loads = start_copies(
        [(ids_hbm, ids_ref), (tok_hbm, tok_ref), (gain_hbm, gain_ref), (gate_hbm, gate_ref), (go_hbm, go_ref)],
        in_sems,
    )
    earlier = lax.broadcasted_iota(jnp.int32, (LANES, LANES), 0) < lax.broadcasted_iota(
        jnp.int32, (LANES, LANES), 1
    )
    earlier = jnp.where(earlier, 1.0, 0.0).astype(BF16)
    loads[0].wait()
    chunks = range(0, tok_rows, LANES)
    wide_ref[...] = jnp.full_like(wide_ref, -1)
    wide_ref[:, :tok_rows] = ids_ref[...]
    ids = [wide_ref[:, c : c + LANES] for c in chunks]
    expert = lax.broadcasted_iota(jnp.int32, (sources, LANES), 0)
    onehots = [jnp.where(expert == chunk, 1.0, 0.0) for chunk in ids]
    within = dot(jnp.concatenate(onehots).astype(BF16), earlier)
    base = jnp.zeros((sources, 1), F32)
    for i, (c, chunk, onehot) in enumerate(zip(chunks, ids, onehots)):
        before = within[i * sources : (i + 1) * sources] + base
        base += jnp.sum(onehot, axis=1, keepdims=True)
        rank = jnp.sum(before * onehot, axis=0, keepdims=True).astype(jnp.int32)
        away = jnp.bitwise_xor(chunk, me[0])
        block = jnp.zeros_like(away)
        for j, k in enumerate(block_order(sources)):
            block = jnp.where(away == k, j, block)
        end = min(LANES, tok_rows - c)
        target = jnp.where(rank < capacity, block * capacity + rank, -1)
        target_ref[:, c : c + end] = target[:, :end]
    for copy in loads[1:]:
        copy.wait()
    put_blocks(0, target_ref[...], gate_ref[...], tok_ref, gain_ref, go_ref, sent_ref, outs, out_sems)


def rest_kernel(first, target_ref, gate_ref, tok_ref, gain_ref, go_ref, *refs):
    *outs, sent_ref, sems = refs
    put_blocks(first, target_ref[...], gate_ref[...], tok_ref, gain_ref, go_ref, sent_ref, outs, sems)


def keep_kernel(block_ref, out_ref):
    out_ref[...] = block_ref[...]


def gelu_parts(value):
    root = 0.7978845608028654
    cubic = root * 0.044715
    square = value * value
    tan = jnp.tanh(value * (root + cubic * square))
    half = 0.5 + 0.5 * tan
    act = value * half
    return act, half + act * (1.0 - tan) * (root + 3.0 * cubic * square)


def shard_order(place):
    second = jnp.where(place < 2, 2 - 2 * place, 7 - 2 * place)
    return [3 - place, second, 3 - second, place]


def expert_work(order, blocks, w_in_ref, w_out_ref, gpre_ref, extra_ref, rows_ref, turned_ref, put):
    capacity = blocks[0].shape[0]
    width, hidden = w_in_ref.shape
    piece_d, piece_f = width // LINE, hidden // LINE
    for j, block in enumerate(blocks):
        rows_ref[j * capacity : (j + 1) * capacity, :] = block[...]
    for j in range(LINE):
        start = pl.multiple_of(order[j] * piece_d, piece_d)
        turned_ref[j * piece_d : (j + 1) * piece_d, :] = rows_ref[:, pl.ds(start, piece_d)].T
    total = jnp.zeros(extra_ref.shape, F32)
    for j in range(LINE):
        part = pl.ds(pl.multiple_of(order[j] * piece_f, piece_f), piece_f)
        delta = rows_ref[:, width:]
        act, slope = gelu_parts(dot(rows_ref[:, :width], w_in_ref[:, part]))
        grad_act = dot(delta, w_out_ref[part, :], ((1,), (1,)))
        products = act * grad_act
        for lane in range(0, piece_f, LANES):
            total += products[:, lane : lane + LANES]
        grad_pre = (grad_act * slope).astype(BF16)
        gpre_ref[:, part] = grad_pre
        put(j, part, dot(turned_ref[...], grad_pre), dot(act.astype(BF16).T, delta))
    total = jnp.sum(total, axis=1, keepdims=True)
    high = total.astype(BF16).astype(F32)
    lane = lax.broadcasted_iota(jnp.int32, extra_ref.shape, 1)
    extra_ref[...] = jnp.where(lane == 0, high, jnp.where(lane == 1, total - high, 0.0)).astype(BF16)


def sooner_kernel(count, groups, place, w_in_ref, w_out_ref, *refs):
    blocks = refs[:count]
    sum_in_ref, sum_out_ref, gpre_ref, extra_ref, rows_ref, turned_ref = refs[count:]
    piece_f = w_in_ref.shape[1] // LINE

    def put(j, part, weight_in, weight_out):
        sum_in_ref[:, part] = weight_in
        sum_out_ref[j * piece_f : (j + 1) * piece_f, :] = weight_out

    order = shard_order(place[0]) if groups == LINE else list(range(LINE))
    expert_work(order, blocks, w_in_ref, w_out_ref, gpre_ref, extra_ref, rows_ref, turned_ref, put)


def next_kernel(count, groups, place, w_in_ref, w_out_ref, old_in_ref, old_out_ref, *refs):
    blocks = refs[:count]
    sum_in_ref, sum_out_ref, gpre_ref, extra_ref, rows_ref, turned_ref = refs[count:]
    piece_f = w_in_ref.shape[1] // LINE

    def put(j, part, weight_in, weight_out):
        chunk = slice(j * piece_f, (j + 1) * piece_f)
        sum_in_ref[:, part] = old_in_ref[:, part] + weight_in
        sum_out_ref[chunk, :] = old_out_ref[chunk, :] + weight_out

    order = shard_order(place[0]) if groups == LINE else list(range(LINE))
    expert_work(order, blocks, w_in_ref, w_out_ref, gpre_ref, extra_ref, rows_ref, turned_ref, put)


def later_kernel(count, groups, place, w_in_ref, w_out_ref, sum_in_ref, sum_out_ref, *refs):
    blocks = refs[:count]
    outs = refs[count : count + LINE]
    gpre_ref, extra_ref, rows_ref, turned_ref = refs[count + LINE :]
    width, hidden = w_in_ref.shape
    piece_d, piece_f = width // LINE, hidden // LINE

    def put(j, part, weight_in, weight_out):
        weight = (sum_out_ref[j * piece_f : (j + 1) * piece_f, :] + weight_out).astype(BF16)
        outs[j][piece_d:, :width] = weight[: piece_f // 2]
        outs[j][piece_d:, width:] = weight[piece_f // 2 :]
        weight = (sum_in_ref[:, part] + weight_in).astype(BF16)
        for i in range(LINE):
            outs[i][:piece_d, part] = weight[i * piece_d : (i + 1) * piece_d]

    order = shard_order(place[0]) if groups == LINE else list(range(LINE))
    expert_work(order, blocks, w_in_ref, w_out_ref, gpre_ref, extra_ref, rows_ref, turned_ref, put)


def back_kernel(capacity, sets, w_in_ref, *refs):
    inputs, outs = refs[: 2 * len(sets)], refs[2 * len(sets) :]
    width = w_in_ref.shape[0]
    for members, gpre_ref, extra_ref in zip(sets, inputs[::2], inputs[1::2]):
        grad = dot(gpre_ref[...], w_in_ref[...], ((1,), (1,))).astype(BF16)
        for i, j in enumerate(members):
            block = slice(i * capacity, (i + 1) * capacity)
            outs[j][:, :width] = grad[block]
            outs[j][:, width:] = extra_ref[block, :]


def finish_kernel(target_ref, gate_ref, tok_ref, gain_ref, go_ref, *refs):
    *blocks, tokens_out, gate_out, back_ref = refs
    rows, capacity = back_ref.shape[0], blocks[0].shape[0]
    for j, block in enumerate(blocks):
        back_ref[j * capacity : (j + 1) * capacity, :] = block[...]
    tok_rows, width = tok_ref.shape
    spots = jnp.broadcast_to(target_ref[...].astype(F32), (8, tok_rows)).T[:, :1].astype(jnp.int32)
    hit = lax.broadcasted_iota(jnp.int32, (tok_rows, rows), 1) == spots
    got = dot(jnp.where(hit, 1.0, 0.0).astype(BF16), back_ref[...])
    sums = got[:, width:].T
    gate_row = gate_ref[...].astype(F32).reshape(1, tok_rows)
    gate_out[...] = ((sums[0:1] + sums[1:2]) / gate_row).astype(BF16).reshape(tok_rows)
    scaled, spread = normalize(tok_ref[...])
    grad = got[:, :width] * gain_ref[...]
    mean = jnp.mean(grad, axis=-1, keepdims=True)
    cross = jnp.mean(grad * scaled, axis=-1, keepdims=True)
    branch = spread * (grad - mean - scaled * cross)
    tokens_out[...] = (go_ref[...].astype(F32) + branch).astype(BF16)


def block_order(sources):
    same = sorted(range(2, sources, 2), key=lambda k: (k.bit_count(), -k))
    return same + list(range(sources - 1, 1, -2)) + [1, 0]


def swap_blocks(blocks, order):
    devices = range(lax.axis_size("space"))
    return [
        lax.ppermute(block, "space", [(i, i ^ k) for i in devices]) if k else block
        for block, k in zip(blocks, order)
    ]


def pass_kernel(middle_ref, inward_ref, third_ref, own_ref, out_ref, sum_ref):
    out_ref[...] = (third_ref[...].astype(F32) + inward_ref[...].astype(F32)).astype(BF16)
    sum_ref[...] = own_ref[...].astype(F32) + middle_ref[...].astype(F32)


def total_kernel(sum_ref, cycle_ref, last_ref, in_ref, out_ref):
    piece_d, half = in_ref.shape[0], out_ref.shape[0] // 2
    width = out_ref.shape[1]
    total = sum_ref[...] + cycle_ref[...].astype(F32) + last_ref[...].astype(F32)
    in_ref[...] = total[:piece_d]
    out_ref[:half, :] = total[piece_d:, :width]
    out_ref[half:, :] = total[piece_d:, width:]


def line_sums(first, second, third, own, width, returned):
    rows, hidden = own.shape
    piece_d = width // LINE
    ahead = 3 * len(returned) // 8
    order = block_order(len(returned))
    inward = lax.ppermute(first, "dp", [(0, 1), (3, 2)])
    middle = lax.ppermute(first, "dp", [(1, 2), (2, 1)])
    cycle = lax.ppermute(second, "dp", [(0, 2), (1, 0), (2, 3), (3, 1)])
    back = swap_blocks(returned[:ahead], order[:ahead])
    third, *back = lax.optimization_barrier((third, *back))
    passed, most = kernel_call(
        pass_kernel,
        "pass",
        1,
        1,
        [jax.ShapeDtypeStruct(own.shape, BF16), jax.ShapeDtypeStruct(own.shape, F32)],
        [vmem] * 4,
    )(middle, inward, third, own)
    last = lax.ppermute(passed, "dp", [(0, 1), (3, 2), (1, 3), (2, 0)])
    cycle, *rest = lax.optimization_barrier((cycle, *returned[ahead:]))
    back += swap_blocks(rest, order[ahead:])
    sums = kernel_call(
        total_kernel,
        "total",
        1,
        1,
        [
            jax.ShapeDtypeStruct((piece_d, hidden), F32),
            jax.ShapeDtypeStruct((2 * (rows - piece_d), width), F32),
        ],
        [vmem] * 3,
    )(most, cycle, last)
    return *sums, back


def body(tokens, gain, w_in, w_out, expert_ids, gate, grad_out):
    sources = lax.axis_size("space")
    groups = lax.axis_size("dp")
    tok_rows, width = tokens.shape
    hidden = w_in.shape[2]
    capacity = ((tok_rows * 5 // 4 + sources - 1) // sources + 7) // 8 * 8
    rows = sources * capacity
    me = lax.axis_index("space").astype(jnp.int32).reshape(1)
    place = lax.axis_index("dp").astype(jnp.int32).reshape(1)
    ids_row = expert_ids.reshape(1, tok_rows)
    gain_row = gain.reshape(1, width)
    weight_in, weight_out = w_in[0], w_out[0]
    shape = jax.ShapeDtypeStruct
    sems = pltpu.SemaphoreType.DMA
    block_place = vmem if capacity % 16 else anywhere
    io_bytes = 2 * (2 * tok_rows * width + 2 * rows * width)

    soon = sources // 2
    blocks = [shape((capacity, 2 * width), BF16)] * soon
    target, *sent = kernel_call(
        functools.partial(place_kernel, sources, capacity),
        "place",
        2 * rows * tok_rows * width,
        io_bytes,
        [shape((1, tok_rows), jnp.int32)] + blocks,
        [smem] * 2 + [hbm] * 5,
        [
            pltpu.VMEM((1, pl.cdiv(tok_rows, LANES) * LANES), jnp.int32),
            pltpu.VMEM((1, tok_rows), jnp.int32),
            pltpu.VMEM((tok_rows,), BF16),
            pltpu.VMEM((tok_rows, width), BF16),
            pltpu.VMEM((1, width), F32),
            pltpu.VMEM((tok_rows, width), BF16),
            pltpu.VMEM((soon * capacity, 2 * width), BF16),
            sems((5,)),
            sems((2, soon)),
        ],
        places=[vmem] + [block_place] * soon,
        vmem_mib=56,
    )(me, place, ids_row, gate, tokens, gain_row, grad_out)
    sent += kernel_call(
        functools.partial(rest_kernel, soon),
        "rest",
        1,
        1,
        blocks,
        [vmem] * 5,
        [pltpu.VMEM((soon * capacity, 2 * width), BF16), sems((2, soon))],
        places=[block_place] * soon,
        vmem_mib=16,
    )(target, gate, tokens, gain_row, grad_out)
    (kept,) = kernel_call(
        keep_kernel,
        "keep",
        1,
        1,
        [shape((capacity, 2 * width), BF16)],
        [vmem],
        vmem_mib=2,
    )(sent[-1])
    arrived = swap_blocks(sent, block_order(sources))
    arrived[-1] = kept

    next_set = list(range(3 * sources // 8, sources // 2))
    late_set = list(range(sources // 2, 3 * sources // 4))
    soon_set = [j for j in range(sources) if j not in next_set + late_set]

    def work(kernel, name, members, outs, *sums):
        count, span = len(members), len(members) * capacity
        return kernel_call(
            functools.partial(kernel, count, groups),
            name,
            8 * span * width * hidden,
            2 * (2 * span * width + 4 * width * hidden + span * hidden),
            outs + [shape((span, hidden), BF16), shape((span, LANES), BF16)],
            [smem] + [vmem] * (2 + len(sums) + count),
            [pltpu.VMEM((span, 2 * width), BF16), pltpu.VMEM((width, span), BF16)],
        )(place, weight_in, weight_out, *sums, *[arrived[j] for j in members])

    sums_shape = [shape((width, hidden), F32), shape((hidden, width), F32)]
    *sums, soon_gpre, soon_extra = work(sooner_kernel, "sooner", soon_set, sums_shape)
    *sums, next_gpre, next_extra = work(next_kernel, "next", next_set, sums_shape, *sums)
    piece = shape((width // LINE + hidden // LINE // 2, hidden), BF16)
    *parts, late_gpre, late_extra = work(later_kernel, "later", late_set, [piece] * LINE, *sums)
    returned = kernel_call(
        functools.partial(back_kernel, capacity, (soon_set, next_set, late_set)),
        "back",
        1,
        1,
        [shape((capacity, width + LANES), BF16)] * sources,
        [vmem] * 7,
    )(weight_in, soon_gpre, soon_extra, next_gpre, next_extra, late_gpre, late_extra)

    if groups == LINE:
        grad_w_in, grad_w_out, back = line_sums(*parts, width, returned)
    else:
        back = swap_blocks(returned, block_order(sources))
        parts_in, parts_out = zip(*[split_piece(part, width, LINE) for part in parts])
        grad_w_in, grad_w_out = (
            lax.psum_scatter(
                jnp.concatenate(part), "dp", scatter_dimension=0, tiled=True
            ).astype(F32)
            for part in (parts_in, parts_out)
        )
    grad_tokens, grad_gate = kernel_call(
        finish_kernel,
        "finish",
        1,
        1,
        [shape((tok_rows, width), BF16), shape((tok_rows,), BF16)],
        [vmem] * (5 + sources),
        [pltpu.VMEM((rows, width + LANES), BF16)],
    )(target, gate, tokens, gain_row, grad_out, *back)
    return (grad_tokens, grad_gate, grad_w_in[None], grad_w_out[None])


def split_piece(piece, width, pieces):
    piece_d = width // pieces
    lower = piece[piece_d:]
    return piece[:piece_d], jnp.concatenate([lower[:, :width], lower[:, width:]])


def solution(mesh):
    placed = (
        P(("space", "dp"), None),
        P(),
        P("space", None, None),
        P("space", None, None),
        P(("space", "dp"), None),
        P(("space", "dp")),
        P(("space", "dp"), None),
    )
    return jax.shard_map(
        body,
        mesh=mesh,
        in_specs=placed,
        out_specs=(
            P(("space", "dp"), None),
            P(("space", "dp")),
            P("space", "dp", None),
            P("space", "dp", None),
        ),
        check_vma=False,
    )
```

```python
import functools

import jax
import jax.numpy as jnp
from jax import lax
from jax.experimental import pallas as pl
from jax.experimental.pallas import tpu as pltpu
from jax.sharding import PartitionSpec as P

epsilon = 1e-05
F32 = jnp.float32
BF16 = jnp.bfloat16
LANES = 128
LINE = 4
MIB = 1024 * 1024

vmem = pl.BlockSpec(memory_space=pltpu.VMEM)
smem = pl.BlockSpec(memory_space=pltpu.SMEM)
hbm = pl.BlockSpec(memory_space=pltpu.HBM)
anywhere = pl.BlockSpec(memory_space=pl.ANY)


def dot(left, right, contract=((1,), (0,))):
    return lax.dot_general(left, right, (contract, ((), ())), preferred_element_type=F32)


def normalize(tokens):
    values = tokens.astype(F32)
    center = values - jnp.mean(values, axis=-1, keepdims=True)
    spread = lax.rsqrt(jnp.mean(center * center, axis=-1, keepdims=True) + epsilon)
    return center * spread, spread


def kernel_call(kernel, name, flops, nbytes, outs, ins, scratch=(), places=None, vmem_mib=24):
    return pl.pallas_call(
        kernel,
        name=name,
        out_shape=outs,
        in_specs=ins,
        out_specs=places or [vmem] * len(outs),
        scratch_shapes=list(scratch),
        compiler_params=pltpu.CompilerParams(vmem_limit_bytes=vmem_mib * MIB),
        cost_estimate=pl.CostEstimate(flops=flops, bytes_accessed=nbytes, transcendentals=0),
    )


def start_copies(pairs, sems):
    copies = [pltpu.make_async_copy(src, dst, sems.at[i]) for i, (src, dst) in enumerate(pairs)]
    for copy in copies:
        copy.start()
    return copies


def put_blocks(first, target, gate, tok_ref, gain_ref, go_ref, sent_ref, outs, sems):
    capacity, width = outs[0].shape[0], tok_ref.shape[1]
    count = len(outs)
    hit = lax.broadcasted_iota(jnp.int32, (count * capacity, target.shape[1]), 0) == (
        target - first * capacity
    )
    gate = gate.astype(F32).reshape(target.shape)
    scaled, _ = normalize(tok_ref[...])
    normed = (scaled * gain_ref[...]).astype(BF16)
    spans = [pl.ds(j * capacity, capacity) for j in range(count)]
    stores = []
    for part, (weight, values) in enumerate(((gate, go_ref[...]), (1.0, normed))):
        columns = pl.ds((1 - part) * width, width)
        sent_ref[:, columns] = dot(jnp.where(hit, weight, 0.0).astype(BF16), values).astype(BF16)
        if capacity % 16:
            for j in range(count):
                outs[j][:, columns] = sent_ref[spans[j], columns]
        else:
            stores += start_copies(
                [(sent_ref.at[spans[j], columns], outs[j].at[:, columns]) for j in range(count)],
                sems.at[part],
            )
    for copy in stores:
        copy.wait()


def place_kernel(
    sources, capacity, me, place, ids_hbm, gate_hbm, tok_hbm, gain_hbm, go_hbm, target_ref, *refs
):
    *outs, wide_ref, ids_ref, gate_ref, tok_ref, gain_ref, go_ref, sent_ref, in_sems, out_sems = refs
    tok_rows = tok_ref.shape[0]
    loads = start_copies(
        [(ids_hbm, ids_ref), (tok_hbm, tok_ref), (gain_hbm, gain_ref), (gate_hbm, gate_ref), (go_hbm, go_ref)],
        in_sems,
    )
    earlier = lax.broadcasted_iota(jnp.int32, (LANES, LANES), 0) < lax.broadcasted_iota(
        jnp.int32, (LANES, LANES), 1
    )
    earlier = jnp.where(earlier, 1.0, 0.0).astype(BF16)
    loads[0].wait()
    chunks = range(0, tok_rows, LANES)
    wide_ref[...] = jnp.full_like(wide_ref, -1)
    wide_ref[:, :tok_rows] = ids_ref[...]
    ids = [wide_ref[:, c : c + LANES] for c in chunks]
    expert = lax.broadcasted_iota(jnp.int32, (sources, LANES), 0)
    onehots = [jnp.where(expert == chunk, 1.0, 0.0) for chunk in ids]
    within = dot(jnp.concatenate(onehots).astype(BF16), earlier)
    base = jnp.zeros((sources, 1), F32)
    for i, (c, chunk, onehot) in enumerate(zip(chunks, ids, onehots)):
        before = within[i * sources : (i + 1) * sources] + base
        base += jnp.sum(onehot, axis=1, keepdims=True)
        rank = jnp.sum(before * onehot, axis=0, keepdims=True).astype(jnp.int32)
        away = jnp.bitwise_xor(chunk, me[0])
        block = jnp.zeros_like(away)
        for j, k in enumerate(block_order(sources)):
            block = jnp.where(away == k, j, block)
        end = min(LANES, tok_rows - c)
        target = jnp.where(rank < capacity, block * capacity + rank, -1)
        target_ref[:, c : c + end] = target[:, :end]
    for copy in loads[1:]:
        copy.wait()
    put_blocks(0, target_ref[...], gate_ref[...], tok_ref, gain_ref, go_ref, sent_ref, outs, out_sems)


def rest_kernel(first, target_ref, gate_ref, tok_ref, gain_ref, go_ref, *refs):
    *outs, sent_ref, sems = refs
    put_blocks(first, target_ref[...], gate_ref[...], tok_ref, gain_ref, go_ref, sent_ref, outs, sems)


def keep_kernel(block_ref, out_ref):
    out_ref[...] = block_ref[...]


def gelu_parts(value):
    root = 0.7978845608028654
    cubic = root * 0.044715
    square = value * value
    tan = jnp.tanh(value * (root + cubic * square))
    half = 0.5 + 0.5 * tan
    act = value * half
    return act, half + act * (1.0 - tan) * (root + 3.0 * cubic * square)


def shard_order(place):
    second = jnp.where(place < 2, 2 - 2 * place, 7 - 2 * place)
    return [3 - place, second, 3 - second, place]


def expert_work(order, blocks, w_in_ref, w_out_ref, gpre_ref, extra_ref, rows_ref, turned_ref, put):
    capacity = blocks[0].shape[0]
    width, hidden = w_in_ref.shape
    piece_d, piece_f = width // LINE, hidden // LINE
    for j, block in enumerate(blocks):
        rows_ref[j * capacity : (j + 1) * capacity, :] = block[...]
    for j in range(LINE):
        start = pl.multiple_of(order[j] * piece_d, piece_d)
        turned_ref[j * piece_d : (j + 1) * piece_d, :] = rows_ref[:, pl.ds(start, piece_d)].T
    total = jnp.zeros(extra_ref.shape, F32)
    for j in range(LINE):
        part = pl.ds(pl.multiple_of(order[j] * piece_f, piece_f), piece_f)
        delta = rows_ref[:, width:]
        act, slope = gelu_parts(dot(rows_ref[:, :width], w_in_ref[:, part]))
        grad_act = dot(delta, w_out_ref[part, :], ((1,), (1,)))
        products = act * grad_act
        for lane in range(0, piece_f, LANES):
            total += products[:, lane : lane + LANES]
        grad_pre = (grad_act * slope).astype(BF16)
        gpre_ref[:, part] = grad_pre
        put(j, part, dot(turned_ref[...], grad_pre), dot(act.astype(BF16).T, delta))
    total = jnp.sum(total, axis=1, keepdims=True)
    high = total.astype(BF16).astype(F32)
    lane = lax.broadcasted_iota(jnp.int32, extra_ref.shape, 1)
    extra_ref[...] = jnp.where(lane == 0, high, jnp.where(lane == 1, total - high, 0.0)).astype(BF16)


def sooner_kernel(count, groups, place, w_in_ref, w_out_ref, *refs):
    blocks = refs[:count]
    sum_in_ref, sum_out_ref, gpre_ref, extra_ref, rows_ref, turned_ref = refs[count:]
    piece_f = w_in_ref.shape[1] // LINE

    def put(j, part, weight_in, weight_out):
        sum_in_ref[:, part] = weight_in
        sum_out_ref[j * piece_f : (j + 1) * piece_f, :] = weight_out

    order = shard_order(place[0]) if groups == LINE else list(range(LINE))
    expert_work(order, blocks, w_in_ref, w_out_ref, gpre_ref, extra_ref, rows_ref, turned_ref, put)


def next_kernel(count, groups, place, w_in_ref, w_out_ref, old_in_ref, old_out_ref, *refs):
    blocks = refs[:count]
    sum_in_ref, sum_out_ref, gpre_ref, extra_ref, rows_ref, turned_ref = refs[count:]
    piece_f = w_in_ref.shape[1] // LINE

    def put(j, part, weight_in, weight_out):
        chunk = slice(j * piece_f, (j + 1) * piece_f)
        sum_in_ref[:, part] = old_in_ref[:, part] + weight_in
        sum_out_ref[chunk, :] = old_out_ref[chunk, :] + weight_out

    order = shard_order(place[0]) if groups == LINE else list(range(LINE))
    expert_work(order, blocks, w_in_ref, w_out_ref, gpre_ref, extra_ref, rows_ref, turned_ref, put)


def later_kernel(count, groups, place, w_in_ref, w_out_ref, sum_in_ref, sum_out_ref, *refs):
    blocks = refs[:count]
    outs = refs[count : count + LINE]
    gpre_ref, extra_ref, rows_ref, turned_ref = refs[count + LINE :]
    width, hidden = w_in_ref.shape
    piece_d, piece_f = width // LINE, hidden // LINE

    def put(j, part, weight_in, weight_out):
        weight = (sum_out_ref[j * piece_f : (j + 1) * piece_f, :] + weight_out).astype(BF16)
        outs[j][piece_d:, :width] = weight[: piece_f // 2]
        outs[j][piece_d:, width:] = weight[piece_f // 2 :]
        weight = (sum_in_ref[:, part] + weight_in).astype(BF16)
        for i in range(LINE):
            outs[i][:piece_d, part] = weight[i * piece_d : (i + 1) * piece_d]

    order = shard_order(place[0]) if groups == LINE else list(range(LINE))
    expert_work(order, blocks, w_in_ref, w_out_ref, gpre_ref, extra_ref, rows_ref, turned_ref, put)


def back_kernel(capacity, sets, w_in_ref, *refs):
    inputs, outs = refs[: 2 * len(sets)], refs[2 * len(sets) :]
    width = w_in_ref.shape[0]
    for members, gpre_ref, extra_ref in zip(sets, inputs[::2], inputs[1::2]):
        grad = dot(gpre_ref[...], w_in_ref[...], ((1,), (1,))).astype(BF16)
        for i, j in enumerate(members):
            block = slice(i * capacity, (i + 1) * capacity)
            outs[j][:, :width] = grad[block]
            outs[j][:, width:] = extra_ref[block, :]


def finish_kernel(target_ref, gate_ref, tok_ref, gain_ref, go_ref, *refs):
    *blocks, tokens_out, gate_out, back_ref = refs
    rows, capacity = back_ref.shape[0], blocks[0].shape[0]
    for j, block in enumerate(blocks):
        back_ref[j * capacity : (j + 1) * capacity, :] = block[...]
    tok_rows, width = tok_ref.shape
    spots = jnp.broadcast_to(target_ref[...].astype(F32), (8, tok_rows)).T[:, :1].astype(jnp.int32)
    hit = lax.broadcasted_iota(jnp.int32, (tok_rows, rows), 1) == spots
    got = dot(jnp.where(hit, 1.0, 0.0).astype(BF16), back_ref[...])
    sums = got[:, width:].T
    gate_row = gate_ref[...].astype(F32).reshape(1, tok_rows)
    gate_out[...] = ((sums[0:1] + sums[1:2]) / gate_row).astype(BF16).reshape(tok_rows)
    scaled, spread = normalize(tok_ref[...])
    grad = got[:, :width] * gain_ref[...]
    mean = jnp.mean(grad, axis=-1, keepdims=True)
    cross = jnp.mean(grad * scaled, axis=-1, keepdims=True)
    branch = spread * (grad - mean - scaled * cross)
    tokens_out[...] = (go_ref[...].astype(F32) + branch).astype(BF16)


def block_order(sources):
    same = sorted(range(2, sources, 2), key=lambda k: (k.bit_count(), -k))
    return same + list(range(sources - 1, 1, -2)) + [1, 0]


def swap_blocks(blocks, order):
    devices = range(lax.axis_size("space"))
    return [
        lax.ppermute(block, "space", [(i, i ^ k) for i in devices]) if k else block
        for block, k in zip(blocks, order)
    ]


def pass_kernel(middle_ref, inward_ref, third_ref, own_ref, out_ref, sum_ref):
    out_ref[...] = (third_ref[...].astype(F32) + inward_ref[...].astype(F32)).astype(BF16)
    sum_ref[...] = own_ref[...].astype(F32) + middle_ref[...].astype(F32)


def total_kernel(sum_ref, cycle_ref, last_ref, in_ref, out_ref):
    piece_d, half = in_ref.shape[0], out_ref.shape[0] // 2
    width = out_ref.shape[1]
    total = sum_ref[...] + cycle_ref[...].astype(F32) + last_ref[...].astype(F32)
    in_ref[...] = total[:piece_d]
    out_ref[:half, :] = total[piece_d:, :width]
    out_ref[half:, :] = total[piece_d:, width:]


def line_sums(first, second, third, own, width, returned):
    rows, hidden = own.shape
    piece_d = width // LINE
    ahead = len(returned) // 4
    order = block_order(len(returned))
    inward = lax.ppermute(first, "dp", [(0, 1), (3, 2)])
    middle = lax.ppermute(first, "dp", [(1, 2), (2, 1)])
    back = swap_blocks(returned[:ahead], order[:ahead])
    second, back[0] = lax.optimization_barrier((second, back[0]))
    cycle = lax.ppermute(second, "dp", [(0, 2), (1, 0), (2, 3), (3, 1)])
    third, *back = lax.optimization_barrier((third, *back))
    passed, most = kernel_call(
        pass_kernel,
        "pass",
        1,
        1,
        [jax.ShapeDtypeStruct(own.shape, BF16), jax.ShapeDtypeStruct(own.shape, F32)],
        [vmem] * 4,
    )(middle, inward, third, own)
    passed, *rest = lax.optimization_barrier((passed, *returned[ahead:]))
    last = lax.ppermute(passed, "dp", [(0, 1), (3, 2), (1, 3), (2, 0)])
    back += swap_blocks(rest, order[ahead:])
    sums = kernel_call(
        total_kernel,
        "total",
        1,
        1,
        [
            jax.ShapeDtypeStruct((piece_d, hidden), F32),
            jax.ShapeDtypeStruct((2 * (rows - piece_d), width), F32),
        ],
        [vmem] * 3,
    )(most, cycle, last)
    return *sums, back


def body(tokens, gain, w_in, w_out, expert_ids, gate, grad_out):
    sources = lax.axis_size("space")
    groups = lax.axis_size("dp")
    tok_rows, width = tokens.shape
    hidden = w_in.shape[2]
    capacity = ((tok_rows * 5 // 4 + sources - 1) // sources + 7) // 8 * 8
    rows = sources * capacity
    me = lax.axis_index("space").astype(jnp.int32).reshape(1)
    place = lax.axis_index("dp").astype(jnp.int32).reshape(1)
    ids_row = expert_ids.reshape(1, tok_rows)
    gain_row = gain.reshape(1, width)
    weight_in, weight_out = w_in[0], w_out[0]
    shape = jax.ShapeDtypeStruct
    sems = pltpu.SemaphoreType.DMA
    block_place = vmem if capacity % 16 else anywhere
    io_bytes = 2 * (2 * tok_rows * width + 2 * rows * width)

    soon = sources // 2
    blocks = [shape((capacity, 2 * width), BF16)] * soon
    target, *sent = kernel_call(
        functools.partial(place_kernel, sources, capacity),
        "place",
        2 * rows * tok_rows * width,
        io_bytes,
        [shape((1, tok_rows), jnp.int32)] + blocks,
        [smem] * 2 + [hbm] * 5,
        [
            pltpu.VMEM((1, pl.cdiv(tok_rows, LANES) * LANES), jnp.int32),
            pltpu.VMEM((1, tok_rows), jnp.int32),
            pltpu.VMEM((tok_rows,), BF16),
            pltpu.VMEM((tok_rows, width), BF16),
            pltpu.VMEM((1, width), F32),
            pltpu.VMEM((tok_rows, width), BF16),
            pltpu.VMEM((soon * capacity, 2 * width), BF16),
            sems((5,)),
            sems((2, soon)),
        ],
        places=[vmem] + [block_place] * soon,
        vmem_mib=56,
    )(me, place, ids_row, gate, tokens, gain_row, grad_out)
    sent += kernel_call(
        functools.partial(rest_kernel, soon),
        "rest",
        1,
        1,
        blocks,
        [vmem] * 5,
        [pltpu.VMEM((soon * capacity, 2 * width), BF16), sems((2, soon))],
        places=[block_place] * soon,
        vmem_mib=16,
    )(target, gate, tokens, gain_row, grad_out)
    (kept,) = kernel_call(
        keep_kernel,
        "keep",
        1,
        1,
        [shape((capacity, 2 * width), BF16)],
        [vmem],
        vmem_mib=2,
    )(sent[-1])
    arrived = swap_blocks(sent, block_order(sources))
    arrived[-1] = kept

    next_set = list(range(3 * sources // 8, sources // 2))
    late_set = list(range(sources // 2, 3 * sources // 4))
    soon_set = [j for j in range(sources) if j not in next_set + late_set]

    def work(kernel, name, members, outs, *sums):
        count, span = len(members), len(members) * capacity
        return kernel_call(
            functools.partial(kernel, count, groups),
            name,
            8 * span * width * hidden,
            2 * (2 * span * width + 4 * width * hidden + span * hidden),
            outs + [shape((span, hidden), BF16), shape((span, LANES), BF16)],
            [smem] + [vmem] * (2 + len(sums) + count),
            [pltpu.VMEM((span, 2 * width), BF16), pltpu.VMEM((width, span), BF16)],
        )(place, weight_in, weight_out, *sums, *[arrived[j] for j in members])

    sums_shape = [shape((width, hidden), F32), shape((hidden, width), F32)]
    *sums, soon_gpre, soon_extra = work(sooner_kernel, "sooner", soon_set, sums_shape)
    *sums, next_gpre, next_extra = work(next_kernel, "next", next_set, sums_shape, *sums)
    piece = shape((width // LINE + hidden // LINE // 2, hidden), BF16)
    *parts, late_gpre, late_extra = work(later_kernel, "later", late_set, [piece] * LINE, *sums)
    returned = kernel_call(
        functools.partial(back_kernel, capacity, (soon_set, next_set, late_set)),
        "back",
        1,
        1,
        [shape((capacity, width + LANES), BF16)] * sources,
        [vmem] * 7,
    )(weight_in, soon_gpre, soon_extra, next_gpre, next_extra, late_gpre, late_extra)

    if groups == LINE:
        grad_w_in, grad_w_out, back = line_sums(*parts, width, returned)
    else:
        back = swap_blocks(returned, block_order(sources))
        parts_in, parts_out = zip(*[split_piece(part, width, LINE) for part in parts])
        grad_w_in, grad_w_out = (
            lax.psum_scatter(
                jnp.concatenate(part), "dp", scatter_dimension=0, tiled=True
            ).astype(F32)
            for part in (parts_in, parts_out)
        )
    grad_tokens, grad_gate = kernel_call(
        finish_kernel,
        "finish",
        1,
        1,
        [shape((tok_rows, width), BF16), shape((tok_rows,), BF16)],
        [vmem] * (5 + sources),
        [pltpu.VMEM((rows, width + LANES), BF16)],
    )(target, gate, tokens, gain_row, grad_out, *back)
    return (grad_tokens, grad_gate, grad_w_in[None], grad_w_out[None])


def split_piece(piece, width, pieces):
    piece_d = width // pieces
    lower = piece[piece_d:]
    return piece[:piece_d], jnp.concatenate([lower[:, :width], lower[:, width:]])


def solution(mesh):
    placed = (
        P(("space", "dp"), None),
        P(),
        P("space", None, None),
        P("space", None, None),
        P(("space", "dp"), None),
        P(("space", "dp")),
        P(("space", "dp"), None),
    )
    return jax.shard_map(
        body,
        mesh=mesh,
        in_specs=placed,
        out_specs=(
            P(("space", "dp"), None),
            P(("space", "dp")),
            P("space", "dp", None),
            P("space", "dp", None),
        ),
        check_vma=False,
    )
```

```python
import functools

import jax
import jax.numpy as jnp
from jax import lax
from jax.experimental import pallas as pl
from jax.experimental.pallas import tpu as pltpu
from jax.sharding import PartitionSpec as P

epsilon = 1e-05
F32 = jnp.float32
BF16 = jnp.bfloat16
LANES = 128
LINE = 4
MIB = 1024 * 1024

vmem = pl.BlockSpec(memory_space=pltpu.VMEM)
smem = pl.BlockSpec(memory_space=pltpu.SMEM)
hbm = pl.BlockSpec(memory_space=pltpu.HBM)
anywhere = pl.BlockSpec(memory_space=pl.ANY)


def dot(left, right, contract=((1,), (0,))):
    return lax.dot_general(left, right, (contract, ((), ())), preferred_element_type=F32)


def normalize(tokens):
    values = tokens.astype(F32)
    center = values - jnp.mean(values, axis=-1, keepdims=True)
    spread = lax.rsqrt(jnp.mean(center * center, axis=-1, keepdims=True) + epsilon)
    return center * spread, spread


def kernel_call(kernel, name, flops, nbytes, outs, ins, scratch=(), places=None, vmem_mib=24):
    return pl.pallas_call(
        kernel,
        name=name,
        out_shape=outs,
        in_specs=ins,
        out_specs=places or [vmem] * len(outs),
        scratch_shapes=list(scratch),
        compiler_params=pltpu.CompilerParams(vmem_limit_bytes=vmem_mib * MIB),
        cost_estimate=pl.CostEstimate(flops=flops, bytes_accessed=nbytes, transcendentals=0),
    )


def start_copies(pairs, sems):
    copies = [pltpu.make_async_copy(src, dst, sems.at[i]) for i, (src, dst) in enumerate(pairs)]
    for copy in copies:
        copy.start()
    return copies


def put_blocks(first, target, gate, tok_ref, gain_ref, go_ref, sent_ref, outs, sems):
    capacity, width = outs[0].shape[0], tok_ref.shape[1]
    count = len(outs)
    hit = lax.broadcasted_iota(jnp.int32, (count * capacity, target.shape[1]), 0) == (
        target - first * capacity
    )
    gate = gate.astype(F32).reshape(target.shape)
    scaled, _ = normalize(tok_ref[...])
    normed = (scaled * gain_ref[...]).astype(BF16)
    spans = [pl.ds(j * capacity, capacity) for j in range(count)]
    stores = []
    for part, (weight, values) in enumerate(((gate, go_ref[...]), (1.0, normed))):
        columns = pl.ds((1 - part) * width, width)
        sent_ref[:, columns] = dot(jnp.where(hit, weight, 0.0).astype(BF16), values).astype(BF16)
        if capacity % 16:
            for j in range(count):
                outs[j][:, columns] = sent_ref[spans[j], columns]
        else:
            stores += start_copies(
                [(sent_ref.at[spans[j], columns], outs[j].at[:, columns]) for j in range(count)],
                sems.at[part],
            )
    for copy in stores:
        copy.wait()


def place_kernel(
    sources, capacity, me, place, ids_hbm, gate_hbm, tok_hbm, gain_hbm, go_hbm, target_ref, *refs
):
    *outs, wide_ref, ids_ref, gate_ref, tok_ref, gain_ref, go_ref, sent_ref, in_sems, out_sems = refs
    tok_rows = tok_ref.shape[0]
    loads = start_copies(
        [(ids_hbm, ids_ref), (tok_hbm, tok_ref), (gain_hbm, gain_ref), (gate_hbm, gate_ref), (go_hbm, go_ref)],
        in_sems,
    )
    earlier = lax.broadcasted_iota(jnp.int32, (LANES, LANES), 0) < lax.broadcasted_iota(
        jnp.int32, (LANES, LANES), 1
    )
    earlier = jnp.where(earlier, 1.0, 0.0).astype(BF16)
    loads[0].wait()
    chunks = range(0, tok_rows, LANES)
    wide_ref[...] = jnp.full_like(wide_ref, -1)
    wide_ref[:, :tok_rows] = ids_ref[...]
    ids = [wide_ref[:, c : c + LANES] for c in chunks]
    expert = lax.broadcasted_iota(jnp.int32, (sources, LANES), 0)
    onehots = [jnp.where(expert == chunk, 1.0, 0.0) for chunk in ids]
    within = dot(jnp.concatenate(onehots).astype(BF16), earlier)
    base = jnp.zeros((sources, 1), F32)
    for i, (c, chunk, onehot) in enumerate(zip(chunks, ids, onehots)):
        before = within[i * sources : (i + 1) * sources] + base
        base += jnp.sum(onehot, axis=1, keepdims=True)
        rank = jnp.sum(before * onehot, axis=0, keepdims=True).astype(jnp.int32)
        away = jnp.bitwise_xor(chunk, me[0])
        block = jnp.zeros_like(away)
        for j, k in enumerate(block_order(sources)):
            block = jnp.where(away == k, j, block)
        end = min(LANES, tok_rows - c)
        target = jnp.where(rank < capacity, block * capacity + rank, -1)
        target_ref[:, c : c + end] = target[:, :end]
    for copy in loads[1:]:
        copy.wait()
    put_blocks(0, target_ref[...], gate_ref[...], tok_ref, gain_ref, go_ref, sent_ref, outs, out_sems)


def rest_kernel(first, target_ref, gate_ref, tok_ref, gain_ref, go_ref, *refs):
    *outs, sent_ref, sems = refs
    put_blocks(first, target_ref[...], gate_ref[...], tok_ref, gain_ref, go_ref, sent_ref, outs, sems)


def keep_kernel(block_ref, out_ref):
    out_ref[...] = block_ref[...]


def gelu_parts(value):
    root = 0.7978845608028654
    cubic = root * 0.044715
    square = value * value
    tan = jnp.tanh(value * (root + cubic * square))
    half = 0.5 + 0.5 * tan
    act = value * half
    return act, half + act * (1.0 - tan) * (root + 3.0 * cubic * square)


def shard_order(place):
    second = jnp.where(place < 2, 2 - 2 * place, 7 - 2 * place)
    return [3 - place, second, 3 - second, place]


def expert_work(order, blocks, w_in_ref, w_out_ref, gpre_ref, extra_ref, rows_ref, turned_ref, put):
    capacity = blocks[0].shape[0]
    width, hidden = w_in_ref.shape
    piece_d, piece_f = width // LINE, hidden // LINE
    for j, block in enumerate(blocks):
        rows_ref[j * capacity : (j + 1) * capacity, :] = block[...]
    for j in range(LINE):
        start = pl.multiple_of(order[j] * piece_d, piece_d)
        turned_ref[j * piece_d : (j + 1) * piece_d, :] = rows_ref[:, pl.ds(start, piece_d)].T
    total = jnp.zeros(extra_ref.shape, F32)
    for j in range(LINE):
        part = pl.ds(pl.multiple_of(order[j] * piece_f, piece_f), piece_f)
        delta = rows_ref[:, width:]
        act, slope = gelu_parts(dot(rows_ref[:, :width], w_in_ref[:, part]))
        grad_act = dot(delta, w_out_ref[part, :], ((1,), (1,)))
        products = act * grad_act
        for lane in range(0, piece_f, LANES):
            total += products[:, lane : lane + LANES]
        grad_pre = (grad_act * slope).astype(BF16)
        gpre_ref[:, part] = grad_pre
        put(j, part, dot(turned_ref[...], grad_pre), dot(act.astype(BF16).T, delta))
    total = jnp.sum(total, axis=1, keepdims=True)
    high = total.astype(BF16).astype(F32)
    lane = lax.broadcasted_iota(jnp.int32, extra_ref.shape, 1)
    extra_ref[...] = jnp.where(lane == 0, high, jnp.where(lane == 1, total - high, 0.0)).astype(BF16)


def sooner_kernel(count, groups, place, w_in_ref, w_out_ref, *refs):
    blocks = refs[:count]
    sum_in_ref, sum_out_ref, gpre_ref, extra_ref, rows_ref, turned_ref = refs[count:]
    piece_f = w_in_ref.shape[1] // LINE

    def put(j, part, weight_in, weight_out):
        sum_in_ref[:, part] = weight_in
        sum_out_ref[j * piece_f : (j + 1) * piece_f, :] = weight_out

    order = shard_order(place[0]) if groups == LINE else list(range(LINE))
    expert_work(order, blocks, w_in_ref, w_out_ref, gpre_ref, extra_ref, rows_ref, turned_ref, put)


def next_kernel(count, groups, place, w_in_ref, w_out_ref, old_in_ref, old_out_ref, *refs):
    blocks = refs[:count]
    sum_in_ref, sum_out_ref, gpre_ref, extra_ref, rows_ref, turned_ref = refs[count:]
    piece_f = w_in_ref.shape[1] // LINE

    def put(j, part, weight_in, weight_out):
        chunk = slice(j * piece_f, (j + 1) * piece_f)
        sum_in_ref[:, part] = old_in_ref[:, part] + weight_in
        sum_out_ref[chunk, :] = old_out_ref[chunk, :] + weight_out

    order = shard_order(place[0]) if groups == LINE else list(range(LINE))
    expert_work(order, blocks, w_in_ref, w_out_ref, gpre_ref, extra_ref, rows_ref, turned_ref, put)


def later_kernel(count, groups, place, w_in_ref, w_out_ref, sum_in_ref, sum_out_ref, *refs):
    blocks = refs[:count]
    outs = refs[count : count + LINE]
    upper_ref, lower_ref, gpre_ref, extra_ref, rows_ref, turned_ref = refs[count + LINE :]
    width, hidden = w_in_ref.shape
    piece_d, piece_f = width // LINE, hidden // LINE

    def put(j, part, weight_in, weight_out):
        weight = (sum_out_ref[j * piece_f : (j + 1) * piece_f, :] + weight_out).astype(BF16)
        outs[j][piece_d:, :width] = weight[: piece_f // 2]
        outs[j][piece_d:, width:] = weight[piece_f // 2 :]
        weight = (sum_in_ref[:, part] + weight_in).astype(BF16)
        for i in range(LINE):
            outs[i][:piece_d, part] = weight[i * piece_d : (i + 1) * piece_d]

    order = shard_order(place[0]) if groups == LINE else list(range(LINE))
    expert_work(order, blocks, w_in_ref, w_out_ref, gpre_ref, extra_ref, rows_ref, turned_ref, put)
    cut = upper_ref.shape[0]
    upper_ref[...] = outs[0][:cut, :]
    lower_ref[...] = outs[0][cut:, :]


def back_kernel(capacity, sets, w_in_ref, *refs):
    inputs, outs = refs[: 2 * len(sets)], refs[2 * len(sets) :]
    width = w_in_ref.shape[0]
    for members, gpre_ref, extra_ref in zip(sets, inputs[::2], inputs[1::2]):
        grad = dot(gpre_ref[...], w_in_ref[...], ((1,), (1,))).astype(BF16)
        for i, j in enumerate(members):
            block = slice(i * capacity, (i + 1) * capacity)
            outs[j][:, :width] = grad[block]
            outs[j][:, width:] = extra_ref[block, :]


def finish_kernel(target_ref, gate_ref, tok_ref, gain_ref, go_ref, *refs):
    *blocks, tokens_out, gate_out, back_ref = refs
    rows, capacity = back_ref.shape[0], blocks[0].shape[0]
    for j, block in enumerate(blocks):
        back_ref[j * capacity : (j + 1) * capacity, :] = block[...]
    tok_rows, width = tok_ref.shape
    spots = jnp.broadcast_to(target_ref[...].astype(F32), (8, tok_rows)).T[:, :1].astype(jnp.int32)
    hit = lax.broadcasted_iota(jnp.int32, (tok_rows, rows), 1) == spots
    got = dot(jnp.where(hit, 1.0, 0.0).astype(BF16), back_ref[...])
    sums = got[:, width:].T
    gate_row = gate_ref[...].astype(F32).reshape(1, tok_rows)
    gate_out[...] = ((sums[0:1] + sums[1:2]) / gate_row).astype(BF16).reshape(tok_rows)
    scaled, spread = normalize(tok_ref[...])
    grad = got[:, :width] * gain_ref[...]
    mean = jnp.mean(grad, axis=-1, keepdims=True)
    cross = jnp.mean(grad * scaled, axis=-1, keepdims=True)
    branch = spread * (grad - mean - scaled * cross)
    tokens_out[...] = (go_ref[...].astype(F32) + branch).astype(BF16)


def block_order(sources):
    same = sorted(range(2, sources, 2), key=lambda k: (k.bit_count(), -k))
    return same + list(range(sources - 1, 1, -2)) + [1, 0]


def swap_blocks(blocks, order):
    devices = range(lax.axis_size("space"))
    return [
        lax.ppermute(block, "space", [(i, i ^ k) for i in devices]) if k else block
        for block, k in zip(blocks, order)
    ]


def pass_kernel(above_ref, inward_ref, third_ref, own_ref, out_ref, sum_ref):
    cut = above_ref.shape[0]
    out_ref[...] = (third_ref[...].astype(F32) + inward_ref[...].astype(F32)).astype(BF16)
    sum_ref[:cut, :] = own_ref[:cut, :].astype(F32) + above_ref[...].astype(F32)
    sum_ref[cut:, :] = own_ref[cut:, :].astype(F32)


def total_kernel(sum_ref, below_ref, cycle_ref, last_ref, in_ref, out_ref):
    piece_d, half = in_ref.shape[0], out_ref.shape[0] // 2
    width = out_ref.shape[1]
    cut = sum_ref.shape[0] - below_ref.shape[0]
    total = sum_ref[...] + cycle_ref[...].astype(F32) + last_ref[...].astype(F32)
    total = jnp.concatenate([total[:cut], total[cut:] + below_ref[...].astype(F32)])
    in_ref[...] = total[:piece_d]
    out_ref[:half, :] = total[piece_d:, :width]
    out_ref[half:, :] = total[piece_d:, width:]


def line_sums(first, second, third, own, upper, lower, width, returned):
    rows, hidden = own.shape
    piece_d = width // LINE
    ahead = len(returned) // 4
    order = block_order(len(returned))
    inward = lax.ppermute(first, "dp", [(0, 1), (3, 2)])
    above = lax.ppermute(upper, "dp", [(1, 2), (2, 1)])
    below = lax.ppermute(lower, "dp", [(1, 2), (2, 1)])
    back = swap_blocks(returned[:ahead], order[:ahead])
    second, back[0] = lax.optimization_barrier((second, back[0]))
    cycle = lax.ppermute(second, "dp", [(0, 2), (1, 0), (2, 3), (3, 1)])
    third, *back = lax.optimization_barrier((third, *back))
    shape = functools.partial(jax.ShapeDtypeStruct, own.shape)
    passed, most = kernel_call(
        pass_kernel, "pass", 1, 1, [shape(BF16), shape(F32)], [vmem] * 4
    )(above, inward, third, own)
    passed, *rest = lax.optimization_barrier((passed, *returned[ahead:]))
    last = lax.ppermute(passed, "dp", [(0, 1), (3, 2), (1, 3), (2, 0)])
    back += swap_blocks(rest, order[ahead:])
    sums = kernel_call(
        total_kernel,
        "total",
        1,
        1,
        [
            jax.ShapeDtypeStruct((piece_d, hidden), F32),
            jax.ShapeDtypeStruct((2 * (rows - piece_d), width), F32),
        ],
        [vmem] * 4,
    )(most, below, cycle, last)
    return *sums, back


def body(tokens, gain, w_in, w_out, expert_ids, gate, grad_out):
    sources = lax.axis_size("space")
    groups = lax.axis_size("dp")
    tok_rows, width = tokens.shape
    hidden = w_in.shape[2]
    capacity = ((tok_rows * 5 // 4 + sources - 1) // sources + 7) // 8 * 8
    rows = sources * capacity
    me = lax.axis_index("space").astype(jnp.int32).reshape(1)
    place = lax.axis_index("dp").astype(jnp.int32).reshape(1)
    ids_row = expert_ids.reshape(1, tok_rows)
    gain_row = gain.reshape(1, width)
    weight_in, weight_out = w_in[0], w_out[0]
    shape = jax.ShapeDtypeStruct
    sems = pltpu.SemaphoreType.DMA
    block_place = vmem if capacity % 16 else anywhere
    io_bytes = 2 * (2 * tok_rows * width + 2 * rows * width)

    soon = sources // 2
    blocks = [shape((capacity, 2 * width), BF16)] * soon
    target, *sent = kernel_call(
        functools.partial(place_kernel, sources, capacity),
        "place",
        2 * rows * tok_rows * width,
        io_bytes,
        [shape((1, tok_rows), jnp.int32)] + blocks,
        [smem] * 2 + [hbm] * 5,
        [
            pltpu.VMEM((1, pl.cdiv(tok_rows, LANES) * LANES), jnp.int32),
            pltpu.VMEM((1, tok_rows), jnp.int32),
            pltpu.VMEM((tok_rows,), BF16),
            pltpu.VMEM((tok_rows, width), BF16),
            pltpu.VMEM((1, width), F32),
            pltpu.VMEM((tok_rows, width), BF16),
            pltpu.VMEM((soon * capacity, 2 * width), BF16),
            sems((5,)),
            sems((2, soon)),
        ],
        places=[vmem] + [block_place] * soon,
        vmem_mib=56,
    )(me, place, ids_row, gate, tokens, gain_row, grad_out)
    sent += kernel_call(
        functools.partial(rest_kernel, soon),
        "rest",
        1,
        1,
        blocks,
        [vmem] * 5,
        [pltpu.VMEM((soon * capacity, 2 * width), BF16), sems((2, soon))],
        places=[block_place] * soon,
        vmem_mib=16,
    )(target, gate, tokens, gain_row, grad_out)
    (kept,) = kernel_call(
        keep_kernel,
        "keep",
        1,
        1,
        [shape((capacity, 2 * width), BF16)],
        [vmem],
        vmem_mib=2,
    )(sent[-1])
    arrived = swap_blocks(sent, block_order(sources))
    arrived[-1] = kept

    next_set = list(range(3 * sources // 8, sources // 2))
    late_set = list(range(sources // 2, 3 * sources // 4))
    soon_set = [j for j in range(sources) if j not in next_set + late_set]

    def work(kernel, name, members, outs, *sums):
        count, span = len(members), len(members) * capacity
        return kernel_call(
            functools.partial(kernel, count, groups),
            name,
            8 * span * width * hidden,
            2 * (2 * span * width + 4 * width * hidden + span * hidden),
            outs + [shape((span, hidden), BF16), shape((span, LANES), BF16)],
            [smem] + [vmem] * (2 + len(sums) + count),
            [pltpu.VMEM((span, 2 * width), BF16), pltpu.VMEM((width, span), BF16)],
        )(place, weight_in, weight_out, *sums, *[arrived[j] for j in members])

    sums_shape = [shape((width, hidden), F32), shape((hidden, width), F32)]
    *sums, soon_gpre, soon_extra = work(sooner_kernel, "sooner", soon_set, sums_shape)
    *sums, next_gpre, next_extra = work(next_kernel, "next", next_set, sums_shape, *sums)
    piece = shape((width // LINE + hidden // LINE // 2, hidden), BF16)
    cut = 3 * piece.shape[0] // 4
    cut_pieces = [shape((cut, hidden), BF16), shape((piece.shape[0] - cut, hidden), BF16)]
    *parts, late_gpre, late_extra = work(
        later_kernel, "later", late_set, [piece] * LINE + cut_pieces, *sums
    )
    returned = kernel_call(
        functools.partial(back_kernel, capacity, (soon_set, next_set, late_set)),
        "back",
        1,
        1,
        [shape((capacity, width + LANES), BF16)] * sources,
        [vmem] * 7,
    )(weight_in, soon_gpre, soon_extra, next_gpre, next_extra, late_gpre, late_extra)

    if groups == LINE:
        grad_w_in, grad_w_out, back = line_sums(*parts, width, returned)
    else:
        back = swap_blocks(returned, block_order(sources))
        parts_in, parts_out = zip(*[split_piece(part, width, LINE) for part in parts[:LINE]])
        grad_w_in, grad_w_out = (
            lax.psum_scatter(
                jnp.concatenate(part), "dp", scatter_dimension=0, tiled=True
            ).astype(F32)
            for part in (parts_in, parts_out)
        )
    grad_tokens, grad_gate = kernel_call(
        finish_kernel,
        "finish",
        1,
        1,
        [shape((tok_rows, width), BF16), shape((tok_rows,), BF16)],
        [vmem] * (5 + sources),
        [pltpu.VMEM((rows, width + LANES), BF16)],
    )(target, gate, tokens, gain_row, grad_out, *back)
    return (grad_tokens, grad_gate, grad_w_in[None], grad_w_out[None])


def split_piece(piece, width, pieces):
    piece_d = width // pieces
    lower = piece[piece_d:]
    return piece[:piece_d], jnp.concatenate([lower[:, :width], lower[:, width:]])


def solution(mesh):
    placed = (
        P(("space", "dp"), None),
        P(),
        P("space", None, None),
        P("space", None, None),
        P(("space", "dp"), None),
        P(("space", "dp")),
        P(("space", "dp"), None),
    )
    return jax.shard_map(
        body,
        mesh=mesh,
        in_specs=placed,
        out_specs=(
            P(("space", "dp"), None),
            P(("space", "dp")),
            P("space", "dp", None),
            P("space", "dp", None),
        ),
        check_vma=False,
    )
```

```python
import functools

import jax
import jax.numpy as jnp
from jax import lax
from jax.experimental import pallas as pl
from jax.experimental.pallas import tpu as pltpu
from jax.sharding import PartitionSpec as P

epsilon = 1e-05
F32 = jnp.float32
BF16 = jnp.bfloat16
LANES = 128
LINE = 4
MIB = 1024 * 1024

vmem = pl.BlockSpec(memory_space=pltpu.VMEM)
smem = pl.BlockSpec(memory_space=pltpu.SMEM)
hbm = pl.BlockSpec(memory_space=pltpu.HBM)
anywhere = pl.BlockSpec(memory_space=pl.ANY)


def dot(left, right, contract=((1,), (0,))):
    return lax.dot_general(left, right, (contract, ((), ())), preferred_element_type=F32)


def normalize(tokens):
    values = tokens.astype(F32)
    center = values - jnp.mean(values, axis=-1, keepdims=True)
    spread = lax.rsqrt(jnp.mean(center * center, axis=-1, keepdims=True) + epsilon)
    return center * spread, spread


def kernel_call(kernel, name, flops, nbytes, outs, ins, scratch=(), places=None, vmem_mib=24):
    return pl.pallas_call(
        kernel,
        name=name,
        out_shape=outs,
        in_specs=ins,
        out_specs=places or [vmem] * len(outs),
        scratch_shapes=list(scratch),
        compiler_params=pltpu.CompilerParams(vmem_limit_bytes=vmem_mib * MIB),
        cost_estimate=pl.CostEstimate(flops=flops, bytes_accessed=nbytes, transcendentals=0),
    )


def start_copies(pairs, sems):
    copies = [pltpu.make_async_copy(src, dst, sems.at[i]) for i, (src, dst) in enumerate(pairs)]
    for copy in copies:
        copy.start()
    return copies


def put_blocks(first, target, gate, tok_ref, gain_ref, go_ref, sent_ref, outs, sems):
    capacity, width = outs[0].shape[0], tok_ref.shape[1]
    count = len(outs)
    hit = lax.broadcasted_iota(jnp.int32, (count * capacity, target.shape[1]), 0) == (
        target - first * capacity
    )
    gate = gate.astype(F32).reshape(target.shape)
    scaled, _ = normalize(tok_ref[...])
    normed = (scaled * gain_ref[...]).astype(BF16)
    spans = [pl.ds(j * capacity, capacity) for j in range(count)]
    stores = []
    for part, (weight, values) in enumerate(((gate, go_ref[...]), (1.0, normed))):
        columns = pl.ds((1 - part) * width, width)
        sent_ref[:, columns] = dot(jnp.where(hit, weight, 0.0).astype(BF16), values).astype(BF16)
        if capacity % 16:
            for j in range(count):
                outs[j][:, columns] = sent_ref[spans[j], columns]
        else:
            stores += start_copies(
                [(sent_ref.at[spans[j], columns], outs[j].at[:, columns]) for j in range(count)],
                sems.at[part],
            )
    for copy in stores:
        copy.wait()


def place_kernel(
    sources, capacity, me, place, ids_hbm, gate_hbm, tok_hbm, gain_hbm, go_hbm, target_ref, *refs
):
    *outs, wide_ref, ids_ref, gate_ref, tok_ref, gain_ref, go_ref, sent_ref, in_sems, out_sems = refs
    tok_rows = tok_ref.shape[0]
    loads = start_copies(
        [(ids_hbm, ids_ref), (tok_hbm, tok_ref), (gain_hbm, gain_ref), (gate_hbm, gate_ref), (go_hbm, go_ref)],
        in_sems,
    )
    earlier = lax.broadcasted_iota(jnp.int32, (LANES, LANES), 0) < lax.broadcasted_iota(
        jnp.int32, (LANES, LANES), 1
    )
    earlier = jnp.where(earlier, 1.0, 0.0).astype(BF16)
    loads[0].wait()
    chunks = range(0, tok_rows, LANES)
    wide_ref[...] = jnp.full_like(wide_ref, -1)
    wide_ref[:, :tok_rows] = ids_ref[...]
    ids = [wide_ref[:, c : c + LANES] for c in chunks]
    expert = lax.broadcasted_iota(jnp.int32, (sources, LANES), 0)
    onehots = [jnp.where(expert == chunk, 1.0, 0.0) for chunk in ids]
    within = dot(jnp.concatenate(onehots).astype(BF16), earlier)
    base = jnp.zeros((sources, 1), F32)
    for i, (c, chunk, onehot) in enumerate(zip(chunks, ids, onehots)):
        before = within[i * sources : (i + 1) * sources] + base
        base += jnp.sum(onehot, axis=1, keepdims=True)
        rank = jnp.sum(before * onehot, axis=0, keepdims=True).astype(jnp.int32)
        away = jnp.bitwise_xor(chunk, me[0])
        block = jnp.zeros_like(away)
        for j, k in enumerate(block_order(sources)):
            block = jnp.where(away == k, j, block)
        end = min(LANES, tok_rows - c)
        target = jnp.where(rank < capacity, block * capacity + rank, -1)
        target_ref[:, c : c + end] = target[:, :end]
    for copy in loads[1:]:
        copy.wait()
    put_blocks(0, target_ref[...], gate_ref[...], tok_ref, gain_ref, go_ref, sent_ref, outs, out_sems)


def rest_kernel(first, target_ref, gate_ref, tok_ref, gain_ref, go_ref, *refs):
    *outs, sent_ref, sems = refs
    put_blocks(first, target_ref[...], gate_ref[...], tok_ref, gain_ref, go_ref, sent_ref, outs, sems)


def keep_kernel(block_ref, out_ref):
    out_ref[...] = block_ref[...]


def gelu_parts(value):
    root = 0.7978845608028654
    cubic = root * 0.044715
    square = value * value
    tan = jnp.tanh(value * (root + cubic * square))
    half = 0.5 + 0.5 * tan
    act = value * half
    return act, half + act * (1.0 - tan) * (root + 3.0 * cubic * square)


def shard_order(place):
    second = jnp.where(place < 2, 2 - 2 * place, 7 - 2 * place)
    return [3 - place, second, 3 - second, place]


def expert_work(order, blocks, w_in_ref, w_out_ref, gpre_ref, extra_ref, rows_ref, turned_ref, put):
    capacity = blocks[0].shape[0]
    width, hidden = w_in_ref.shape
    piece_d, piece_f = width // LINE, hidden // LINE
    for j, block in enumerate(blocks):
        rows_ref[j * capacity : (j + 1) * capacity, :] = block[...]
    for j in range(LINE):
        start = pl.multiple_of(order[j] * piece_d, piece_d)
        turned_ref[j * piece_d : (j + 1) * piece_d, :] = rows_ref[:, pl.ds(start, piece_d)].T
    total = jnp.zeros(extra_ref.shape, F32)
    for j in range(LINE):
        part = pl.ds(pl.multiple_of(order[j] * piece_f, piece_f), piece_f)
        delta = rows_ref[:, width:]
        act, slope = gelu_parts(dot(rows_ref[:, :width], w_in_ref[:, part]))
        grad_act = dot(delta, w_out_ref[part, :], ((1,), (1,)))
        products = act * grad_act
        for lane in range(0, piece_f, LANES):
            total += products[:, lane : lane + LANES]
        grad_pre = (grad_act * slope).astype(BF16)
        gpre_ref[:, part] = grad_pre
        put(j, part, dot(turned_ref[...], grad_pre), dot(act.astype(BF16).T, delta))
    total = jnp.sum(total, axis=1, keepdims=True)
    high = total.astype(BF16).astype(F32)
    lane = lax.broadcasted_iota(jnp.int32, extra_ref.shape, 1)
    extra_ref[...] = jnp.where(lane == 0, high, jnp.where(lane == 1, total - high, 0.0)).astype(BF16)


def sooner_kernel(count, groups, place, w_in_ref, w_out_ref, *refs):
    blocks = refs[:count]
    sum_in_ref, sum_out_ref, gpre_ref, extra_ref, rows_ref, turned_ref = refs[count:]
    piece_f = w_in_ref.shape[1] // LINE

    def put(j, part, weight_in, weight_out):
        sum_in_ref[:, part] = weight_in
        sum_out_ref[j * piece_f : (j + 1) * piece_f, :] = weight_out

    order = shard_order(place[0]) if groups == LINE else list(range(LINE))
    expert_work(order, blocks, w_in_ref, w_out_ref, gpre_ref, extra_ref, rows_ref, turned_ref, put)


def next_kernel(count, groups, place, w_in_ref, w_out_ref, old_in_ref, old_out_ref, *refs):
    blocks = refs[:count]
    sum_in_ref, sum_out_ref, gpre_ref, extra_ref, rows_ref, turned_ref = refs[count:]
    piece_f = w_in_ref.shape[1] // LINE

    def put(j, part, weight_in, weight_out):
        chunk = slice(j * piece_f, (j + 1) * piece_f)
        sum_in_ref[:, part] = old_in_ref[:, part] + weight_in
        sum_out_ref[chunk, :] = old_out_ref[chunk, :] + weight_out

    order = shard_order(place[0]) if groups == LINE else list(range(LINE))
    expert_work(order, blocks, w_in_ref, w_out_ref, gpre_ref, extra_ref, rows_ref, turned_ref, put)


def later_kernel(count, groups, place, w_in_ref, w_out_ref, sum_in_ref, sum_out_ref, *refs):
    blocks = refs[:count]
    outs = refs[count : count + LINE]
    upper_ref, lower_ref, gpre_ref, extra_ref, rows_ref, turned_ref = refs[count + LINE :]
    width, hidden = w_in_ref.shape
    piece_d, piece_f = width // LINE, hidden // LINE

    def put(j, part, weight_in, weight_out):
        weight = (sum_out_ref[j * piece_f : (j + 1) * piece_f, :] + weight_out).astype(BF16)
        outs[j][piece_d:, :width] = weight[: piece_f // 2]
        outs[j][piece_d:, width:] = weight[piece_f // 2 :]
        weight = (sum_in_ref[:, part] + weight_in).astype(BF16)
        for i in range(LINE):
            outs[i][:piece_d, part] = weight[i * piece_d : (i + 1) * piece_d]

    order = shard_order(place[0]) if groups == LINE else list(range(LINE))
    expert_work(order, blocks, w_in_ref, w_out_ref, gpre_ref, extra_ref, rows_ref, turned_ref, put)
    cut = upper_ref.shape[0]
    upper_ref[...] = outs[0][:cut, :]
    lower_ref[...] = outs[0][cut:, :]


def back_kernel(capacity, sets, w_in_ref, *refs):
    inputs, outs = refs[: 2 * len(sets)], refs[2 * len(sets) :]
    width = w_in_ref.shape[0]
    for members, gpre_ref, extra_ref in zip(sets, inputs[::2], inputs[1::2]):
        grad = dot(gpre_ref[...], w_in_ref[...], ((1,), (1,))).astype(BF16)
        for i, j in enumerate(members):
            block = slice(i * capacity, (i + 1) * capacity)
            outs[j][:, :width] = grad[block]
            outs[j][:, width:] = extra_ref[block, :]


def finish_kernel(target_ref, gate_ref, tok_ref, gain_ref, go_ref, *refs):
    *blocks, tokens_out, gate_out, back_ref = refs
    rows, capacity = back_ref.shape[0], blocks[0].shape[0]
    for j, block in enumerate(blocks):
        back_ref[j * capacity : (j + 1) * capacity, :] = block[...]
    tok_rows, width = tok_ref.shape
    spots = jnp.broadcast_to(target_ref[...].astype(F32), (8, tok_rows)).T[:, :1].astype(jnp.int32)
    hit = lax.broadcasted_iota(jnp.int32, (tok_rows, rows), 1) == spots
    got = dot(jnp.where(hit, 1.0, 0.0).astype(BF16), back_ref[...])
    sums = got[:, width:].T
    gate_row = gate_ref[...].astype(F32).reshape(1, tok_rows)
    gate_out[...] = ((sums[0:1] + sums[1:2]) / gate_row).astype(BF16).reshape(tok_rows)
    scaled, spread = normalize(tok_ref[...])
    grad = got[:, :width] * gain_ref[...]
    mean = jnp.mean(grad, axis=-1, keepdims=True)
    cross = jnp.mean(grad * scaled, axis=-1, keepdims=True)
    branch = spread * (grad - mean - scaled * cross)
    tokens_out[...] = (go_ref[...].astype(F32) + branch).astype(BF16)


def block_order(sources):
    same = sorted(range(2, sources, 2), key=lambda k: (k.bit_count(), -k))
    return same + list(range(sources - 1, 1, -2)) + [1, 0]


def swap_blocks(blocks, order):
    devices = range(lax.axis_size("space"))
    return [
        lax.ppermute(block, "space", [(i, i ^ k) for i in devices]) if k else block
        for block, k in zip(blocks, order)
    ]


def pass_kernel(above_ref, inward_ref, third_ref, own_ref, out_ref, sum_ref):
    cut = above_ref.shape[0]
    out_ref[...] = (third_ref[...].astype(F32) + inward_ref[...].astype(F32)).astype(BF16)
    sum_ref[:cut, :] = own_ref[:cut, :].astype(F32) + above_ref[...].astype(F32)
    sum_ref[cut:, :] = own_ref[cut:, :].astype(F32)


def total_kernel(sum_ref, below_ref, cycle_ref, last_ref, in_hbm, out_hbm, in_ref, out_ref, sems):
    piece_d, half = in_ref.shape[0], out_ref.shape[0] // 2
    width = out_ref.shape[1]
    cut = sum_ref.shape[0] - below_ref.shape[0]
    in_ref[...] = (
        sum_ref[:piece_d, :] + cycle_ref[:piece_d, :].astype(F32) + last_ref[:piece_d, :].astype(F32)
    )
    copies = start_copies([(in_ref, in_hbm)], sems.at[0])
    total = sum_ref[piece_d:, :] + cycle_ref[piece_d:, :].astype(F32) + last_ref[piece_d:, :].astype(F32)
    split = cut - piece_d
    total = jnp.concatenate([total[:split], total[split:] + below_ref[...].astype(F32)])
    out_ref[:half, :] = total[:, :width]
    out_ref[half:, :] = total[:, width:]
    for copy in copies + start_copies([(out_ref, out_hbm)], sems.at[1]):
        copy.wait()


def line_sums(first, second, third, own, upper, lower, width, returned):
    rows, hidden = own.shape
    piece_d = width // LINE
    ahead = len(returned) // 4
    order = block_order(len(returned))
    inward = lax.ppermute(first, "dp", [(0, 1), (3, 2)])
    above = lax.ppermute(upper, "dp", [(1, 2), (2, 1)])
    below = lax.ppermute(lower, "dp", [(1, 2), (2, 1)])
    back = swap_blocks(returned[:ahead], order[:ahead])
    second, back[0] = lax.optimization_barrier((second, back[0]))
    cycle = lax.ppermute(second, "dp", [(0, 2), (1, 0), (2, 3), (3, 1)])
    third, *back = lax.optimization_barrier((third, *back))
    shape = functools.partial(jax.ShapeDtypeStruct, own.shape)
    passed, most = kernel_call(
        pass_kernel, "pass", 1, 1, [shape(BF16), shape(F32)], [vmem] * 4
    )(above, inward, third, own)
    passed, *rest = lax.optimization_barrier((passed, *returned[ahead:]))
    last = lax.ppermute(passed, "dp", [(0, 1), (3, 2), (1, 3), (2, 0)])
    back += swap_blocks(rest, order[ahead:])
    ends = (piece_d, hidden), (2 * (rows - piece_d), width)
    sums = kernel_call(
        total_kernel,
        "total",
        1,
        1,
        [jax.ShapeDtypeStruct(end, F32) for end in ends],
        [vmem] * 4,
        [pltpu.VMEM(end, F32) for end in ends] + [pltpu.SemaphoreType.DMA((2, 1))],
        places=[hbm] * 2,
    )(most, below, cycle, last)
    return *sums, back


def body(tokens, gain, w_in, w_out, expert_ids, gate, grad_out):
    sources = lax.axis_size("space")
    groups = lax.axis_size("dp")
    tok_rows, width = tokens.shape
    hidden = w_in.shape[2]
    capacity = ((tok_rows * 5 // 4 + sources - 1) // sources + 7) // 8 * 8
    rows = sources * capacity
    me = lax.axis_index("space").astype(jnp.int32).reshape(1)
    place = lax.axis_index("dp").astype(jnp.int32).reshape(1)
    ids_row = expert_ids.reshape(1, tok_rows)
    gain_row = gain.reshape(1, width)
    weight_in, weight_out = w_in[0], w_out[0]
    shape = jax.ShapeDtypeStruct
    sems = pltpu.SemaphoreType.DMA
    block_place = vmem if capacity % 16 else anywhere
    io_bytes = 2 * (2 * tok_rows * width + 2 * rows * width)

    soon = sources // 2
    blocks = [shape((capacity, 2 * width), BF16)] * soon
    target, *sent = kernel_call(
        functools.partial(place_kernel, sources, capacity),
        "place",
        2 * rows * tok_rows * width,
        io_bytes,
        [shape((1, tok_rows), jnp.int32)] + blocks,
        [smem] * 2 + [hbm] * 5,
        [
            pltpu.VMEM((1, pl.cdiv(tok_rows, LANES) * LANES), jnp.int32),
            pltpu.VMEM((1, tok_rows), jnp.int32),
            pltpu.VMEM((tok_rows,), BF16),
            pltpu.VMEM((tok_rows, width), BF16),
            pltpu.VMEM((1, width), F32),
            pltpu.VMEM((tok_rows, width), BF16),
            pltpu.VMEM((soon * capacity, 2 * width), BF16),
            sems((5,)),
            sems((2, soon)),
        ],
        places=[vmem] + [block_place] * soon,
        vmem_mib=56,
    )(me, place, ids_row, gate, tokens, gain_row, grad_out)
    sent += kernel_call(
        functools.partial(rest_kernel, soon),
        "rest",
        1,
        1,
        blocks,
        [vmem] * 5,
        [pltpu.VMEM((soon * capacity, 2 * width), BF16), sems((2, soon))],
        places=[block_place] * soon,
        vmem_mib=16,
    )(target, gate, tokens, gain_row, grad_out)
    (kept,) = kernel_call(
        keep_kernel,
        "keep",
        1,
        1,
        [shape((capacity, 2 * width), BF16)],
        [vmem],
        vmem_mib=2,
    )(sent[-1])
    arrived = swap_blocks(sent, block_order(sources))
    arrived[-1] = kept

    next_set = list(range(3 * sources // 8, sources // 2))
    late_set = list(range(sources // 2, 3 * sources // 4))
    soon_set = [j for j in range(sources) if j not in next_set + late_set]

    def work(kernel, name, members, outs, *sums):
        count, span = len(members), len(members) * capacity
        return kernel_call(
            functools.partial(kernel, count, groups),
            name,
            8 * span * width * hidden,
            2 * (2 * span * width + 4 * width * hidden + span * hidden),
            outs + [shape((span, hidden), BF16), shape((span, LANES), BF16)],
            [smem] + [vmem] * (2 + len(sums) + count),
            [pltpu.VMEM((span, 2 * width), BF16), pltpu.VMEM((width, span), BF16)],
        )(place, weight_in, weight_out, *sums, *[arrived[j] for j in members])

    sums_shape = [shape((width, hidden), F32), shape((hidden, width), F32)]
    *sums, soon_gpre, soon_extra = work(sooner_kernel, "sooner", soon_set, sums_shape)
    *sums, next_gpre, next_extra = work(next_kernel, "next", next_set, sums_shape, *sums)
    piece = shape((width // LINE + hidden // LINE // 2, hidden), BF16)
    cut = 7 * piece.shape[0] // 8
    cut_pieces = [shape((cut, hidden), BF16), shape((piece.shape[0] - cut, hidden), BF16)]
    *parts, late_gpre, late_extra = work(
        later_kernel, "later", late_set, [piece] * LINE + cut_pieces, *sums
    )
    returned = kernel_call(
        functools.partial(back_kernel, capacity, (soon_set, next_set, late_set)),
        "back",
        1,
        1,
        [shape((capacity, width + LANES), BF16)] * sources,
        [vmem] * 7,
    )(weight_in, soon_gpre, soon_extra, next_gpre, next_extra, late_gpre, late_extra)

    if groups == LINE:
        grad_w_in, grad_w_out, back = line_sums(*parts, width, returned)
    else:
        back = swap_blocks(returned, block_order(sources))
        parts_in, parts_out = zip(*[split_piece(part, width, LINE) for part in parts[:LINE]])
        grad_w_in, grad_w_out = (
            lax.psum_scatter(
                jnp.concatenate(part), "dp", scatter_dimension=0, tiled=True
            ).astype(F32)
            for part in (parts_in, parts_out)
        )
    grad_tokens, grad_gate = kernel_call(
        finish_kernel,
        "finish",
        1,
        1,
        [shape((tok_rows, width), BF16), shape((tok_rows,), BF16)],
        [vmem] * (5 + sources),
        [pltpu.VMEM((rows, width + LANES), BF16)],
    )(target, gate, tokens, gain_row, grad_out, *back)
    return (grad_tokens, grad_gate, grad_w_in[None], grad_w_out[None])


def split_piece(piece, width, pieces):
    piece_d = width // pieces
    lower = piece[piece_d:]
    return piece[:piece_d], jnp.concatenate([lower[:, :width], lower[:, width:]])


def solution(mesh):
    placed = (
        P(("space", "dp"), None),
        P(),
        P("space", None, None),
        P("space", None, None),
        P(("space", "dp"), None),
        P(("space", "dp")),
        P(("space", "dp"), None),
    )
    return jax.shard_map(
        body,
        mesh=mesh,
        in_specs=placed,
        out_specs=(
            P(("space", "dp"), None),
            P(("space", "dp")),
            P("space", "dp", None),
            P("space", "dp", None),
        ),
        check_vma=False,
    )
```

```python
import functools

import jax
import jax.numpy as jnp
from jax import lax
from jax.experimental import pallas as pl
from jax.experimental.pallas import tpu as pltpu
from jax.sharding import PartitionSpec as P

epsilon = 1e-05
F32 = jnp.float32
BF16 = jnp.bfloat16
LANES = 128
LINE = 4
MIB = 1024 * 1024

vmem = pl.BlockSpec(memory_space=pltpu.VMEM)
smem = pl.BlockSpec(memory_space=pltpu.SMEM)
hbm = pl.BlockSpec(memory_space=pltpu.HBM)
anywhere = pl.BlockSpec(memory_space=pl.ANY)


def dot(left, right, contract=((1,), (0,))):
    return lax.dot_general(left, right, (contract, ((), ())), preferred_element_type=F32)


def normalize(tokens):
    values = tokens.astype(F32)
    center = values - jnp.mean(values, axis=-1, keepdims=True)
    spread = lax.rsqrt(jnp.mean(center * center, axis=-1, keepdims=True) + epsilon)
    return center * spread, spread


def kernel_call(kernel, name, flops, nbytes, outs, ins, scratch=(), places=None, vmem_mib=24):
    return pl.pallas_call(
        kernel,
        name=name,
        out_shape=outs,
        in_specs=ins,
        out_specs=places or [vmem] * len(outs),
        scratch_shapes=list(scratch),
        compiler_params=pltpu.CompilerParams(vmem_limit_bytes=vmem_mib * MIB),
        cost_estimate=pl.CostEstimate(flops=flops, bytes_accessed=nbytes, transcendentals=0),
    )


def start_copies(pairs, sems):
    copies = [pltpu.make_async_copy(src, dst, sems.at[i]) for i, (src, dst) in enumerate(pairs)]
    for copy in copies:
        copy.start()
    return copies


def put_blocks(first, target, gate, tok_ref, gain_ref, go_ref, sent_ref, outs, sems):
    capacity, width = outs[0].shape[0], tok_ref.shape[1]
    count = len(outs)
    hit = lax.broadcasted_iota(jnp.int32, (count * capacity, target.shape[1]), 0) == (
        target - first * capacity
    )
    gate = gate.astype(F32).reshape(target.shape)
    scaled, _ = normalize(tok_ref[...])
    normed = (scaled * gain_ref[...]).astype(BF16)
    spans = [pl.ds(j * capacity, capacity) for j in range(count)]
    stores = []
    for part, (weight, values) in enumerate(((gate, go_ref[...]), (1.0, normed))):
        columns = pl.ds((1 - part) * width, width)
        sent_ref[:, columns] = dot(jnp.where(hit, weight, 0.0).astype(BF16), values).astype(BF16)
        if capacity % 16:
            for j in range(count):
                outs[j][:, columns] = sent_ref[spans[j], columns]
        else:
            stores += start_copies(
                [(sent_ref.at[spans[j], columns], outs[j].at[:, columns]) for j in range(count)],
                sems.at[part],
            )
    for copy in stores:
        copy.wait()


def place_kernel(
    sources, capacity, me, place, ids_hbm, gate_hbm, tok_hbm, gain_hbm, go_hbm, target_ref, *refs
):
    *outs, wide_ref, ids_ref, gate_ref, tok_ref, gain_ref, go_ref, sent_ref, in_sems, out_sems = refs
    tok_rows = tok_ref.shape[0]
    loads = start_copies(
        [(ids_hbm, ids_ref), (tok_hbm, tok_ref), (gain_hbm, gain_ref), (gate_hbm, gate_ref), (go_hbm, go_ref)],
        in_sems,
    )
    earlier = lax.broadcasted_iota(jnp.int32, (LANES, LANES), 0) < lax.broadcasted_iota(
        jnp.int32, (LANES, LANES), 1
    )
    earlier = jnp.where(earlier, 1.0, 0.0).astype(BF16)
    loads[0].wait()
    chunks = range(0, tok_rows, LANES)
    wide_ref[...] = jnp.full_like(wide_ref, -1)
    wide_ref[:, :tok_rows] = ids_ref[...]
    ids = [wide_ref[:, c : c + LANES] for c in chunks]
    expert = lax.broadcasted_iota(jnp.int32, (sources, LANES), 0)
    onehots = [jnp.where(expert == chunk, 1.0, 0.0) for chunk in ids]
    within = dot(jnp.concatenate(onehots).astype(BF16), earlier)
    base = jnp.zeros((sources, 1), F32)
    for i, (c, chunk, onehot) in enumerate(zip(chunks, ids, onehots)):
        before = within[i * sources : (i + 1) * sources] + base
        base += jnp.sum(onehot, axis=1, keepdims=True)
        rank = jnp.sum(before * onehot, axis=0, keepdims=True).astype(jnp.int32)
        away = jnp.bitwise_xor(chunk, me[0])
        block = jnp.zeros_like(away)
        for j, k in enumerate(block_order(sources)):
            block = jnp.where(away == k, j, block)
        end = min(LANES, tok_rows - c)
        target = jnp.where(rank < capacity, block * capacity + rank, -1)
        target_ref[:, c : c + end] = target[:, :end]
    for copy in loads[1:]:
        copy.wait()
    put_blocks(0, target_ref[...], gate_ref[...], tok_ref, gain_ref, go_ref, sent_ref, outs, out_sems)


def rest_kernel(first, target_ref, gate_ref, tok_ref, gain_ref, go_ref, *refs):
    *outs, sent_ref, sems = refs
    put_blocks(first, target_ref[...], gate_ref[...], tok_ref, gain_ref, go_ref, sent_ref, outs, sems)


def keep_kernel(block_ref, out_ref):
    out_ref[...] = block_ref[...]


def gelu_parts(value):
    root = 0.7978845608028654
    cubic = root * 0.044715
    square = value * value
    tan = jnp.tanh(value * (root + cubic * square))
    half = 0.5 + 0.5 * tan
    act = value * half
    return act, half + act * (1.0 - tan) * (root + 3.0 * cubic * square)


def shard_order(place):
    first = jnp.where(lax.rem(place, 2) == 0, 3, 0)
    second = jnp.where(place < 2, 2, 1)
    return [first, second, 6 - first - second - place, place]


def expert_work(order, blocks, w_in_ref, w_out_ref, gpre_ref, extra_ref, rows_ref, turned_ref, put):
    capacity = blocks[0].shape[0]
    width, hidden = w_in_ref.shape
    piece_d, piece_f = width // LINE, hidden // LINE
    for j, block in enumerate(blocks):
        rows_ref[j * capacity : (j + 1) * capacity, :] = block[...]
    for j in range(LINE):
        start = pl.multiple_of(order[j] * piece_d, piece_d)
        turned_ref[j * piece_d : (j + 1) * piece_d, :] = rows_ref[:, pl.ds(start, piece_d)].T
    total = jnp.zeros(extra_ref.shape, F32)
    for j in range(LINE):
        part = pl.ds(pl.multiple_of(order[j] * piece_f, piece_f), piece_f)
        delta = rows_ref[:, width:]
        act, slope = gelu_parts(dot(rows_ref[:, :width], w_in_ref[:, part]))
        grad_act = dot(delta, w_out_ref[part, :], ((1,), (1,)))
        products = act * grad_act
        for lane in range(0, piece_f, LANES):
            total += products[:, lane : lane + LANES]
        grad_pre = (grad_act * slope).astype(BF16)
        gpre_ref[:, part] = grad_pre
        put(j, part, dot(turned_ref[...], grad_pre), dot(act.astype(BF16).T, delta))
    total = jnp.sum(total, axis=1, keepdims=True)
    high = total.astype(BF16).astype(F32)
    lane = lax.broadcasted_iota(jnp.int32, extra_ref.shape, 1)
    extra_ref[...] = jnp.where(lane == 0, high, jnp.where(lane == 1, total - high, 0.0)).astype(BF16)


def sooner_kernel(count, groups, place, w_in_ref, w_out_ref, *refs):
    blocks = refs[:count]
    sum_in_ref, sum_out_ref, gpre_ref, extra_ref, rows_ref, turned_ref = refs[count:]
    piece_f = w_in_ref.shape[1] // LINE

    def put(j, part, weight_in, weight_out):
        sum_in_ref[:, part] = weight_in
        sum_out_ref[j * piece_f : (j + 1) * piece_f, :] = weight_out

    order = shard_order(place[0]) if groups == LINE else list(range(LINE))
    expert_work(order, blocks, w_in_ref, w_out_ref, gpre_ref, extra_ref, rows_ref, turned_ref, put)


def next_kernel(count, groups, place, w_in_ref, w_out_ref, old_in_ref, old_out_ref, *refs):
    blocks = refs[:count]
    sum_in_ref, sum_out_ref, gpre_ref, extra_ref, rows_ref, turned_ref = refs[count:]
    piece_f = w_in_ref.shape[1] // LINE

    def put(j, part, weight_in, weight_out):
        chunk = slice(j * piece_f, (j + 1) * piece_f)
        sum_in_ref[:, part] = old_in_ref[:, part] + weight_in
        sum_out_ref[chunk, :] = old_out_ref[chunk, :] + weight_out

    order = shard_order(place[0]) if groups == LINE else list(range(LINE))
    expert_work(order, blocks, w_in_ref, w_out_ref, gpre_ref, extra_ref, rows_ref, turned_ref, put)


def later_kernel(count, groups, place, w_in_ref, w_out_ref, sum_in_ref, sum_out_ref, *refs):
    blocks = refs[:count]
    outs = refs[count : count + LINE]
    upper_ref, lower_ref, gpre_ref, extra_ref, rows_ref, turned_ref = refs[count + LINE :]
    width, hidden = w_in_ref.shape
    piece_d, piece_f = width // LINE, hidden // LINE

    def put(j, part, weight_in, weight_out):
        weight = (sum_out_ref[j * piece_f : (j + 1) * piece_f, :] + weight_out).astype(BF16)
        outs[j][piece_d:, :width] = weight[: piece_f // 2]
        outs[j][piece_d:, width:] = weight[piece_f // 2 :]
        weight = (sum_in_ref[:, part] + weight_in).astype(BF16)
        for i in range(LINE):
            outs[i][:piece_d, part] = weight[i * piece_d : (i + 1) * piece_d]

    order = shard_order(place[0]) if groups == LINE else list(range(LINE))
    expert_work(order, blocks, w_in_ref, w_out_ref, gpre_ref, extra_ref, rows_ref, turned_ref, put)
    cut = upper_ref.shape[0]
    upper_ref[...] = outs[1][:cut, :]
    lower_ref[...] = outs[1][cut:, :]


def back_kernel(capacity, sets, w_in_ref, *refs):
    inputs, outs = refs[: 2 * len(sets)], refs[2 * len(sets) :]
    width = w_in_ref.shape[0]
    for members, gpre_ref, extra_ref in zip(sets, inputs[::2], inputs[1::2]):
        grad = dot(gpre_ref[...], w_in_ref[...], ((1,), (1,))).astype(BF16)
        for i, j in enumerate(members):
            block = slice(i * capacity, (i + 1) * capacity)
            outs[j][:, :width] = grad[block]
            outs[j][:, width:] = extra_ref[block, :]


def finish_kernel(target_ref, gate_ref, tok_ref, gain_ref, go_ref, *refs):
    *blocks, tokens_out, gate_out, back_ref = refs
    rows, capacity = back_ref.shape[0], blocks[0].shape[0]
    for j, block in enumerate(blocks):
        back_ref[j * capacity : (j + 1) * capacity, :] = block[...]
    tok_rows, width = tok_ref.shape
    spots = jnp.broadcast_to(target_ref[...].astype(F32), (8, tok_rows)).T[:, :1].astype(jnp.int32)
    hit = lax.broadcasted_iota(jnp.int32, (tok_rows, rows), 1) == spots
    got = dot(jnp.where(hit, 1.0, 0.0).astype(BF16), back_ref[...])
    sums = got[:, width:].T
    gate_row = gate_ref[...].astype(F32).reshape(1, tok_rows)
    gate_out[...] = ((sums[0:1] + sums[1:2]) / gate_row).astype(BF16).reshape(tok_rows)
    scaled, spread = normalize(tok_ref[...])
    grad = got[:, :width] * gain_ref[...]
    mean = jnp.mean(grad, axis=-1, keepdims=True)
    cross = jnp.mean(grad * scaled, axis=-1, keepdims=True)
    branch = spread * (grad - mean - scaled * cross)
    tokens_out[...] = (go_ref[...].astype(F32) + branch).astype(BF16)


def block_order(sources):
    same = sorted(range(2, sources, 2), key=lambda k: (k.bit_count(), -k))
    return same + list(range(sources - 1, 1, -2)) + [1, 0]


def swap_blocks(blocks, order):
    devices = range(lax.axis_size("space"))
    return [
        lax.ppermute(block, "space", [(i, i ^ k) for i in devices]) if k else block
        for block, k in zip(blocks, order)
    ]


def pass_kernel(
    place, swapped_ref, above_ref, quarter_ref, third_ref, own_ref, lower_ref, out_ref, sum_ref, on_ref
):
    inner = (place[0] == 1) | (place[0] == 2)
    cut = above_ref.shape[0]
    swapped = swapped_ref[...].astype(F32)
    out_ref[...] = (third_ref[...].astype(F32) + jnp.where(inner, swapped, 0.0)).astype(BF16)
    total = own_ref[...].astype(F32) + jnp.where(inner, 0.0, swapped)
    sum_ref[:cut, :] = total[:cut] + jnp.where(inner, above_ref[...].astype(F32), 0.0)
    sum_ref[cut:, :] = total[cut:]
    on_ref[...] = (lower_ref[...].astype(F32) + quarter_ref[...].astype(F32)).astype(BF16)


def total_kernel(sum_ref, below_ref, across_ref, last_ref, in_hbm, out_hbm, in_ref, out_ref, sems):
    piece_d, half = in_ref.shape[0], out_ref.shape[0] // 2
    width = out_ref.shape[1]
    cut = across_ref.shape[0]

    def part(start, end, more):
        return sum_ref[start:end, :] + last_ref[start:end, :].astype(F32) + more.astype(F32)

    in_ref[...] = part(0, piece_d, across_ref[:piece_d, :])
    copies = start_copies([(in_ref, in_hbm)], sems.at[0])
    total = jnp.concatenate(
        [part(piece_d, cut, across_ref[piece_d:, :]), part(cut, sum_ref.shape[0], below_ref[...])]
    )
    out_ref[:half, :] = total[:, :width]
    out_ref[half:, :] = total[:, width:]
    for copy in copies + start_copies([(out_ref, out_hbm)], sems.at[1]):
        copy.wait()


def line_sums(place, first, third, own, upper, lower, width, returned):
    rows, hidden = own.shape
    piece_d = width // LINE
    ahead = 3 * len(returned) // 8
    order = block_order(len(returned))
    swap = [(0, 1), (1, 0), (2, 3), (3, 2)]
    swapped = lax.ppermute(first, "dp", swap)
    above = lax.ppermute(upper, "dp", [(1, 2), (2, 1)])
    quarter = lax.ppermute(lower, "dp", swap)
    back = swap_blocks(returned[:ahead], order[:ahead])
    upper, back[0] = lax.optimization_barrier((upper, back[0]))
    across = lax.ppermute(upper, "dp", [(0, 2), (3, 1)])
    third, *back = lax.optimization_barrier((third, *back))
    shape = functools.partial(jax.ShapeDtypeStruct, own.shape)
    passed, most, onward = kernel_call(
        pass_kernel,
        "pass",
        1,
        1,
        [shape(BF16), shape(F32), jax.ShapeDtypeStruct(lower.shape, BF16)],
        [smem] + [vmem] * 6,
    )(place, swapped, above, quarter, third, own, lower)
    passed, *rest = lax.optimization_barrier((passed, *returned[ahead:]))
    last = lax.ppermute(passed, "dp", [(0, 1), (3, 2), (1, 3), (2, 0)])
    below = lax.ppermute(onward, "dp", [(1, 2), (2, 1)])
    across, rest[-2] = lax.optimization_barrier((across, rest[-2]))
    back += swap_blocks(rest, order[ahead:])
    ends = (piece_d, hidden), (2 * (rows - piece_d), width)
    sums = kernel_call(
        total_kernel,
        "total",
        1,
        1,
        [jax.ShapeDtypeStruct(end, F32) for end in ends],
        [vmem] * 4,
        [pltpu.VMEM(end, F32) for end in ends] + [pltpu.SemaphoreType.DMA((2, 1))],
        places=[hbm] * 2,
    )(most, below, across, last)
    return *sums, back


def body(tokens, gain, w_in, w_out, expert_ids, gate, grad_out):
    sources = lax.axis_size("space")
    groups = lax.axis_size("dp")
    tok_rows, width = tokens.shape
    hidden = w_in.shape[2]
    capacity = ((tok_rows * 5 // 4 + sources - 1) // sources + 7) // 8 * 8
    rows = sources * capacity
    me = lax.axis_index("space").astype(jnp.int32).reshape(1)
    place = lax.axis_index("dp").astype(jnp.int32).reshape(1)
    ids_row = expert_ids.reshape(1, tok_rows)
    gain_row = gain.reshape(1, width)
    weight_in, weight_out = w_in[0], w_out[0]
    shape = jax.ShapeDtypeStruct
    sems = pltpu.SemaphoreType.DMA
    block_place = vmem if capacity % 16 else anywhere
    io_bytes = 2 * (2 * tok_rows * width + 2 * rows * width)

    soon = sources // 2
    blocks = [shape((capacity, 2 * width), BF16)] * soon
    target, *sent = kernel_call(
        functools.partial(place_kernel, sources, capacity),
        "place",
        2 * rows * tok_rows * width,
        io_bytes,
        [shape((1, tok_rows), jnp.int32)] + blocks,
        [smem] * 2 + [hbm] * 5,
        [
            pltpu.VMEM((1, pl.cdiv(tok_rows, LANES) * LANES), jnp.int32),
            pltpu.VMEM((1, tok_rows), jnp.int32),
            pltpu.VMEM((tok_rows,), BF16),
            pltpu.VMEM((tok_rows, width), BF16),
            pltpu.VMEM((1, width), F32),
            pltpu.VMEM((tok_rows, width), BF16),
            pltpu.VMEM((soon * capacity, 2 * width), BF16),
            sems((5,)),
            sems((2, soon)),
        ],
        places=[vmem] + [block_place] * soon,
        vmem_mib=56,
    )(me, place, ids_row, gate, tokens, gain_row, grad_out)
    sent += kernel_call(
        functools.partial(rest_kernel, soon),
        "rest",
        1,
        1,
        blocks,
        [vmem] * 5,
        [pltpu.VMEM((soon * capacity, 2 * width), BF16), sems((2, soon))],
        places=[block_place] * soon,
        vmem_mib=16,
    )(target, gate, tokens, gain_row, grad_out)
    (kept,) = kernel_call(
        keep_kernel,
        "keep",
        1,
        1,
        [shape((capacity, 2 * width), BF16)],
        [vmem],
        vmem_mib=2,
    )(sent[-1])
    arrived = swap_blocks(sent, block_order(sources))
    arrived[-1] = kept

    next_set = list(range(3 * sources // 8, sources // 2))
    late_set = list(range(sources // 2, 3 * sources // 4))
    soon_set = [j for j in range(sources) if j not in next_set + late_set]

    def work(kernel, name, members, outs, *sums):
        count, span = len(members), len(members) * capacity
        return kernel_call(
            functools.partial(kernel, count, groups),
            name,
            8 * span * width * hidden,
            2 * (2 * span * width + 4 * width * hidden + span * hidden),
            outs + [shape((span, hidden), BF16), shape((span, LANES), BF16)],
            [smem] + [vmem] * (2 + len(sums) + count),
            [pltpu.VMEM((span, 2 * width), BF16), pltpu.VMEM((width, span), BF16)],
        )(place, weight_in, weight_out, *sums, *[arrived[j] for j in members])

    sums_shape = [shape((width, hidden), F32), shape((hidden, width), F32)]
    *sums, soon_gpre, soon_extra = work(sooner_kernel, "sooner", soon_set, sums_shape)
    *sums, next_gpre, next_extra = work(next_kernel, "next", next_set, sums_shape, *sums)
    piece = shape((width // LINE + hidden // LINE // 2, hidden), BF16)
    cut = 3 * piece.shape[0] // 4
    cut_pieces = [shape((cut, hidden), BF16), shape((piece.shape[0] - cut, hidden), BF16)]
    *parts, late_gpre, late_extra = work(
        later_kernel, "later", late_set, [piece] * LINE + cut_pieces, *sums
    )
    returned = kernel_call(
        functools.partial(back_kernel, capacity, (soon_set, next_set, late_set)),
        "back",
        1,
        1,
        [shape((capacity, width + LANES), BF16)] * sources,
        [vmem] * 7,
    )(weight_in, soon_gpre, soon_extra, next_gpre, next_extra, late_gpre, late_extra)

    if groups == LINE:
        grad_w_in, grad_w_out, back = line_sums(
            place, parts[0], *parts[2:], width, returned
        )
    else:
        back = swap_blocks(returned, block_order(sources))
        parts_in, parts_out = zip(*[split_piece(part, width, LINE) for part in parts[:LINE]])
        grad_w_in, grad_w_out = (
            lax.psum_scatter(
                jnp.concatenate(part), "dp", scatter_dimension=0, tiled=True
            ).astype(F32)
            for part in (parts_in, parts_out)
        )
    grad_tokens, grad_gate = kernel_call(
        finish_kernel,
        "finish",
        1,
        1,
        [shape((tok_rows, width), BF16), shape((tok_rows,), BF16)],
        [vmem] * (5 + sources),
        [pltpu.VMEM((rows, width + LANES), BF16)],
    )(target, gate, tokens, gain_row, grad_out, *back)
    return (grad_tokens, grad_gate, grad_w_in[None], grad_w_out[None])


def split_piece(piece, width, pieces):
    piece_d = width // pieces
    lower = piece[piece_d:]
    return piece[:piece_d], jnp.concatenate([lower[:, :width], lower[:, width:]])


def solution(mesh):
    placed = (
        P(("space", "dp"), None),
        P(),
        P("space", None, None),
        P("space", None, None),
        P(("space", "dp"), None),
        P(("space", "dp")),
        P(("space", "dp"), None),
    )
    return jax.shard_map(
        body,
        mesh=mesh,
        in_specs=placed,
        out_specs=(
            P(("space", "dp"), None),
            P(("space", "dp")),
            P("space", "dp", None),
            P("space", "dp", None),
        ),
        check_vma=False,
    )
```

```python
import functools

import jax
import jax.numpy as jnp
from jax import lax
from jax.experimental import pallas as pl
from jax.experimental.pallas import tpu as pltpu
from jax.sharding import PartitionSpec as P

epsilon = 1e-05
F32 = jnp.float32
BF16 = jnp.bfloat16
LANES = 128
LINE = 4
MIB = 1024 * 1024

vmem = pl.BlockSpec(memory_space=pltpu.VMEM)
smem = pl.BlockSpec(memory_space=pltpu.SMEM)
hbm = pl.BlockSpec(memory_space=pltpu.HBM)
anywhere = pl.BlockSpec(memory_space=pl.ANY)


def dot(left, right, contract=((1,), (0,))):
    return lax.dot_general(left, right, (contract, ((), ())), preferred_element_type=F32)


def normalize(tokens):
    values = tokens.astype(F32)
    center = values - jnp.mean(values, axis=-1, keepdims=True)
    spread = lax.rsqrt(jnp.mean(center * center, axis=-1, keepdims=True) + epsilon)
    return center * spread, spread


def kernel_call(kernel, name, flops, nbytes, outs, ins, scratch=(), places=None, vmem_mib=24):
    return pl.pallas_call(
        kernel,
        name=name,
        out_shape=outs,
        in_specs=ins,
        out_specs=places or [vmem] * len(outs),
        scratch_shapes=list(scratch),
        compiler_params=pltpu.CompilerParams(vmem_limit_bytes=vmem_mib * MIB),
        cost_estimate=pl.CostEstimate(flops=flops, bytes_accessed=nbytes, transcendentals=0),
    )


def start_copies(pairs, sems):
    copies = [pltpu.make_async_copy(src, dst, sems.at[i]) for i, (src, dst) in enumerate(pairs)]
    for copy in copies:
        copy.start()
    return copies


def put_blocks(first, target, gate, tok_ref, gain_ref, go_ref, sent_ref, outs, sems):
    capacity, width = outs[0].shape[0], tok_ref.shape[1]
    count = len(outs)
    hit = lax.broadcasted_iota(jnp.int32, (count * capacity, target.shape[1]), 0) == (
        target - first * capacity
    )
    gate = gate.astype(F32).reshape(target.shape)
    scaled, _ = normalize(tok_ref[...])
    normed = (scaled * gain_ref[...]).astype(BF16)
    spans = [pl.ds(j * capacity, capacity) for j in range(count)]
    stores = []
    for part, (weight, values) in enumerate(((gate, go_ref[...]), (1.0, normed))):
        columns = pl.ds((1 - part) * width, width)
        sent_ref[:, columns] = dot(jnp.where(hit, weight, 0.0).astype(BF16), values).astype(BF16)
        if capacity % 16:
            for j in range(count):
                outs[j][:, columns] = sent_ref[spans[j], columns]
        else:
            stores += start_copies(
                [(sent_ref.at[spans[j], columns], outs[j].at[:, columns]) for j in range(count)],
                sems.at[part],
            )
    for copy in stores:
        copy.wait()


def place_kernel(
    sources, capacity, me, place, ids_hbm, gate_hbm, tok_hbm, gain_hbm, go_hbm, target_ref, *refs
):
    *outs, wide_ref, ids_ref, gate_ref, tok_ref, gain_ref, go_ref, sent_ref, in_sems, out_sems = refs
    tok_rows = tok_ref.shape[0]
    loads = start_copies(
        [(ids_hbm, ids_ref), (tok_hbm, tok_ref), (gain_hbm, gain_ref), (gate_hbm, gate_ref), (go_hbm, go_ref)],
        in_sems,
    )
    earlier = lax.broadcasted_iota(jnp.int32, (LANES, LANES), 0) < lax.broadcasted_iota(
        jnp.int32, (LANES, LANES), 1
    )
    earlier = jnp.where(earlier, 1.0, 0.0).astype(BF16)
    loads[0].wait()
    chunks = range(0, tok_rows, LANES)
    wide_ref[...] = jnp.full_like(wide_ref, -1)
    wide_ref[:, :tok_rows] = ids_ref[...]
    ids = [wide_ref[:, c : c + LANES] for c in chunks]
    expert = lax.broadcasted_iota(jnp.int32, (sources, LANES), 0)
    onehots = [jnp.where(expert == chunk, 1.0, 0.0) for chunk in ids]
    within = dot(jnp.concatenate(onehots).astype(BF16), earlier)
    base = jnp.zeros((sources, 1), F32)
    for i, (c, chunk, onehot) in enumerate(zip(chunks, ids, onehots)):
        before = within[i * sources : (i + 1) * sources] + base
        base += jnp.sum(onehot, axis=1, keepdims=True)
        rank = jnp.sum(before * onehot, axis=0, keepdims=True).astype(jnp.int32)
        away = jnp.bitwise_xor(chunk, me[0])
        block = jnp.zeros_like(away)
        for j, k in enumerate(block_order(sources)):
            block = jnp.where(away == k, j, block)
        end = min(LANES, tok_rows - c)
        target = jnp.where(rank < capacity, block * capacity + rank, -1)
        target_ref[:, c : c + end] = target[:, :end]
    for copy in loads[1:]:
        copy.wait()
    put_blocks(0, target_ref[...], gate_ref[...], tok_ref, gain_ref, go_ref, sent_ref, outs, out_sems)


def rest_kernel(first, target_ref, gate_ref, tok_ref, gain_ref, go_ref, *refs):
    *outs, sent_ref, sems = refs
    put_blocks(first, target_ref[...], gate_ref[...], tok_ref, gain_ref, go_ref, sent_ref, outs, sems)


def keep_kernel(block_ref, out_ref):
    out_ref[...] = block_ref[...]


def gelu_parts(value):
    root = 0.7978845608028654
    cubic = root * 0.044715
    square = value * value
    tan = jnp.tanh(value * (root + cubic * square))
    half = 0.5 + 0.5 * tan
    act = value * half
    return act, half + act * (1.0 - tan) * (root + 3.0 * cubic * square)


def shard_order(place):
    first = jnp.where(lax.rem(place, 2) == 0, 3, 0)
    second = jnp.where(place < 2, 2, 1)
    return [first, second, 6 - first - second - place, place]


def expert_work(order, blocks, w_in_ref, w_out_ref, gpre_ref, extra_ref, rows_ref, turned_ref, put):
    capacity = blocks[0].shape[0]
    width, hidden = w_in_ref.shape
    piece_d, piece_f = width // LINE, hidden // LINE
    for j, block in enumerate(blocks):
        rows_ref[j * capacity : (j + 1) * capacity, :] = block[...]
    for j in range(LINE):
        start = pl.multiple_of(order[j] * piece_d, piece_d)
        turned_ref[j * piece_d : (j + 1) * piece_d, :] = rows_ref[:, pl.ds(start, piece_d)].T
    total = jnp.zeros(extra_ref.shape, F32)
    for j in range(LINE):
        part = pl.ds(pl.multiple_of(order[j] * piece_f, piece_f), piece_f)
        delta = rows_ref[:, width:]
        act, slope = gelu_parts(dot(rows_ref[:, :width], w_in_ref[:, part]))
        grad_act = dot(delta, w_out_ref[part, :], ((1,), (1,)))
        products = act * grad_act
        for lane in range(0, piece_f, LANES):
            total += products[:, lane : lane + LANES]
        grad_pre = (grad_act * slope).astype(BF16)
        gpre_ref[:, part] = grad_pre
        put(j, part, dot(turned_ref[...], grad_pre), dot(act.astype(BF16).T, delta))
    total = jnp.sum(total, axis=1, keepdims=True)
    high = total.astype(BF16).astype(F32)
    lane = lax.broadcasted_iota(jnp.int32, extra_ref.shape, 1)
    extra_ref[...] = jnp.where(lane == 0, high, jnp.where(lane == 1, total - high, 0.0)).astype(BF16)


def sooner_kernel(count, groups, place, w_in_ref, w_out_ref, *refs):
    blocks = refs[:count]
    sum_in_ref, sum_out_ref, gpre_ref, extra_ref, rows_ref, turned_ref = refs[count:]
    piece_f = w_in_ref.shape[1] // LINE

    def put(j, part, weight_in, weight_out):
        sum_in_ref[:, part] = weight_in
        sum_out_ref[j * piece_f : (j + 1) * piece_f, :] = weight_out

    order = shard_order(place[0]) if groups == LINE else list(range(LINE))
    expert_work(order, blocks, w_in_ref, w_out_ref, gpre_ref, extra_ref, rows_ref, turned_ref, put)


def next_kernel(count, groups, place, w_in_ref, w_out_ref, old_in_ref, old_out_ref, *refs):
    blocks = refs[:count]
    sum_in_ref, sum_out_ref, gpre_ref, extra_ref, rows_ref, turned_ref = refs[count:]
    piece_f = w_in_ref.shape[1] // LINE

    def put(j, part, weight_in, weight_out):
        chunk = slice(j * piece_f, (j + 1) * piece_f)
        sum_in_ref[:, part] = old_in_ref[:, part] + weight_in
        sum_out_ref[chunk, :] = old_out_ref[chunk, :] + weight_out

    order = shard_order(place[0]) if groups == LINE else list(range(LINE))
    expert_work(order, blocks, w_in_ref, w_out_ref, gpre_ref, extra_ref, rows_ref, turned_ref, put)


def later_kernel(count, groups, place, w_in_ref, w_out_ref, sum_in_ref, sum_out_ref, *refs):
    blocks = refs[:count]
    first_ref, third_ref, own_ref, upper_ref, lower_ref, gpre_ref, extra_ref = refs[count:-3]
    rows_ref, turned_ref, second_ref = refs[-3:]
    outs = (first_ref, second_ref, third_ref, own_ref)
    width, hidden = w_in_ref.shape
    piece_d, piece_f = width // LINE, hidden // LINE

    def put(j, part, weight_in, weight_out):
        weight = (sum_out_ref[j * piece_f : (j + 1) * piece_f, :] + weight_out).astype(BF16)
        outs[j][piece_d:, :width] = weight[: piece_f // 2]
        outs[j][piece_d:, width:] = weight[piece_f // 2 :]
        weight = (sum_in_ref[:, part] + weight_in).astype(BF16)
        for i in range(LINE):
            outs[i][:piece_d, part] = weight[i * piece_d : (i + 1) * piece_d]

    order = shard_order(place[0]) if groups == LINE else list(range(LINE))
    expert_work(order, blocks, w_in_ref, w_out_ref, gpre_ref, extra_ref, rows_ref, turned_ref, put)
    cut = upper_ref.shape[0]
    upper_ref[...] = second_ref[:cut, :]
    lower_ref[...] = second_ref[cut:, :]


def back_kernel(capacity, sets, w_in_ref, *refs):
    inputs, outs = refs[: 2 * len(sets)], refs[2 * len(sets) :]
    width = w_in_ref.shape[0]
    for members, gpre_ref, extra_ref in zip(sets, inputs[::2], inputs[1::2]):
        grad = dot(gpre_ref[...], w_in_ref[...], ((1,), (1,))).astype(BF16)
        for i, j in enumerate(members):
            block = slice(i * capacity, (i + 1) * capacity)
            outs[j][:, :width] = grad[block]
            outs[j][:, width:] = extra_ref[block, :]


def finish_kernel(target_ref, gate_ref, tok_ref, gain_ref, go_ref, *refs):
    *blocks, tokens_out, gate_out, back_ref = refs
    rows, capacity = back_ref.shape[0], blocks[0].shape[0]
    for j, block in enumerate(blocks):
        back_ref[j * capacity : (j + 1) * capacity, :] = block[...]
    tok_rows, width = tok_ref.shape
    spots = jnp.broadcast_to(target_ref[...].astype(F32), (8, tok_rows)).T[:, :1].astype(jnp.int32)
    hit = lax.broadcasted_iota(jnp.int32, (tok_rows, rows), 1) == spots
    got = dot(jnp.where(hit, 1.0, 0.0).astype(BF16), back_ref[...])
    sums = got[:, width:].T
    gate_row = gate_ref[...].astype(F32).reshape(1, tok_rows)
    gate_out[...] = ((sums[0:1] + sums[1:2]) / gate_row).astype(BF16).reshape(tok_rows)
    scaled, spread = normalize(tok_ref[...])
    grad = got[:, :width] * gain_ref[...]
    mean = jnp.mean(grad, axis=-1, keepdims=True)
    cross = jnp.mean(grad * scaled, axis=-1, keepdims=True)
    branch = spread * (grad - mean - scaled * cross)
    tokens_out[...] = (go_ref[...].astype(F32) + branch).astype(BF16)


def block_order(sources):
    same = sorted(range(2, sources, 2), key=lambda k: (k.bit_count(), -k))
    return same + list(range(sources - 1, 1, -2)) + [1, 0]


def swap_blocks(blocks, order):
    devices = range(lax.axis_size("space"))
    return [
        lax.ppermute(block, "space", [(i, i ^ k) for i in devices]) if k else block
        for block, k in zip(blocks, order)
    ]


def pass_kernel(
    place, swapped_ref, above_ref, quarter_ref, third_ref, own_ref, lower_ref, out_ref, sum_ref, on_ref
):
    inner = (place[0] == 1) | (place[0] == 2)
    cut = above_ref.shape[0]
    swapped = swapped_ref[...].astype(F32)
    out_ref[...] = (third_ref[...].astype(F32) + jnp.where(inner, swapped, 0.0)).astype(BF16)
    total = own_ref[...].astype(F32) + jnp.where(inner, 0.0, swapped)
    sum_ref[:cut, :] = total[:cut] + jnp.where(inner, above_ref[...].astype(F32), 0.0)
    sum_ref[cut:, :] = total[cut:]
    on_ref[...] = (lower_ref[...].astype(F32) + quarter_ref[...].astype(F32)).astype(BF16)


def most_kernel(sum_ref, across_ref, out_ref):
    cut = across_ref.shape[0]
    out_ref[:cut, :] = sum_ref[:cut, :] + across_ref[...].astype(F32)
    out_ref[cut:, :] = sum_ref[cut:, :]


def total_kernel(sum_ref, below_ref, last_ref, in_hbm, out_hbm, in_ref, out_ref, sems):
    piece_d, half = in_ref.shape[0], out_ref.shape[0] // 2
    width = out_ref.shape[1]
    split = sum_ref.shape[0] - below_ref.shape[0] - piece_d
    in_ref[...] = sum_ref[:piece_d, :] + last_ref[:piece_d, :].astype(F32)
    copies = start_copies([(in_ref, in_hbm)], sems.at[0])
    total = sum_ref[piece_d:, :] + last_ref[piece_d:, :].astype(F32)
    total = jnp.concatenate([total[:split], total[split:] + below_ref[...].astype(F32)])
    out_ref[:half, :] = total[:, :width]
    out_ref[half:, :] = total[:, width:]
    for copy in copies + start_copies([(out_ref, out_hbm)], sems.at[1]):
        copy.wait()


def line_sums(place, first, third, own, upper, lower, width, returned):
    rows, hidden = own.shape
    piece_d = width // LINE
    ahead = 2 * len(returned) // 8
    order = block_order(len(returned))
    swap = [(0, 1), (1, 0), (2, 3), (3, 2)]
    swapped = lax.ppermute(first, "dp", swap)
    above = lax.ppermute(upper, "dp", [(1, 2), (2, 1)])
    quarter = lax.ppermute(lower, "dp", swap)
    back = swap_blocks(returned[:ahead], order[:ahead])
    upper, back[0] = lax.optimization_barrier((upper, back[0]))
    across = lax.ppermute(upper, "dp", [(0, 2), (3, 1)])
    third, *back = lax.optimization_barrier((third, *back))
    shape = functools.partial(jax.ShapeDtypeStruct, own.shape)
    passed, most, onward = kernel_call(
        pass_kernel,
        "pass",
        1,
        1,
        [shape(BF16), shape(F32), jax.ShapeDtypeStruct(lower.shape, BF16)],
        [smem] + [vmem] * 6,
    )(place, swapped, above, quarter, third, own, lower)
    passed, *rest = lax.optimization_barrier((passed, *returned[ahead:]))
    last = lax.ppermute(passed, "dp", [(0, 1), (3, 2), (1, 3), (2, 0)])
    below = lax.ppermute(onward, "dp", [(1, 2), (2, 1)])
    back += swap_blocks(rest, order[ahead:])
    (most,) = kernel_call(most_kernel, "most", 32 * rows * width * hidden, 1, [shape(F32)], [vmem] * 2)(most, across)
    ends = (piece_d, hidden), (2 * (rows - piece_d), width)
    sums = kernel_call(
        total_kernel,
        "total",
        1,
        1,
        [jax.ShapeDtypeStruct(end, F32) for end in ends],
        [vmem] * 3,
        [pltpu.VMEM(end, F32) for end in ends] + [pltpu.SemaphoreType.DMA((2, 1))],
        places=[hbm] * 2,
    )(most, below, last)
    return *sums, back


def body(tokens, gain, w_in, w_out, expert_ids, gate, grad_out):
    sources = lax.axis_size("space")
    groups = lax.axis_size("dp")
    tok_rows, width = tokens.shape
    hidden = w_in.shape[2]
    capacity = ((tok_rows * 5 // 4 + sources - 1) // sources + 7) // 8 * 8
    rows = sources * capacity
    me = lax.axis_index("space").astype(jnp.int32).reshape(1)
    place = lax.axis_index("dp").astype(jnp.int32).reshape(1)
    ids_row = expert_ids.reshape(1, tok_rows)
    gain_row = gain.reshape(1, width)
    weight_in, weight_out = w_in[0], w_out[0]
    shape = jax.ShapeDtypeStruct
    sems = pltpu.SemaphoreType.DMA
    block_place = vmem if capacity % 16 else anywhere
    io_bytes = 2 * (2 * tok_rows * width + 2 * rows * width)

    soon = sources // 2
    blocks = [shape((capacity, 2 * width), BF16)] * soon
    target, *sent = kernel_call(
        functools.partial(place_kernel, sources, capacity),
        "place",
        2 * rows * tok_rows * width,
        io_bytes,
        [shape((1, tok_rows), jnp.int32)] + blocks,
        [smem] * 2 + [hbm] * 5,
        [
            pltpu.VMEM((1, pl.cdiv(tok_rows, LANES) * LANES), jnp.int32),
            pltpu.VMEM((1, tok_rows), jnp.int32),
            pltpu.VMEM((tok_rows,), BF16),
            pltpu.VMEM((tok_rows, width), BF16),
            pltpu.VMEM((1, width), F32),
            pltpu.VMEM((tok_rows, width), BF16),
            pltpu.VMEM((soon * capacity, 2 * width), BF16),
            sems((5,)),
            sems((2, soon)),
        ],
        places=[vmem] + [block_place] * soon,
        vmem_mib=56,
    )(me, place, ids_row, gate, tokens, gain_row, grad_out)
    sent += kernel_call(
        functools.partial(rest_kernel, soon),
        "rest",
        1,
        1,
        blocks,
        [vmem] * 5,
        [pltpu.VMEM((soon * capacity, 2 * width), BF16), sems((2, soon))],
        places=[block_place] * soon,
        vmem_mib=16,
    )(target, gate, tokens, gain_row, grad_out)
    (kept,) = kernel_call(
        keep_kernel,
        "keep",
        1,
        1,
        [shape((capacity, 2 * width), BF16)],
        [vmem],
        vmem_mib=2,
    )(sent[-1])
    arrived = swap_blocks(sent, block_order(sources))
    arrived[-1] = kept

    next_set = list(range(3 * sources // 8, sources // 2))
    late_set = list(range(sources // 2, 3 * sources // 4))
    soon_set = [j for j in range(sources) if j not in next_set + late_set]

    def work(kernel, name, members, outs, *sums, scratch=()):
        count, span = len(members), len(members) * capacity
        return kernel_call(
            functools.partial(kernel, count, groups),
            name,
            8 * span * width * hidden,
            2 * (2 * span * width + 4 * width * hidden + span * hidden),
            outs + [shape((span, hidden), BF16), shape((span, LANES), BF16)],
            [smem] + [vmem] * (2 + len(sums) + count),
            [pltpu.VMEM((span, 2 * width), BF16), pltpu.VMEM((width, span), BF16), *scratch],
        )(place, weight_in, weight_out, *sums, *[arrived[j] for j in members])

    sums_shape = [shape((width, hidden), F32), shape((hidden, width), F32)]
    *sums, soon_gpre, soon_extra = work(sooner_kernel, "sooner", soon_set, sums_shape)
    *sums, next_gpre, next_extra = work(next_kernel, "next", next_set, sums_shape, *sums)
    piece = shape((width // LINE + hidden // LINE // 2, hidden), BF16)
    cut = 3 * piece.shape[0] // 4
    cut_pieces = [shape((cut, hidden), BF16), shape((piece.shape[0] - cut, hidden), BF16)]
    *parts, late_gpre, late_extra = work(
        later_kernel,
        "later",
        late_set,
        [piece] * (LINE - 1) + cut_pieces,
        *sums,
        scratch=[pltpu.VMEM(piece.shape, BF16)],
    )
    returned = kernel_call(
        functools.partial(back_kernel, capacity, (soon_set, next_set, late_set)),
        "back",
        1,
        1,
        [shape((capacity, width + LANES), BF16)] * sources,
        [vmem] * 7,
    )(weight_in, soon_gpre, soon_extra, next_gpre, next_extra, late_gpre, late_extra)

    if groups == LINE:
        grad_w_in, grad_w_out, back = line_sums(
            place, *parts, width, returned
        )
    else:
        back = swap_blocks(returned, block_order(sources))
        pieces = [parts[0], jnp.concatenate(parts[LINE - 1 :]), *parts[1 : LINE - 1]]
        parts_in, parts_out = zip(*[split_piece(part, width, LINE) for part in pieces])
        grad_w_in, grad_w_out = (
            lax.psum_scatter(
                jnp.concatenate(part), "dp", scatter_dimension=0, tiled=True
            ).astype(F32)
            for part in (parts_in, parts_out)
        )
    grad_tokens, grad_gate = kernel_call(
        finish_kernel,
        "finish",
        1,
        1,
        [shape((tok_rows, width), BF16), shape((tok_rows,), BF16)],
        [vmem] * (5 + sources),
        [pltpu.VMEM((rows, width + LANES), BF16)],
    )(target, gate, tokens, gain_row, grad_out, *back)
    return (grad_tokens, grad_gate, grad_w_in[None], grad_w_out[None])


def split_piece(piece, width, pieces):
    piece_d = width // pieces
    lower = piece[piece_d:]
    return piece[:piece_d], jnp.concatenate([lower[:, :width], lower[:, width:]])


def solution(mesh):
    placed = (
        P(("space", "dp"), None),
        P(),
        P("space", None, None),
        P("space", None, None),
        P(("space", "dp"), None),
        P(("space", "dp")),
        P(("space", "dp"), None),
    )
    return jax.shard_map(
        body,
        mesh=mesh,
        in_specs=placed,
        out_specs=(
            P(("space", "dp"), None),
            P(("space", "dp")),
            P("space", "dp", None),
            P("space", "dp", None),
        ),
        check_vma=False,
    )
```

```python
import functools

import jax
import jax.numpy as jnp
from jax import lax
from jax.experimental import pallas as pl
from jax.experimental.pallas import tpu as pltpu
from jax.sharding import PartitionSpec as P

epsilon = 1e-05
F32 = jnp.float32
BF16 = jnp.bfloat16
LANES = 128
LINE = 4
MIB = 1024 * 1024

vmem = pl.BlockSpec(memory_space=pltpu.VMEM)
smem = pl.BlockSpec(memory_space=pltpu.SMEM)
hbm = pl.BlockSpec(memory_space=pltpu.HBM)
anywhere = pl.BlockSpec(memory_space=pl.ANY)


def dot(left, right, contract=((1,), (0,))):
    return lax.dot_general(left, right, (contract, ((), ())), preferred_element_type=F32)


def normalize(tokens):
    values = tokens.astype(F32)
    center = values - jnp.mean(values, axis=-1, keepdims=True)
    spread = lax.rsqrt(jnp.mean(center * center, axis=-1, keepdims=True) + epsilon)
    return center * spread, spread


def kernel_call(kernel, name, flops, nbytes, outs, ins, scratch=(), places=None, vmem_mib=24):
    return pl.pallas_call(
        kernel,
        name=name,
        out_shape=outs,
        in_specs=ins,
        out_specs=places or [vmem] * len(outs),
        scratch_shapes=list(scratch),
        compiler_params=pltpu.CompilerParams(vmem_limit_bytes=vmem_mib * MIB),
        cost_estimate=pl.CostEstimate(flops=flops, bytes_accessed=nbytes, transcendentals=0),
    )


def start_copies(pairs, sems):
    copies = [pltpu.make_async_copy(src, dst, sems.at[i]) for i, (src, dst) in enumerate(pairs)]
    for copy in copies:
        copy.start()
    return copies


def put_blocks(first, target, gate, tok_ref, gain_ref, go_ref, sent_ref, outs, sems):
    capacity, width = outs[0].shape[0], tok_ref.shape[1]
    count = len(outs)
    hit = lax.broadcasted_iota(jnp.int32, (count * capacity, target.shape[1]), 0) == (
        target - first * capacity
    )
    gate = gate.astype(F32).reshape(target.shape)
    scaled, _ = normalize(tok_ref[...])
    normed = (scaled * gain_ref[...]).astype(BF16)
    spans = [pl.ds(j * capacity, capacity) for j in range(count)]
    stores = []
    for part, (weight, values) in enumerate(((gate, go_ref[...]), (1.0, normed))):
        columns = pl.ds((1 - part) * width, width)
        sent_ref[:, columns] = dot(jnp.where(hit, weight, 0.0).astype(BF16), values).astype(BF16)
        if capacity % 16:
            for j in range(count):
                outs[j][:, columns] = sent_ref[spans[j], columns]
        else:
            stores += start_copies(
                [(sent_ref.at[spans[j], columns], outs[j].at[:, columns]) for j in range(count)],
                sems.at[part],
            )
    for copy in stores:
        copy.wait()


def place_kernel(
    sources, capacity, me, place, ids_hbm, gate_hbm, tok_hbm, gain_hbm, go_hbm, target_ref, *refs
):
    *outs, wide_ref, ids_ref, gate_ref, tok_ref, gain_ref, go_ref, sent_ref, in_sems, out_sems = refs
    tok_rows = tok_ref.shape[0]
    loads = start_copies(
        [(ids_hbm, ids_ref), (tok_hbm, tok_ref), (gain_hbm, gain_ref), (gate_hbm, gate_ref), (go_hbm, go_ref)],
        in_sems,
    )
    earlier = lax.broadcasted_iota(jnp.int32, (LANES, LANES), 0) < lax.broadcasted_iota(
        jnp.int32, (LANES, LANES), 1
    )
    earlier = jnp.where(earlier, 1.0, 0.0).astype(BF16)
    loads[0].wait()
    chunks = range(0, tok_rows, LANES)
    wide_ref[...] = jnp.full_like(wide_ref, -1)
    wide_ref[:, :tok_rows] = ids_ref[...]
    ids = [wide_ref[:, c : c + LANES] for c in chunks]
    expert = lax.broadcasted_iota(jnp.int32, (sources, LANES), 0)
    onehots = [jnp.where(expert == chunk, 1.0, 0.0) for chunk in ids]
    within = dot(jnp.concatenate(onehots).astype(BF16), earlier)
    base = jnp.zeros((sources, 1), F32)
    for i, (c, chunk, onehot) in enumerate(zip(chunks, ids, onehots)):
        before = within[i * sources : (i + 1) * sources] + base
        base += jnp.sum(onehot, axis=1, keepdims=True)
        rank = jnp.sum(before * onehot, axis=0, keepdims=True).astype(jnp.int32)
        away = jnp.bitwise_xor(chunk, me[0])
        block = jnp.zeros_like(away)
        for j, k in enumerate(block_order(sources)):
            block = jnp.where(away == k, j, block)
        end = min(LANES, tok_rows - c)
        target = jnp.where(rank < capacity, block * capacity + rank, -1)
        target_ref[:, c : c + end] = target[:, :end]
    for copy in loads[1:]:
        copy.wait()
    put_blocks(0, target_ref[...], gate_ref[...], tok_ref, gain_ref, go_ref, sent_ref, outs, out_sems)


def rest_kernel(first, target_ref, gate_ref, tok_ref, gain_ref, go_ref, *refs):
    *outs, sent_ref, sems = refs
    put_blocks(first, target_ref[...], gate_ref[...], tok_ref, gain_ref, go_ref, sent_ref, outs, sems)


def keep_kernel(block_ref, out_ref):
    out_ref[...] = block_ref[...]


def gelu_parts(value):
    root = 0.7978845608028654
    cubic = root * 0.044715
    square = value * value
    tan = jnp.tanh(value * (root + cubic * square))
    half = 0.5 + 0.5 * tan
    act = value * half
    return act, half + act * (1.0 - tan) * (root + 3.0 * cubic * square)


def shard_order(place):
    first = jnp.where(lax.rem(place, 2) == 0, 3, 0)
    second = jnp.where(place < 2, 2, 1)
    return [first, second, 6 - first - second - place, place]


def expert_work(order, blocks, w_in_ref, w_out_ref, gpre_ref, extra_ref, rows_ref, turned_ref, put):
    capacity = blocks[0].shape[0]
    width, hidden = w_in_ref.shape
    piece_d, piece_f = width // LINE, hidden // LINE
    for j, block in enumerate(blocks):
        rows_ref[j * capacity : (j + 1) * capacity, :] = block[...]
    for j in range(LINE):
        start = pl.multiple_of(order[j] * piece_d, piece_d)
        turned_ref[j * piece_d : (j + 1) * piece_d, :] = rows_ref[:, pl.ds(start, piece_d)].T
    total = jnp.zeros(extra_ref.shape, F32)
    for j in range(LINE):
        part = pl.ds(pl.multiple_of(order[j] * piece_f, piece_f), piece_f)
        delta = rows_ref[:, width:]
        act, slope = gelu_parts(dot(rows_ref[:, :width], w_in_ref[:, part]))
        grad_act = dot(delta, w_out_ref[part, :], ((1,), (1,)))
        products = act * grad_act
        for lane in range(0, piece_f, LANES):
            total += products[:, lane : lane + LANES]
        grad_pre = (grad_act * slope).astype(BF16)
        gpre_ref[:, part] = grad_pre
        put(j, part, dot(turned_ref[...], grad_pre), dot(act.astype(BF16).T, delta))
    total = jnp.sum(total, axis=1, keepdims=True)
    high = total.astype(BF16).astype(F32)
    lane = lax.broadcasted_iota(jnp.int32, extra_ref.shape, 1)
    extra_ref[...] = jnp.where(lane == 0, high, jnp.where(lane == 1, total - high, 0.0)).astype(BF16)


def sooner_kernel(count, groups, place, w_in_ref, w_out_ref, *refs):
    blocks = refs[:count]
    sum_in_ref, sum_out_ref, gpre_ref, extra_ref, rows_ref, turned_ref = refs[count:]
    piece_f = w_in_ref.shape[1] // LINE

    def put(j, part, weight_in, weight_out):
        sum_in_ref[:, part] = weight_in
        sum_out_ref[j * piece_f : (j + 1) * piece_f, :] = weight_out

    order = shard_order(place[0]) if groups == LINE else list(range(LINE))
    expert_work(order, blocks, w_in_ref, w_out_ref, gpre_ref, extra_ref, rows_ref, turned_ref, put)


def next_kernel(count, groups, place, w_in_ref, w_out_ref, old_in_ref, old_out_ref, *refs):
    blocks = refs[:count]
    sum_in_ref, sum_out_ref, gpre_ref, extra_ref, rows_ref, turned_ref = refs[count:]
    piece_f = w_in_ref.shape[1] // LINE

    def put(j, part, weight_in, weight_out):
        chunk = slice(j * piece_f, (j + 1) * piece_f)
        sum_in_ref[:, part] = old_in_ref[:, part] + weight_in
        sum_out_ref[chunk, :] = old_out_ref[chunk, :] + weight_out

    order = shard_order(place[0]) if groups == LINE else list(range(LINE))
    expert_work(order, blocks, w_in_ref, w_out_ref, gpre_ref, extra_ref, rows_ref, turned_ref, put)


def later_kernel(count, groups, place, w_in_ref, w_out_ref, sum_in_ref, sum_out_ref, *refs):
    blocks = refs[:count]
    first_ref, third_ref, own_ref, upper_ref, lower_ref, gpre_ref, extra_ref = refs[count:-3]
    rows_ref, turned_ref, second_ref = refs[-3:]
    outs = (first_ref, second_ref, third_ref, own_ref)
    width, hidden = w_in_ref.shape
    piece_d, piece_f = width // LINE, hidden // LINE

    def put(j, part, weight_in, weight_out):
        weight = (sum_out_ref[j * piece_f : (j + 1) * piece_f, :] + weight_out).astype(BF16)
        outs[j][piece_d:, :width] = weight[: piece_f // 2]
        outs[j][piece_d:, width:] = weight[piece_f // 2 :]
        weight = (sum_in_ref[:, part] + weight_in).astype(BF16)
        for i in range(LINE):
            outs[i][:piece_d, part] = weight[i * piece_d : (i + 1) * piece_d]

    order = shard_order(place[0]) if groups == LINE else list(range(LINE))
    expert_work(order, blocks, w_in_ref, w_out_ref, gpre_ref, extra_ref, rows_ref, turned_ref, put)
    cut = upper_ref.shape[0]
    upper_ref[...] = second_ref[:cut, :]
    lower_ref[...] = second_ref[cut:, :]


def back_kernel(capacity, sets, w_in_ref, *refs):
    inputs, outs = refs[: 2 * len(sets)], refs[2 * len(sets) :]
    width = w_in_ref.shape[0]
    for members, gpre_ref, extra_ref in zip(sets, inputs[::2], inputs[1::2]):
        grad = dot(gpre_ref[...], w_in_ref[...], ((1,), (1,))).astype(BF16)
        for i, j in enumerate(members):
            block = slice(i * capacity, (i + 1) * capacity)
            outs[j][:, :width] = grad[block]
            outs[j][:, width:] = extra_ref[block, :]


def finish_kernel(target_ref, gate_ref, tok_ref, gain_ref, go_ref, *refs):
    *blocks, tokens_out, gate_out, back_ref = refs
    rows, capacity = back_ref.shape[0], blocks[0].shape[0]
    for j, block in enumerate(blocks):
        back_ref[j * capacity : (j + 1) * capacity, :] = block[...]
    tok_rows, width = tok_ref.shape
    spots = jnp.broadcast_to(target_ref[...].astype(F32), (8, tok_rows)).T[:, :1].astype(jnp.int32)
    hit = lax.broadcasted_iota(jnp.int32, (tok_rows, rows), 1) == spots
    got = dot(jnp.where(hit, 1.0, 0.0).astype(BF16), back_ref[...])
    sums = got[:, width:].T
    gate_row = gate_ref[...].astype(F32).reshape(1, tok_rows)
    gate_out[...] = ((sums[0:1] + sums[1:2]) / gate_row).astype(BF16).reshape(tok_rows)
    scaled, spread = normalize(tok_ref[...])
    grad = got[:, :width] * gain_ref[...]
    mean = jnp.mean(grad, axis=-1, keepdims=True)
    cross = jnp.mean(grad * scaled, axis=-1, keepdims=True)
    branch = spread * (grad - mean - scaled * cross)
    tokens_out[...] = (go_ref[...].astype(F32) + branch).astype(BF16)


def block_order(sources):
    same = sorted(range(2, sources, 2), key=lambda k: (k.bit_count(), -k))
    return same + list(range(sources - 1, 1, -2)) + [1, 0]


def swap_blocks(blocks, order):
    devices = range(lax.axis_size("space"))
    return [
        lax.ppermute(block, "space", [(i, i ^ k) for i in devices]) if k else block
        for block, k in zip(blocks, order)
    ]


def pass_kernel(
    place, swapped_ref, above_ref, quarter_ref, third_ref, own_ref, lower_ref, out_ref, sum_ref, on_ref
):
    inner = (place[0] == 1) | (place[0] == 2)
    cut = above_ref.shape[0]
    swapped = swapped_ref[...].astype(F32)
    out_ref[...] = (third_ref[...].astype(F32) + jnp.where(inner, swapped, 0.0)).astype(BF16)
    total = own_ref[...].astype(F32) + jnp.where(inner, 0.0, swapped)
    sum_ref[:cut, :] = total[:cut] + jnp.where(inner, above_ref[...].astype(F32), 0.0)
    sum_ref[cut:, :] = total[cut:]
    on_ref[...] = (lower_ref[...].astype(F32) + quarter_ref[...].astype(F32)).astype(BF16)


def most_kernel(sum_ref, across_ref, out_ref):
    cut = across_ref.shape[0]
    out_ref[:cut, :] = sum_ref[:cut, :] + across_ref[...].astype(F32)
    out_ref[cut:, :] = sum_ref[cut:, :]


def total_kernel(sum_ref, below_ref, last_ref, in_hbm, out_hbm, in_ref, out_ref, sems):
    piece_d, half = in_ref.shape[0], out_ref.shape[0] // 2
    width = out_ref.shape[1]
    split = sum_ref.shape[0] - below_ref.shape[0] - piece_d
    in_ref[...] = sum_ref[:piece_d, :] + last_ref[:piece_d, :].astype(F32)
    copies = start_copies([(in_ref, in_hbm)], sems.at[0])
    total = sum_ref[piece_d:, :] + last_ref[piece_d:, :].astype(F32)
    total = jnp.concatenate([total[:split], total[split:] + below_ref[...].astype(F32)])
    out_ref[:half, :] = total[:, :width]
    out_ref[half:, :] = total[:, width:]
    for copy in copies + start_copies([(out_ref, out_hbm)], sems.at[1]):
        copy.wait()


def line_sums(place, first, third, own, upper, lower, width, returned):
    rows, hidden = own.shape
    piece_d = width // LINE
    ahead = 2 * len(returned) // 8
    order = block_order(len(returned))
    swap = [(0, 1), (1, 0), (2, 3), (3, 2)]
    swapped = lax.ppermute(first, "dp", swap)
    above = lax.ppermute(upper, "dp", [(1, 2), (2, 1)])
    quarter = lax.ppermute(lower, "dp", swap)
    back = swap_blocks(returned[:ahead], order[:ahead])
    upper, quarter = lax.optimization_barrier((upper, quarter))
    across = lax.ppermute(upper, "dp", [(0, 2), (3, 1)])
    third, *back = lax.optimization_barrier((third, *back))
    shape = functools.partial(jax.ShapeDtypeStruct, own.shape)
    passed, most, onward = kernel_call(
        pass_kernel,
        "pass",
        1,
        1,
        [shape(BF16), shape(F32), jax.ShapeDtypeStruct(lower.shape, BF16)],
        [smem] + [vmem] * 6,
    )(place, swapped, above, quarter, third, own, lower)
    passed, *rest = lax.optimization_barrier((passed, *returned[ahead:]))
    last = lax.ppermute(passed, "dp", [(0, 1), (3, 2), (1, 3), (2, 0)])
    below = lax.ppermute(onward, "dp", [(1, 2), (2, 1)])
    back += swap_blocks(rest, order[ahead:])
    (most,) = kernel_call(most_kernel, "most", 32 * rows * width * hidden, 1, [shape(F32)], [vmem] * 2)(most, across)
    ends = (piece_d, hidden), (2 * (rows - piece_d), width)
    sums = kernel_call(
        total_kernel,
        "total",
        1,
        1,
        [jax.ShapeDtypeStruct(end, F32) for end in ends],
        [vmem] * 3,
        [pltpu.VMEM(end, F32) for end in ends] + [pltpu.SemaphoreType.DMA((2, 1))],
        places=[hbm] * 2,
    )(most, below, last)
    return *sums, back


def body(tokens, gain, w_in, w_out, expert_ids, gate, grad_out):
    sources = lax.axis_size("space")
    groups = lax.axis_size("dp")
    tok_rows, width = tokens.shape
    hidden = w_in.shape[2]
    capacity = ((tok_rows * 5 // 4 + sources - 1) // sources + 7) // 8 * 8
    rows = sources * capacity
    me = lax.axis_index("space").astype(jnp.int32).reshape(1)
    place = lax.axis_index("dp").astype(jnp.int32).reshape(1)
    ids_row = expert_ids.reshape(1, tok_rows)
    gain_row = gain.reshape(1, width)
    weight_in, weight_out = w_in[0], w_out[0]
    shape = jax.ShapeDtypeStruct
    sems = pltpu.SemaphoreType.DMA
    block_place = vmem if capacity % 16 else anywhere
    io_bytes = 2 * (2 * tok_rows * width + 2 * rows * width)

    soon = sources // 2
    blocks = [shape((capacity, 2 * width), BF16)] * soon
    target, *sent = kernel_call(
        functools.partial(place_kernel, sources, capacity),
        "place",
        2 * rows * tok_rows * width,
        io_bytes,
        [shape((1, tok_rows), jnp.int32)] + blocks,
        [smem] * 2 + [hbm] * 5,
        [
            pltpu.VMEM((1, pl.cdiv(tok_rows, LANES) * LANES), jnp.int32),
            pltpu.VMEM((1, tok_rows), jnp.int32),
            pltpu.VMEM((tok_rows,), BF16),
            pltpu.VMEM((tok_rows, width), BF16),
            pltpu.VMEM((1, width), F32),
            pltpu.VMEM((tok_rows, width), BF16),
            pltpu.VMEM((soon * capacity, 2 * width), BF16),
            sems((5,)),
            sems((2, soon)),
        ],
        places=[vmem] + [block_place] * soon,
        vmem_mib=56,
    )(me, place, ids_row, gate, tokens, gain_row, grad_out)
    sent += kernel_call(
        functools.partial(rest_kernel, soon),
        "rest",
        1,
        1,
        blocks,
        [vmem] * 5,
        [pltpu.VMEM((soon * capacity, 2 * width), BF16), sems((2, soon))],
        places=[block_place] * soon,
        vmem_mib=16,
    )(target, gate, tokens, gain_row, grad_out)
    (kept,) = kernel_call(
        keep_kernel,
        "keep",
        1,
        1,
        [shape((capacity, 2 * width), BF16)],
        [vmem],
        vmem_mib=2,
    )(sent[-1])
    arrived = swap_blocks(sent, block_order(sources))
    arrived[-1] = kept

    next_set = list(range(3 * sources // 8, sources // 2))
    late_set = list(range(sources // 2, 3 * sources // 4))
    soon_set = [j for j in range(sources) if j not in next_set + late_set]

    def work(kernel, name, members, outs, *sums, scratch=()):
        count, span = len(members), len(members) * capacity
        return kernel_call(
            functools.partial(kernel, count, groups),
            name,
            8 * span * width * hidden,
            2 * (2 * span * width + 4 * width * hidden + span * hidden),
            outs + [shape((span, hidden), BF16), shape((span, LANES), BF16)],
            [smem] + [vmem] * (2 + len(sums) + count),
            [pltpu.VMEM((span, 2 * width), BF16), pltpu.VMEM((width, span), BF16), *scratch],
        )(place, weight_in, weight_out, *sums, *[arrived[j] for j in members])

    sums_shape = [shape((width, hidden), F32), shape((hidden, width), F32)]
    *sums, soon_gpre, soon_extra = work(sooner_kernel, "sooner", soon_set, sums_shape)
    *sums, next_gpre, next_extra = work(next_kernel, "next", next_set, sums_shape, *sums)
    piece = shape((width // LINE + hidden // LINE // 2, hidden), BF16)
    cut = 3 * piece.shape[0] // 4
    cut_pieces = [shape((cut, hidden), BF16), shape((piece.shape[0] - cut, hidden), BF16)]
    *parts, late_gpre, late_extra = work(
        later_kernel,
        "later",
        late_set,
        [piece] * (LINE - 1) + cut_pieces,
        *sums,
        scratch=[pltpu.VMEM(piece.shape, BF16)],
    )
    returned = kernel_call(
        functools.partial(back_kernel, capacity, (soon_set, next_set, late_set)),
        "back",
        1,
        1,
        [shape((capacity, width + LANES), BF16)] * sources,
        [vmem] * 7,
    )(weight_in, soon_gpre, soon_extra, next_gpre, next_extra, late_gpre, late_extra)

    if groups == LINE:
        grad_w_in, grad_w_out, back = line_sums(
            place, *parts, width, returned
        )
    else:
        back = swap_blocks(returned, block_order(sources))
        pieces = [parts[0], jnp.concatenate(parts[LINE - 1 :]), *parts[1 : LINE - 1]]
        parts_in, parts_out = zip(*[split_piece(part, width, LINE) for part in pieces])
        grad_w_in, grad_w_out = (
            lax.psum_scatter(
                jnp.concatenate(part), "dp", scatter_dimension=0, tiled=True
            ).astype(F32)
            for part in (parts_in, parts_out)
        )
    grad_tokens, grad_gate = kernel_call(
        finish_kernel,
        "finish",
        1,
        1,
        [shape((tok_rows, width), BF16), shape((tok_rows,), BF16)],
        [vmem] * (5 + sources),
        [pltpu.VMEM((rows, width + LANES), BF16)],
    )(target, gate, tokens, gain_row, grad_out, *back)
    return (grad_tokens, grad_gate, grad_w_in[None], grad_w_out[None])


def split_piece(piece, width, pieces):
    piece_d = width // pieces
    lower = piece[piece_d:]
    return piece[:piece_d], jnp.concatenate([lower[:, :width], lower[:, width:]])


def solution(mesh):
    placed = (
        P(("space", "dp"), None),
        P(),
        P("space", None, None),
        P("space", None, None),
        P(("space", "dp"), None),
        P(("space", "dp")),
        P(("space", "dp"), None),
    )
    return jax.shard_map(
        body,
        mesh=mesh,
        in_specs=placed,
        out_specs=(
            P(("space", "dp"), None),
            P(("space", "dp")),
            P("space", "dp", None),
            P("space", "dp", None),
        ),
        check_vma=False,
    )
```

```python
import functools

import jax
import jax.numpy as jnp
from jax import lax
from jax.experimental import pallas as pl
from jax.experimental.pallas import tpu as pltpu
from jax.sharding import PartitionSpec as P

epsilon = 1e-05
F32 = jnp.float32
BF16 = jnp.bfloat16
LANES = 128
LINE = 4
MIB = 1024 * 1024

vmem = pl.BlockSpec(memory_space=pltpu.VMEM)
smem = pl.BlockSpec(memory_space=pltpu.SMEM)
hbm = pl.BlockSpec(memory_space=pltpu.HBM)
anywhere = pl.BlockSpec(memory_space=pl.ANY)


def dot(left, right, contract=((1,), (0,))):
    return lax.dot_general(left, right, (contract, ((), ())), preferred_element_type=F32)


def normalize(tokens):
    values = tokens.astype(F32)
    center = values - jnp.mean(values, axis=-1, keepdims=True)
    spread = lax.rsqrt(jnp.mean(center * center, axis=-1, keepdims=True) + epsilon)
    return center * spread, spread


def kernel_call(kernel, name, flops, nbytes, outs, ins, scratch=(), places=None, vmem_mib=24):
    return pl.pallas_call(
        kernel,
        name=name,
        out_shape=outs,
        in_specs=ins,
        out_specs=places or [vmem] * len(outs),
        scratch_shapes=list(scratch),
        compiler_params=pltpu.CompilerParams(vmem_limit_bytes=vmem_mib * MIB),
        cost_estimate=pl.CostEstimate(flops=flops, bytes_accessed=nbytes, transcendentals=0),
    )


def start_copies(pairs, sems):
    copies = [pltpu.make_async_copy(src, dst, sems.at[i]) for i, (src, dst) in enumerate(pairs)]
    for copy in copies:
        copy.start()
    return copies


def put_blocks(first, target, gate, tok_ref, gain_ref, go_ref, sent_ref, outs, sems):
    capacity, width = outs[0].shape[0], tok_ref.shape[1]
    count = len(outs)
    hit = lax.broadcasted_iota(jnp.int32, (count * capacity, target.shape[1]), 0) == (
        target - first * capacity
    )
    gate = gate.astype(F32).reshape(target.shape)
    scaled, _ = normalize(tok_ref[...])
    normed = (scaled * gain_ref[...]).astype(BF16)
    spans = [pl.ds(j * capacity, capacity) for j in range(count)]
    stores = []
    for part, (weight, values) in enumerate(((gate, go_ref[...]), (1.0, normed))):
        columns = pl.ds((1 - part) * width, width)
        sent_ref[:, columns] = dot(jnp.where(hit, weight, 0.0).astype(BF16), values).astype(BF16)
        if capacity % 16:
            for j in range(count):
                outs[j][:, columns] = sent_ref[spans[j], columns]
        else:
            stores += start_copies(
                [(sent_ref.at[spans[j], columns], outs[j].at[:, columns]) for j in range(count)],
                sems.at[part],
            )
    for copy in stores:
        copy.wait()


def place_kernel(
    sources, capacity, me, place, ids_hbm, gate_hbm, tok_hbm, gain_hbm, go_hbm, target_ref, *refs
):
    *outs, wide_ref, ids_ref, gate_ref, tok_ref, gain_ref, go_ref, sent_ref, in_sems, out_sems = refs
    tok_rows = tok_ref.shape[0]
    loads = start_copies(
        [(ids_hbm, ids_ref), (tok_hbm, tok_ref), (gain_hbm, gain_ref), (gate_hbm, gate_ref), (go_hbm, go_ref)],
        in_sems,
    )
    earlier = lax.broadcasted_iota(jnp.int32, (LANES, LANES), 0) < lax.broadcasted_iota(
        jnp.int32, (LANES, LANES), 1
    )
    earlier = jnp.where(earlier, 1.0, 0.0).astype(BF16)
    loads[0].wait()
    chunks = range(0, tok_rows, LANES)
    wide_ref[...] = jnp.full_like(wide_ref, -1)
    wide_ref[:, :tok_rows] = ids_ref[...]
    ids = [wide_ref[:, c : c + LANES] for c in chunks]
    expert = lax.broadcasted_iota(jnp.int32, (sources, LANES), 0)
    onehots = [jnp.where(expert == chunk, 1.0, 0.0) for chunk in ids]
    within = dot(jnp.concatenate(onehots).astype(BF16), earlier)
    base = jnp.zeros((sources, 1), F32)
    for i, (c, chunk, onehot) in enumerate(zip(chunks, ids, onehots)):
        before = within[i * sources : (i + 1) * sources] + base
        base += jnp.sum(onehot, axis=1, keepdims=True)
        rank = jnp.sum(before * onehot, axis=0, keepdims=True).astype(jnp.int32)
        away = jnp.bitwise_xor(chunk, me[0])
        block = jnp.zeros_like(away)
        for j, k in enumerate(block_order(sources)):
            block = jnp.where(away == k, j, block)
        end = min(LANES, tok_rows - c)
        target = jnp.where(rank < capacity, block * capacity + rank, -1)
        target_ref[:, c : c + end] = target[:, :end]
    for copy in loads[1:]:
        copy.wait()
    put_blocks(0, target_ref[...], gate_ref[...], tok_ref, gain_ref, go_ref, sent_ref, outs, out_sems)


def rest_kernel(first, target_ref, gate_ref, tok_ref, gain_ref, go_ref, *refs):
    *outs, sent_ref, sems = refs
    put_blocks(first, target_ref[...], gate_ref[...], tok_ref, gain_ref, go_ref, sent_ref, outs, sems)


def keep_kernel(block_ref, out_ref):
    out_ref[...] = block_ref[...]


def gelu_parts(value):
    root = 0.7978845608028654
    cubic = root * 0.044715
    square = value * value
    tan = jnp.tanh(value * (root + cubic * square))
    half = 0.5 + 0.5 * tan
    act = value * half
    return act, half + act * (1.0 - tan) * (root + 3.0 * cubic * square)


def shard_order(place):
    second = jnp.where(place < 2, 2 - 2 * place, 7 - 2 * place)
    return [3 - place, second, 3 - second, place]


def expert_work(order, blocks, w_in_ref, w_out_ref, gpre_ref, extra_ref, rows_ref, turned_ref, put):
    capacity = blocks[0].shape[0]
    width, hidden = w_in_ref.shape
    piece_d, piece_f = width // LINE, hidden // LINE
    for j, block in enumerate(blocks):
        rows_ref[j * capacity : (j + 1) * capacity, :] = block[...]
    for j in range(LINE):
        start = pl.multiple_of(order[j] * piece_d, piece_d)
        turned_ref[j * piece_d : (j + 1) * piece_d, :] = rows_ref[:, pl.ds(start, piece_d)].T
    total = jnp.zeros(extra_ref.shape, F32)
    for j in range(LINE):
        part = pl.ds(pl.multiple_of(order[j] * piece_f, piece_f), piece_f)
        delta = rows_ref[:, width:]
        act, slope = gelu_parts(dot(rows_ref[:, :width], w_in_ref[:, part]))
        grad_act = dot(delta, w_out_ref[part, :], ((1,), (1,)))
        products = act * grad_act
        for lane in range(0, piece_f, LANES):
            total += products[:, lane : lane + LANES]
        grad_pre = (grad_act * slope).astype(BF16)
        gpre_ref[:, part] = grad_pre
        put(j, part, dot(turned_ref[...], grad_pre), dot(act.astype(BF16).T, delta))
    total = jnp.sum(total, axis=1, keepdims=True)
    high = total.astype(BF16).astype(F32)
    lane = lax.broadcasted_iota(jnp.int32, extra_ref.shape, 1)
    extra_ref[...] = jnp.where(lane == 0, high, jnp.where(lane == 1, total - high, 0.0)).astype(BF16)


def sooner_kernel(count, groups, place, w_in_ref, w_out_ref, *refs):
    blocks = refs[:count]
    sum_in_ref, sum_out_ref, gpre_ref, extra_ref, rows_ref, turned_ref = refs[count:]
    piece_f = w_in_ref.shape[1] // LINE

    def put(j, part, weight_in, weight_out):
        sum_in_ref[:, part] = weight_in
        sum_out_ref[j * piece_f : (j + 1) * piece_f, :] = weight_out

    order = shard_order(place[0]) if groups == LINE else list(range(LINE))
    expert_work(order, blocks, w_in_ref, w_out_ref, gpre_ref, extra_ref, rows_ref, turned_ref, put)


def next_kernel(count, groups, place, w_in_ref, w_out_ref, old_in_ref, old_out_ref, *refs):
    blocks = refs[:count]
    sum_in_ref, sum_out_ref, gpre_ref, extra_ref, rows_ref, turned_ref = refs[count:]
    piece_f = w_in_ref.shape[1] // LINE

    def put(j, part, weight_in, weight_out):
        chunk = slice(j * piece_f, (j + 1) * piece_f)
        sum_in_ref[:, part] = old_in_ref[:, part] + weight_in
        sum_out_ref[chunk, :] = old_out_ref[chunk, :] + weight_out

    order = shard_order(place[0]) if groups == LINE else list(range(LINE))
    expert_work(order, blocks, w_in_ref, w_out_ref, gpre_ref, extra_ref, rows_ref, turned_ref, put)


def later_kernel(count, groups, place, w_in_ref, w_out_ref, sum_in_ref, sum_out_ref, *refs):
    blocks = refs[:count]
    outs = refs[count : count + LINE]
    upper_ref, lower_ref, gpre_ref, extra_ref, rows_ref, turned_ref = refs[count + LINE :]
    width, hidden = w_in_ref.shape
    piece_d, piece_f = width // LINE, hidden // LINE

    def put(j, part, weight_in, weight_out):
        weight = (sum_out_ref[j * piece_f : (j + 1) * piece_f, :] + weight_out).astype(BF16)
        outs[j][piece_d:, :width] = weight[: piece_f // 2]
        outs[j][piece_d:, width:] = weight[piece_f // 2 :]
        weight = (sum_in_ref[:, part] + weight_in).astype(BF16)
        for i in range(LINE):
            outs[i][:piece_d, part] = weight[i * piece_d : (i + 1) * piece_d]

    order = shard_order(place[0]) if groups == LINE else list(range(LINE))
    expert_work(order, blocks, w_in_ref, w_out_ref, gpre_ref, extra_ref, rows_ref, turned_ref, put)
    cut = upper_ref.shape[0]
    upper_ref[...] = outs[0][:cut, :]
    lower_ref[...] = outs[0][cut:, :]


def back_kernel(capacity, sets, w_in_ref, *refs):
    inputs, outs = refs[: 2 * len(sets)], refs[2 * len(sets) :]
    width = w_in_ref.shape[0]
    for members, gpre_ref, extra_ref in zip(sets, inputs[::2], inputs[1::2]):
        grad = dot(gpre_ref[...], w_in_ref[...], ((1,), (1,))).astype(BF16)
        for i, j in enumerate(members):
            block = slice(i * capacity, (i + 1) * capacity)
            outs[j][:, :width] = grad[block]
            outs[j][:, width:] = extra_ref[block, :]


def finish_kernel(target_ref, gate_ref, tok_ref, gain_ref, go_ref, *refs):
    *blocks, tokens_out, gate_out, back_ref = refs
    rows, capacity = back_ref.shape[0], blocks[0].shape[0]
    for j, block in enumerate(blocks):
        back_ref[j * capacity : (j + 1) * capacity, :] = block[...]
    tok_rows, width = tok_ref.shape
    spots = jnp.broadcast_to(target_ref[...].astype(F32), (8, tok_rows)).T[:, :1].astype(jnp.int32)
    hit = lax.broadcasted_iota(jnp.int32, (tok_rows, rows), 1) == spots
    got = dot(jnp.where(hit, 1.0, 0.0).astype(BF16), back_ref[...])
    sums = got[:, width:].T
    gate_row = gate_ref[...].astype(F32).reshape(1, tok_rows)
    gate_out[...] = ((sums[0:1] + sums[1:2]) / gate_row).astype(BF16).reshape(tok_rows)
    scaled, spread = normalize(tok_ref[...])
    grad = got[:, :width] * gain_ref[...]
    mean = jnp.mean(grad, axis=-1, keepdims=True)
    cross = jnp.mean(grad * scaled, axis=-1, keepdims=True)
    branch = spread * (grad - mean - scaled * cross)
    tokens_out[...] = (go_ref[...].astype(F32) + branch).astype(BF16)


def block_order(sources):
    same = sorted(range(2, sources, 2), key=lambda k: (k.bit_count(), k))
    return same + list(range(sources - 1, 1, -2)) + [1, 0]


def swap_blocks(blocks, order):
    devices = range(lax.axis_size("space"))
    return [
        lax.ppermute(block, "space", [(i, i ^ k) for i in devices]) if k else block
        for block, k in zip(blocks, order)
    ]


def pass_kernel(above_ref, inward_ref, third_ref, own_ref, out_ref, sum_ref):
    cut = above_ref.shape[0]
    out_ref[...] = (third_ref[...].astype(F32) + inward_ref[...].astype(F32)).astype(BF16)
    sum_ref[:cut, :] = own_ref[:cut, :].astype(F32) + above_ref[...].astype(F32)
    sum_ref[cut:, :] = own_ref[cut:, :].astype(F32)


def total_kernel(sum_ref, below_ref, cycle_ref, last_ref, in_hbm, out_hbm, in_ref, out_ref, sems):
    piece_d, half = in_ref.shape[0], out_ref.shape[0] // 2
    width = out_ref.shape[1]
    cut = sum_ref.shape[0] - below_ref.shape[0]
    in_ref[...] = (
        sum_ref[:piece_d, :] + cycle_ref[:piece_d, :].astype(F32) + last_ref[:piece_d, :].astype(F32)
    )
    copies = start_copies([(in_ref, in_hbm)], sems.at[0])
    total = sum_ref[piece_d:, :] + cycle_ref[piece_d:, :].astype(F32) + last_ref[piece_d:, :].astype(F32)
    split = cut - piece_d
    total = jnp.concatenate([total[:split], total[split:] + below_ref[...].astype(F32)])
    out_ref[:half, :] = total[:, :width]
    out_ref[half:, :] = total[:, width:]
    for copy in copies + start_copies([(out_ref, out_hbm)], sems.at[1]):
        copy.wait()


def line_sums(first, second, third, own, upper, lower, width, returned):
    rows, hidden = own.shape
    piece_d = width // LINE
    ahead = len(returned) // 4
    order = block_order(len(returned))
    inward = lax.ppermute(first, "dp", [(0, 1), (3, 2)])
    above = lax.ppermute(upper, "dp", [(1, 2), (2, 1)])
    below = lax.ppermute(lower, "dp", [(1, 2), (2, 1)])
    back = swap_blocks(returned[:ahead], order[:ahead])
    second, back[0] = lax.optimization_barrier((second, back[0]))
    cycle = lax.ppermute(second, "dp", [(0, 2), (1, 0), (2, 3), (3, 1)])
    third, *back = lax.optimization_barrier((third, *back))
    shape = functools.partial(jax.ShapeDtypeStruct, own.shape)
    passed, most = kernel_call(
        pass_kernel, "pass", 1, 1, [shape(BF16), shape(F32)], [vmem] * 4
    )(above, inward, third, own)
    passed, *rest = lax.optimization_barrier((passed, *returned[ahead:]))
    last = lax.ppermute(passed, "dp", [(0, 1), (3, 2), (1, 3), (2, 0)])
    back += swap_blocks(rest, order[ahead:])
    ends = (piece_d, hidden), (2 * (rows - piece_d), width)
    sums = kernel_call(
        total_kernel,
        "total",
        1,
        1,
        [jax.ShapeDtypeStruct(end, F32) for end in ends],
        [vmem] * 4,
        [pltpu.VMEM(end, F32) for end in ends] + [pltpu.SemaphoreType.DMA((2, 1))],
        places=[hbm] * 2,
    )(most, below, cycle, last)
    return *sums, back


def body(tokens, gain, w_in, w_out, expert_ids, gate, grad_out):
    sources = lax.axis_size("space")
    groups = lax.axis_size("dp")
    tok_rows, width = tokens.shape
    hidden = w_in.shape[2]
    capacity = ((tok_rows * 5 // 4 + sources - 1) // sources + 7) // 8 * 8
    rows = sources * capacity
    me = lax.axis_index("space").astype(jnp.int32).reshape(1)
    place = lax.axis_index("dp").astype(jnp.int32).reshape(1)
    ids_row = expert_ids.reshape(1, tok_rows)
    gain_row = gain.reshape(1, width)
    weight_in, weight_out = w_in[0], w_out[0]
    shape = jax.ShapeDtypeStruct
    sems = pltpu.SemaphoreType.DMA
    block_place = vmem if capacity % 16 else anywhere
    io_bytes = 2 * (2 * tok_rows * width + 2 * rows * width)

    soon = sources // 2
    blocks = [shape((capacity, 2 * width), BF16)] * soon
    target, *sent = kernel_call(
        functools.partial(place_kernel, sources, capacity),
        "place",
        2 * rows * tok_rows * width,
        io_bytes,
        [shape((1, tok_rows), jnp.int32)] + blocks,
        [smem] * 2 + [hbm] * 5,
        [
            pltpu.VMEM((1, pl.cdiv(tok_rows, LANES) * LANES), jnp.int32),
            pltpu.VMEM((1, tok_rows), jnp.int32),
            pltpu.VMEM((tok_rows,), BF16),
            pltpu.VMEM((tok_rows, width), BF16),
            pltpu.VMEM((1, width), F32),
            pltpu.VMEM((tok_rows, width), BF16),
            pltpu.VMEM((soon * capacity, 2 * width), BF16),
            sems((5,)),
            sems((2, soon)),
        ],
        places=[vmem] + [block_place] * soon,
        vmem_mib=56,
    )(me, place, ids_row, gate, tokens, gain_row, grad_out)
    sent += kernel_call(
        functools.partial(rest_kernel, soon),
        "rest",
        1,
        1,
        blocks,
        [vmem] * 5,
        [pltpu.VMEM((soon * capacity, 2 * width), BF16), sems((2, soon))],
        places=[block_place] * soon,
        vmem_mib=16,
    )(target, gate, tokens, gain_row, grad_out)
    (kept,) = kernel_call(
        keep_kernel,
        "keep",
        1,
        1,
        [shape((capacity, 2 * width), BF16)],
        [vmem],
        vmem_mib=2,
    )(sent[-1])
    arrived = swap_blocks(sent, block_order(sources))
    arrived[-1] = kept

    next_set = list(range(3 * sources // 8, sources // 2))
    late_set = list(range(sources // 2, 3 * sources // 4))
    soon_set = [j for j in range(sources) if j not in next_set + late_set]

    def work(kernel, name, members, outs, *sums):
        count, span = len(members), len(members) * capacity
        return kernel_call(
            functools.partial(kernel, count, groups),
            name,
            8 * span * width * hidden,
            2 * (2 * span * width + 4 * width * hidden + span * hidden),
            outs + [shape((span, hidden), BF16), shape((span, LANES), BF16)],
            [smem] + [vmem] * (2 + len(sums) + count),
            [pltpu.VMEM((span, 2 * width), BF16), pltpu.VMEM((width, span), BF16)],
        )(place, weight_in, weight_out, *sums, *[arrived[j] for j in members])

    sums_shape = [shape((width, hidden), F32), shape((hidden, width), F32)]
    *sums, soon_gpre, soon_extra = work(sooner_kernel, "sooner", soon_set, sums_shape)
    *sums, next_gpre, next_extra = work(next_kernel, "next", next_set, sums_shape, *sums)
    piece = shape((width // LINE + hidden // LINE // 2, hidden), BF16)
    cut = 7 * piece.shape[0] // 8
    cut_pieces = [shape((cut, hidden), BF16), shape((piece.shape[0] - cut, hidden), BF16)]
    *parts, late_gpre, late_extra = work(
        later_kernel, "later", late_set, [piece] * LINE + cut_pieces, *sums
    )
    returned = kernel_call(
        functools.partial(back_kernel, capacity, (soon_set, next_set, late_set)),
        "back",
        1,
        1,
        [shape((capacity, width + LANES), BF16)] * sources,
        [vmem] * 7,
    )(weight_in, soon_gpre, soon_extra, next_gpre, next_extra, late_gpre, late_extra)

    if groups == LINE:
        grad_w_in, grad_w_out, back = line_sums(*parts, width, returned)
    else:
        back = swap_blocks(returned, block_order(sources))
        parts_in, parts_out = zip(*[split_piece(part, width, LINE) for part in parts[:LINE]])
        grad_w_in, grad_w_out = (
            lax.psum_scatter(
                jnp.concatenate(part), "dp", scatter_dimension=0, tiled=True
            ).astype(F32)
            for part in (parts_in, parts_out)
        )
    grad_tokens, grad_gate = kernel_call(
        finish_kernel,
        "finish",
        1,
        1,
        [shape((tok_rows, width), BF16), shape((tok_rows,), BF16)],
        [vmem] * (5 + sources),
        [pltpu.VMEM((rows, width + LANES), BF16)],
    )(target, gate, tokens, gain_row, grad_out, *back)
    return (grad_tokens, grad_gate, grad_w_in[None], grad_w_out[None])


def split_piece(piece, width, pieces):
    piece_d = width // pieces
    lower = piece[piece_d:]
    return piece[:piece_d], jnp.concatenate([lower[:, :width], lower[:, width:]])


def solution(mesh):
    placed = (
        P(("space", "dp"), None),
        P(),
        P("space", None, None),
        P("space", None, None),
        P(("space", "dp"), None),
        P(("space", "dp")),
        P(("space", "dp"), None),
    )
    return jax.shard_map(
        body,
        mesh=mesh,
        in_specs=placed,
        out_specs=(
            P(("space", "dp"), None),
            P(("space", "dp")),
            P("space", "dp", None),
            P("space", "dp", None),
        ),
        check_vma=False,
    )
```

```python
import functools

import jax
import jax.numpy as jnp
from jax import lax
from jax.experimental import pallas as pl
from jax.experimental.pallas import tpu as pltpu
from jax.sharding import PartitionSpec as P

epsilon = 1e-05
F32 = jnp.float32
BF16 = jnp.bfloat16
LANES = 128
LINE = 4
MIB = 1024 * 1024

vmem = pl.BlockSpec(memory_space=pltpu.VMEM)
smem = pl.BlockSpec(memory_space=pltpu.SMEM)
hbm = pl.BlockSpec(memory_space=pltpu.HBM)
anywhere = pl.BlockSpec(memory_space=pl.ANY)


def dot(left, right, contract=((1,), (0,))):
    return lax.dot_general(left, right, (contract, ((), ())), preferred_element_type=F32)


def normalize(tokens):
    values = tokens.astype(F32)
    center = values - jnp.mean(values, axis=-1, keepdims=True)
    spread = lax.rsqrt(jnp.mean(center * center, axis=-1, keepdims=True) + epsilon)
    return center * spread, spread


def kernel_call(kernel, name, flops, nbytes, outs, ins, scratch=(), places=None, vmem_mib=24):
    return pl.pallas_call(
        kernel,
        name=name,
        out_shape=outs,
        in_specs=ins,
        out_specs=places or [vmem] * len(outs),
        scratch_shapes=list(scratch),
        compiler_params=pltpu.CompilerParams(vmem_limit_bytes=vmem_mib * MIB),
        cost_estimate=pl.CostEstimate(flops=flops, bytes_accessed=nbytes, transcendentals=0),
    )


def start_copies(pairs, sems):
    copies = [pltpu.make_async_copy(src, dst, sems.at[i]) for i, (src, dst) in enumerate(pairs)]
    for copy in copies:
        copy.start()
    return copies


def put_blocks(first, target, gate, tok_ref, gain_ref, go_ref, sent_ref, outs, sems):
    capacity, width = outs[0].shape[0], tok_ref.shape[1]
    count = len(outs)
    hit = lax.broadcasted_iota(jnp.int32, (count * capacity, target.shape[1]), 0) == (
        target - first * capacity
    )
    gate = gate.astype(F32).reshape(target.shape)
    scaled, _ = normalize(tok_ref[...])
    normed = (scaled * gain_ref[...]).astype(BF16)
    spans = [pl.ds(j * capacity, capacity) for j in range(count)]
    stores = []
    for part, (weight, values) in enumerate(((gate, go_ref[...]), (1.0, normed))):
        columns = pl.ds((1 - part) * width, width)
        sent_ref[:, columns] = dot(jnp.where(hit, weight, 0.0).astype(BF16), values).astype(BF16)
        if capacity % 16:
            for j in range(count):
                outs[j][:, columns] = sent_ref[spans[j], columns]
        else:
            stores += start_copies(
                [(sent_ref.at[spans[j], columns], outs[j].at[:, columns]) for j in range(count)],
                sems.at[part],
            )
    for copy in stores:
        copy.wait()


def place_kernel(
    sources, capacity, me, place, ids_hbm, gate_hbm, tok_hbm, gain_hbm, go_hbm, target_ref, *refs
):
    *outs, wide_ref, ids_ref, gate_ref, tok_ref, gain_ref, go_ref, sent_ref, in_sems, out_sems = refs
    tok_rows = tok_ref.shape[0]
    loads = start_copies(
        [(ids_hbm, ids_ref), (tok_hbm, tok_ref), (gain_hbm, gain_ref), (gate_hbm, gate_ref), (go_hbm, go_ref)],
        in_sems,
    )
    earlier = lax.broadcasted_iota(jnp.int32, (LANES, LANES), 0) < lax.broadcasted_iota(
        jnp.int32, (LANES, LANES), 1
    )
    earlier = jnp.where(earlier, 1.0, 0.0).astype(BF16)
    loads[0].wait()
    chunks = range(0, tok_rows, LANES)
    wide_ref[...] = jnp.full_like(wide_ref, -1)
    wide_ref[:, :tok_rows] = ids_ref[...]
    ids = [wide_ref[:, c : c + LANES] for c in chunks]
    expert = lax.broadcasted_iota(jnp.int32, (sources, LANES), 0)
    onehots = [jnp.where(expert == chunk, 1.0, 0.0) for chunk in ids]
    within = dot(jnp.concatenate(onehots).astype(BF16), earlier)
    base = jnp.zeros((sources, 1), F32)
    for i, (c, chunk, onehot) in enumerate(zip(chunks, ids, onehots)):
        before = within[i * sources : (i + 1) * sources] + base
        base += jnp.sum(onehot, axis=1, keepdims=True)
        rank = jnp.sum(before * onehot, axis=0, keepdims=True).astype(jnp.int32)
        away = jnp.bitwise_xor(chunk, me[0])
        block = jnp.zeros_like(away)
        for j, k in enumerate(block_order(sources)):
            block = jnp.where(away == k, j, block)
        end = min(LANES, tok_rows - c)
        target = jnp.where(rank < capacity, block * capacity + rank, -1)
        target_ref[:, c : c + end] = target[:, :end]
    for copy in loads[1:]:
        copy.wait()
    put_blocks(0, target_ref[...], gate_ref[...], tok_ref, gain_ref, go_ref, sent_ref, outs, out_sems)


def rest_kernel(first, target_ref, gate_ref, tok_ref, gain_ref, go_ref, *refs):
    *outs, sent_ref, sems = refs
    put_blocks(first, target_ref[...], gate_ref[...], tok_ref, gain_ref, go_ref, sent_ref, outs, sems)


def keep_kernel(block_ref, out_ref):
    out_ref[...] = block_ref[...]


def gelu_parts(value):
    root = 0.7978845608028654
    cubic = root * 0.044715
    square = value * value
    tan = jnp.tanh(value * (root + cubic * square))
    half = 0.5 + 0.5 * tan
    act = value * half
    return act, half + act * (1.0 - tan) * (root + 3.0 * cubic * square)


def shard_order(place):
    second = jnp.where(place < 2, 2 - 2 * place, 7 - 2 * place)
    return [3 - place, second, 3 - second, place]


def expert_work(order, blocks, w_in_ref, w_out_ref, gpre_ref, extra_ref, rows_ref, turned_ref, put):
    capacity = blocks[0].shape[0]
    width, hidden = w_in_ref.shape
    piece_d, piece_f = width // LINE, hidden // LINE
    for j, block in enumerate(blocks):
        rows_ref[j * capacity : (j + 1) * capacity, :] = block[...]
    for j in range(LINE):
        start = pl.multiple_of(order[j] * piece_d, piece_d)
        turned_ref[j * piece_d : (j + 1) * piece_d, :] = rows_ref[:, pl.ds(start, piece_d)].T
    total = jnp.zeros(extra_ref.shape, F32)
    for j in range(LINE):
        part = pl.ds(pl.multiple_of(order[j] * piece_f, piece_f), piece_f)
        delta = rows_ref[:, width:]
        act, slope = gelu_parts(dot(rows_ref[:, :width], w_in_ref[:, part]))
        grad_act = dot(delta, w_out_ref[part, :], ((1,), (1,)))
        products = act * grad_act
        for lane in range(0, piece_f, LANES):
            total += products[:, lane : lane + LANES]
        grad_pre = (grad_act * slope).astype(BF16)
        gpre_ref[:, part] = grad_pre
        put(j, part, dot(turned_ref[...], grad_pre), dot(act.astype(BF16).T, delta))
    total = jnp.sum(total, axis=1, keepdims=True)
    high = total.astype(BF16).astype(F32)
    lane = lax.broadcasted_iota(jnp.int32, extra_ref.shape, 1)
    extra_ref[...] = jnp.where(lane == 0, high, jnp.where(lane == 1, total - high, 0.0)).astype(BF16)


def sooner_kernel(count, groups, place, w_in_ref, w_out_ref, *refs):
    blocks = refs[:count]
    sum_in_ref, sum_out_ref, gpre_ref, extra_ref, rows_ref, turned_ref = refs[count:]
    piece_f = w_in_ref.shape[1] // LINE

    def put(j, part, weight_in, weight_out):
        sum_in_ref[:, part] = weight_in.astype(BF16)
        sum_out_ref[j * piece_f : (j + 1) * piece_f, :] = weight_out.astype(BF16)

    order = shard_order(place[0]) if groups == LINE else list(range(LINE))
    expert_work(order, blocks, w_in_ref, w_out_ref, gpre_ref, extra_ref, rows_ref, turned_ref, put)


def next_kernel(count, groups, place, w_in_ref, w_out_ref, old_in_ref, old_out_ref, *refs):
    blocks = refs[:count]
    sum_in_ref, sum_out_ref, gpre_ref, extra_ref, rows_ref, turned_ref = refs[count:]
    piece_f = w_in_ref.shape[1] // LINE

    def put(j, part, weight_in, weight_out):
        chunk = slice(j * piece_f, (j + 1) * piece_f)
        sum_in_ref[:, part] = (old_in_ref[:, part].astype(F32) + weight_in).astype(BF16)
        sum_out_ref[chunk, :] = (old_out_ref[chunk, :].astype(F32) + weight_out).astype(BF16)

    order = shard_order(place[0]) if groups == LINE else list(range(LINE))
    expert_work(order, blocks, w_in_ref, w_out_ref, gpre_ref, extra_ref, rows_ref, turned_ref, put)


def later_kernel(count, groups, place, w_in_ref, w_out_ref, sum_in_ref, sum_out_ref, *refs):
    blocks = refs[:count]
    outs = refs[count : count + LINE]
    upper_ref, lower_ref, gpre_ref, extra_ref, rows_ref, turned_ref = refs[count + LINE :]
    width, hidden = w_in_ref.shape
    piece_d, piece_f = width // LINE, hidden // LINE

    def put(j, part, weight_in, weight_out):
        weight = (sum_out_ref[j * piece_f : (j + 1) * piece_f, :].astype(F32) + weight_out).astype(BF16)
        outs[j][piece_d:, :width] = weight[: piece_f // 2]
        outs[j][piece_d:, width:] = weight[piece_f // 2 :]
        weight = (sum_in_ref[:, part].astype(F32) + weight_in).astype(BF16)
        for i in range(LINE):
            outs[i][:piece_d, part] = weight[i * piece_d : (i + 1) * piece_d]

    order = shard_order(place[0]) if groups == LINE else list(range(LINE))
    expert_work(order, blocks, w_in_ref, w_out_ref, gpre_ref, extra_ref, rows_ref, turned_ref, put)
    cut = upper_ref.shape[0]
    upper_ref[...] = outs[0][:cut, :]
    lower_ref[...] = outs[0][cut:, :]


def back_kernel(capacity, sets, w_in_ref, *refs):
    inputs, outs = refs[: 2 * len(sets)], refs[2 * len(sets) :]
    width = w_in_ref.shape[0]
    for members, gpre_ref, extra_ref in zip(sets, inputs[::2], inputs[1::2]):
        grad = dot(gpre_ref[...], w_in_ref[...], ((1,), (1,))).astype(BF16)
        for i, j in enumerate(members):
            block = slice(i * capacity, (i + 1) * capacity)
            outs[j][:, :width] = grad[block]
            outs[j][:, width:] = extra_ref[block, :]


def finish_kernel(target_ref, gate_ref, tok_ref, gain_ref, go_ref, *refs):
    *blocks, tokens_out, gate_out, back_ref = refs
    rows, capacity = back_ref.shape[0], blocks[0].shape[0]
    for j, block in enumerate(blocks):
        back_ref[j * capacity : (j + 1) * capacity, :] = block[...]
    tok_rows, width = tok_ref.shape
    spots = jnp.broadcast_to(target_ref[...].astype(F32), (8, tok_rows)).T[:, :1].astype(jnp.int32)
    hit = lax.broadcasted_iota(jnp.int32, (tok_rows, rows), 1) == spots
    got = dot(jnp.where(hit, 1.0, 0.0).astype(BF16), back_ref[...])
    sums = got[:, width:].T
    gate_row = gate_ref[...].astype(F32).reshape(1, tok_rows)
    gate_out[...] = ((sums[0:1] + sums[1:2]) / gate_row).astype(BF16).reshape(tok_rows)
    scaled, spread = normalize(tok_ref[...])
    grad = got[:, :width] * gain_ref[...]
    mean = jnp.mean(grad, axis=-1, keepdims=True)
    cross = jnp.mean(grad * scaled, axis=-1, keepdims=True)
    branch = spread * (grad - mean - scaled * cross)
    tokens_out[...] = (go_ref[...].astype(F32) + branch).astype(BF16)


def block_order(sources):
    same = sorted(range(2, sources, 2), key=lambda k: (k.bit_count(), -k))
    return same + list(range(sources - 1, 1, -2)) + [1, 0]


def swap_blocks(blocks, order):
    devices = range(lax.axis_size("space"))
    return [
        lax.ppermute(block, "space", [(i, i ^ k) for i in devices]) if k else block
        for block, k in zip(blocks, order)
    ]


def pass_kernel(above_ref, inward_ref, third_ref, own_ref, out_ref, sum_ref):
    cut = above_ref.shape[0]
    out_ref[...] = (third_ref[...].astype(F32) + inward_ref[...].astype(F32)).astype(BF16)
    sum_ref[:cut, :] = own_ref[:cut, :].astype(F32) + above_ref[...].astype(F32)
    sum_ref[cut:, :] = own_ref[cut:, :].astype(F32)


def total_kernel(sum_ref, below_ref, cycle_ref, last_ref, in_hbm, out_hbm, in_ref, out_ref, sems):
    piece_d, half = in_ref.shape[0], out_ref.shape[0] // 2
    width = out_ref.shape[1]
    cut = sum_ref.shape[0] - below_ref.shape[0]
    in_ref[...] = (
        sum_ref[:piece_d, :] + cycle_ref[:piece_d, :].astype(F32) + last_ref[:piece_d, :].astype(F32)
    )
    copies = start_copies([(in_ref, in_hbm)], sems.at[0])
    total = sum_ref[piece_d:, :] + cycle_ref[piece_d:, :].astype(F32) + last_ref[piece_d:, :].astype(F32)
    split = cut - piece_d
    total = jnp.concatenate([total[:split], total[split:] + below_ref[...].astype(F32)])
    out_ref[:half, :] = total[:, :width]
    out_ref[half:, :] = total[:, width:]
    for copy in copies + start_copies([(out_ref, out_hbm)], sems.at[1]):
        copy.wait()


def line_sums(first, second, third, own, upper, lower, width, returned):
    rows, hidden = own.shape
    piece_d = width // LINE
    ahead = len(returned) // 4
    order = block_order(len(returned))
    inward = lax.ppermute(first, "dp", [(0, 1), (3, 2)])
    above = lax.ppermute(upper, "dp", [(1, 2), (2, 1)])
    below = lax.ppermute(lower, "dp", [(1, 2), (2, 1)])
    back = swap_blocks(returned[:ahead], order[:ahead])
    second, back[0] = lax.optimization_barrier((second, back[0]))
    cycle = lax.ppermute(second, "dp", [(0, 2), (1, 0), (2, 3), (3, 1)])
    third, *back = lax.optimization_barrier((third, *back))
    shape = functools.partial(jax.ShapeDtypeStruct, own.shape)
    passed, most = kernel_call(
        pass_kernel, "pass", 1, 1, [shape(BF16), shape(F32)], [vmem] * 4
    )(above, inward, third, own)
    passed, *rest = lax.optimization_barrier((passed, *returned[ahead:]))
    last = lax.ppermute(passed, "dp", [(0, 1), (3, 2), (1, 3), (2, 0)])
    back += swap_blocks(rest, order[ahead:])
    ends = (piece_d, hidden), (2 * (rows - piece_d), width)
    sums = kernel_call(
        total_kernel,
        "total",
        1,
        1,
        [jax.ShapeDtypeStruct(end, F32) for end in ends],
        [vmem] * 4,
        [pltpu.VMEM(end, F32) for end in ends] + [pltpu.SemaphoreType.DMA((2, 1))],
        places=[hbm] * 2,
    )(most, below, cycle, last)
    return *sums, back


def body(tokens, gain, w_in, w_out, expert_ids, gate, grad_out):
    sources = lax.axis_size("space")
    groups = lax.axis_size("dp")
    tok_rows, width = tokens.shape
    hidden = w_in.shape[2]
    capacity = ((tok_rows * 5 // 4 + sources - 1) // sources + 7) // 8 * 8
    rows = sources * capacity
    me = lax.axis_index("space").astype(jnp.int32).reshape(1)
    place = lax.axis_index("dp").astype(jnp.int32).reshape(1)
    ids_row = expert_ids.reshape(1, tok_rows)
    gain_row = gain.reshape(1, width)
    weight_in, weight_out = w_in[0], w_out[0]
    shape = jax.ShapeDtypeStruct
    sems = pltpu.SemaphoreType.DMA
    block_place = vmem if capacity % 16 else anywhere
    io_bytes = 2 * (2 * tok_rows * width + 2 * rows * width)

    soon = sources // 2
    blocks = [shape((capacity, 2 * width), BF16)] * soon
    target, *sent = kernel_call(
        functools.partial(place_kernel, sources, capacity),
        "place",
        2 * rows * tok_rows * width,
        io_bytes,
        [shape((1, tok_rows), jnp.int32)] + blocks,
        [smem] * 2 + [hbm] * 5,
        [
            pltpu.VMEM((1, pl.cdiv(tok_rows, LANES) * LANES), jnp.int32),
            pltpu.VMEM((1, tok_rows), jnp.int32),
            pltpu.VMEM((tok_rows,), BF16),
            pltpu.VMEM((tok_rows, width), BF16),
            pltpu.VMEM((1, width), F32),
            pltpu.VMEM((tok_rows, width), BF16),
            pltpu.VMEM((soon * capacity, 2 * width), BF16),
            sems((5,)),
            sems((2, soon)),
        ],
        places=[vmem] + [block_place] * soon,
        vmem_mib=56,
    )(me, place, ids_row, gate, tokens, gain_row, grad_out)
    sent += kernel_call(
        functools.partial(rest_kernel, soon),
        "rest",
        1,
        1,
        blocks,
        [vmem] * 5,
        [pltpu.VMEM((soon * capacity, 2 * width), BF16), sems((2, soon))],
        places=[block_place] * soon,
        vmem_mib=16,
    )(target, gate, tokens, gain_row, grad_out)
    (kept,) = kernel_call(
        keep_kernel,
        "keep",
        1,
        1,
        [shape((capacity, 2 * width), BF16)],
        [vmem],
        vmem_mib=2,
    )(sent[-1])
    arrived = swap_blocks(sent, block_order(sources))
    arrived[-1] = kept

    next_set = list(range(3 * sources // 8, sources // 2))
    late_set = list(range(sources // 2, 3 * sources // 4))
    soon_set = [j for j in range(sources) if j not in next_set + late_set]

    def work(kernel, name, members, outs, *sums):
        count, span = len(members), len(members) * capacity
        return kernel_call(
            functools.partial(kernel, count, groups),
            name,
            8 * span * width * hidden,
            2 * (2 * span * width + 4 * width * hidden + span * hidden),
            outs + [shape((span, hidden), BF16), shape((span, LANES), BF16)],
            [smem] + [vmem] * (2 + len(sums) + count),
            [pltpu.VMEM((span, 2 * width), BF16), pltpu.VMEM((width, span), BF16)],
        )(place, weight_in, weight_out, *sums, *[arrived[j] for j in members])

    sums_shape = [shape((width, hidden), BF16), shape((hidden, width), BF16)]
    *sums, soon_gpre, soon_extra = work(sooner_kernel, "sooner", soon_set, sums_shape)
    *sums, next_gpre, next_extra = work(next_kernel, "next", next_set, sums_shape, *sums)
    piece = shape((width // LINE + hidden // LINE // 2, hidden), BF16)
    cut = 7 * piece.shape[0] // 8
    cut_pieces = [shape((cut, hidden), BF16), shape((piece.shape[0] - cut, hidden), BF16)]
    *parts, late_gpre, late_extra = work(
        later_kernel, "later", late_set, [piece] * LINE + cut_pieces, *sums
    )
    returned = kernel_call(
        functools.partial(back_kernel, capacity, (soon_set, next_set, late_set)),
        "back",
        1,
        1,
        [shape((capacity, width + LANES), BF16)] * sources,
        [vmem] * 7,
    )(weight_in, soon_gpre, soon_extra, next_gpre, next_extra, late_gpre, late_extra)

    if groups == LINE:
        grad_w_in, grad_w_out, back = line_sums(*parts, width, returned)
    else:
        back = swap_blocks(returned, block_order(sources))
        parts_in, parts_out = zip(*[split_piece(part, width, LINE) for part in parts[:LINE]])
        grad_w_in, grad_w_out = (
            lax.psum_scatter(
                jnp.concatenate(part), "dp", scatter_dimension=0, tiled=True
            ).astype(F32)
            for part in (parts_in, parts_out)
        )
    grad_tokens, grad_gate = kernel_call(
        finish_kernel,
        "finish",
        1,
        1,
        [shape((tok_rows, width), BF16), shape((tok_rows,), BF16)],
        [vmem] * (5 + sources),
        [pltpu.VMEM((rows, width + LANES), BF16)],
    )(target, gate, tokens, gain_row, grad_out, *back)
    return (grad_tokens, grad_gate, grad_w_in[None], grad_w_out[None])


def split_piece(piece, width, pieces):
    piece_d = width // pieces
    lower = piece[piece_d:]
    return piece[:piece_d], jnp.concatenate([lower[:, :width], lower[:, width:]])


def solution(mesh):
    placed = (
        P(("space", "dp"), None),
        P(),
        P("space", None, None),
        P("space", None, None),
        P(("space", "dp"), None),
        P(("space", "dp")),
        P(("space", "dp"), None),
    )
    return jax.shard_map(
        body,
        mesh=mesh,
        in_specs=placed,
        out_specs=(
            P(("space", "dp"), None),
            P(("space", "dp")),
            P("space", "dp", None),
            P("space", "dp", None),
        ),
        check_vma=False,
    )
```
